32 devices in a mesh: expert: 8 (over z, x), replica: 4 (over y, core).
Axes of the slice: x: 2, y: 2, z: 4, core: 2. Of those that a mesh axis runs over, the one named last changes fastest.
Arguments:
- tokens: bfloat16 [8192, 1024], P(('expert', 'replica')), may hold values from -6 to 6
- route: int32 [32, 256], P(('expert', 'replica')), may hold values from 0 to 255, each once within a row
- w_qkv: bfloat16 [1024, 3072], P(('expert', 'replica')), may hold values from -0.1875 to 0.1875
- w_attn_out: bfloat16 [1024, 1024], P(('expert', 'replica')), may hold values from -1 to 1
- w_up: bfloat16 [1024, 4096], P(('expert', 'replica')), may hold values from -0.1875 to 0.1875
- w_down: bfloat16 [4096, 1024], P(('expert', 'replica')), may hold values from -0.09375 to 0.09375
- gain_attn: bfloat16 [1024], P(('expert', 'replica')), may hold values from 0.25 to 1.75
- gain_ffn: bfloat16 [1024], P(('expert', 'replica')), may hold values from 0.25 to 1.75
- expert_in: bfloat16 [8, 1024, 4096], P('expert'), may hold values from -0.1875 to 0.1875
- expert_out: bfloat16 [8, 4096, 1024], P('expert'), may hold values from -0.09375 to 0.09375
- centroids: bfloat16 [8, 1024], P('expert'), may hold values from -0.09375 to 0.09375
- expert_gain: bfloat16 [8, 1024], P('expert'), may hold values from 0.25 to 1.75
- cotangent: bfloat16 [8192, 1024], P(('expert', 'replica')), may hold values from -6 to 6
Outputs:
- mixed: bfloat16 [8192, 1024], P(('expert', 'replica'))
- grad_tokens: float32 [8192, 1024], P(('expert', 'replica'))
- grad_qkv: float32 [1024, 3072], P(('expert', 'replica'))
- grad_attn_out: float32 [1024, 1024], P(('expert', 'replica'))
- grad_up: float32 [1024, 4096], P(('expert', 'replica'))
- grad_down: float32 [4096, 1024], P(('expert', 'replica'))
- grad_gain_attn: float32 [1024], P(('expert', 'replica'))
- grad_gain_ffn: float32 [1024], P(('expert', 'replica'))
- grad_expert_in: float32 [8, 1024, 4096], P('expert', 'replica')
- grad_expert_out: float32 [8, 4096, 1024], P('expert', 'replica')
- grad_centroids: float32 [8, 1024], P('expert', 'replica')
- grad_expert_gain: float32 [8, 1024], P('expert', 'replica')
The draws below stay inside these ranges and needn't reach their ends.
Inputs may be any that keep to these rules, and one draw needn't show every extreme that they name: `route`: each row is a permutation of 0 to 255.
All inputs are finite; a program needn't handle non-finite values.
Results may differ from the reference program's by a relative error of at most 0.015.
Values may be sent and summed in bfloat16 or wider, within the bound.
No kernel may reach another device: no remote copies, remote signals or barrier semaphores. Data moves between devices by JAX's collectives and lax.ppermute only.
A program may use at most 256 MiB of HBM per device.

```python
import math
import jax
import jax.numpy as jnp
from jax import lax

D = 1024
HEADS = 16
HEAD_DIM = 64
FF = 4096
EXPERT_FF = 4096
TOK_DEV = 256
EXPERTS = 8
SEQS = 32
PER_EXPERT = 32
TOKENS = 8192
N_EXPERT = 8
N_REPLICA = 4


def with_spikes(result, key, source, target, blocks, factor):
    def block_of(dim):
        return (jnp.arange(result.shape[dim]) // (result.shape[dim] // blocks)).reshape((-1,) + (1,) * (result.ndim - 1 - dim))

    first = jax.random.permutation(key, blocks)[block_of(target)]
    second = (block_of(target) + blocks // 2) % blocks
    return jnp.where((block_of(source) == first) | (block_of(source) == second), factor * result, result)


def steps_of(stream_key, dims, split, low, top_value):
    factor_of, own = 1.0, jax.random.fold_in(stream_key, 6)
    for axis_at, blocks in split:
        draws = jnp.exp(jax.random.uniform(jax.random.fold_in(own, axis_at), (blocks,), jnp.float32, low / len(split), top_value / len(split)))
        factor_of = factor_of * jnp.repeat(draws, dims[axis_at] // blocks).reshape([-1 if axis == axis_at else 1 for axis in range(len(dims))])
    return factor_of


def normal_values(rng, dims, spread, reach, shards=(), held_as=jnp.bfloat16):
    level = steps_of(rng, dims, shards, -0.22, 0.18) if shards else 1.0
    result = jax.random.normal(rng, dims, jnp.float32) * spread * level
    return jnp.minimum(jnp.maximum(result, -reach), reach).astype(held_as)


def noise_with(key, extent, spread, most, pieces, heavy, kind=jnp.bfloat16):
    result = spread * jax.random.normal(key, extent, jnp.float32)
    if pieces:
        result = result * steps_of(key, extent, pieces, -0.22, 0.18)
    return jnp.clip(with_spikes(result, jax.random.fold_in(key, 3), *heavy), -most, most).astype(kind)


def setup_inputs(seed: int = 0) -> dict:
    seeds = jax.random.split(jax.random.key(seed), 14)
    return {
        "tokens": normal_values(seeds[0], (TOKENS, D), 1.0, 6.0, ((0, 32),)),
        "route": jax.vmap(lambda own: jax.random.permutation(own, TOK_DEV))(jax.random.split(seeds[1], SEQS)).reshape((SEQS, TOK_DEV)).astype(jnp.int32),
        "w_qkv": normal_values(seeds[2], (D, 3 * D), D ** -0.5, 0.1875, ((0, 32),)),
        "w_attn_out": normal_values(seeds[3], (D, D), (D // 32) ** -0.5, 1.0, ((0, 32),)),
        "w_up": normal_values(seeds[4], (D, FF), D ** -0.5, 0.1875, ((0, 32),)),
        "w_down": normal_values(seeds[5], (FF, D), FF ** -0.5, 0.09375, ((0, 32),)),
        "gain_attn": jnp.clip(1.0 + 0.15 * jax.random.normal(seeds[6], (D,), jnp.float32), 0.25, 1.75).astype(jnp.bfloat16),
        "gain_ffn": jnp.clip(1.0 + 0.15 * jax.random.normal(seeds[7], (D,), jnp.float32), 0.25, 1.75).astype(jnp.bfloat16),
        "expert_in": normal_values(seeds[8], (EXPERTS, D, EXPERT_FF), D ** -0.5, 0.1875, ((0, 8),)),
        "expert_out": normal_values(seeds[9], (EXPERTS, EXPERT_FF, D), EXPERT_FF ** -0.5, 0.09375, ((0, 8),)),
        "centroids": normal_values(seeds[10], (EXPERTS, D), (4 * D) ** -0.5, 0.09375, ((0, 8),)),
        "expert_gain": jnp.clip(1.0 + 0.15 * jax.random.normal(seeds[11], (EXPERTS, D), jnp.float32), 0.25, 1.75).astype(jnp.bfloat16),
        "cotangent": noise_with(seeds[12], (TOKENS, D), 1.0, 6.0, ((0, 32),), (0, 1, 32, 2.75)),
    }


@jax.custom_vjp
def low(v):
    return lax.optimization_barrier(v.astype(jnp.bfloat16)).astype(jnp.float32)

@jax.custom_vjp
def low_back(v):
    return v

def low_keep(v):
    return (low(v), None)

def low_pass(kept, grad):
    return (grad,)

def back_keep(v):
    return (v, None)

def back_low(kept, grad):
    return (low(grad),)
low.defvjp(low_keep, low_pass)
low_back.defvjp(back_keep, back_low)
EPSILON = 1e-05
HIGHEST = lax.Precision.HIGHEST

def product(left_rows, right_rows):
    return jnp.dot(left_rows, right_rows, precision=HIGHEST, preferred_element_type=jnp.float32)

def layer_norm(values, norm_gain):
    centered = values - lax.optimization_barrier(jnp.mean(values, axis=-1, keepdims=True))
    variance = lax.optimization_barrier(jnp.mean(centered * centered, axis=-1, keepdims=True))
    return centered * lax.rsqrt(variance + EPSILON) * norm_gain

def dense_sequence(inputs, w_qkv, w_attn_out, w_up, w_down, gain_attn, gain_ffn):
    length = inputs.shape[0]
    attn_in = low(layer_norm(inputs, gain_attn))
    qkv_rows = low_back(low(product(attn_in, w_qkv))).reshape(length, 3, HEADS, HEAD_DIM)
    queries = qkv_rows[:, 0]
    key_rows = qkv_rows[:, 1]
    value_rows = qkv_rows[:, 2]
    factor = 1.0 / math.sqrt(HEAD_DIM)
    scores = low_back(jnp.einsum('qhd,khd->hqk', queries, key_rows, precision=HIGHEST) * factor)
    causal = lax.broadcasted_iota(jnp.int32, (length, length), 0) >= lax.broadcasted_iota(jnp.int32, (length, length), 1)
    scores = jnp.where(causal[None], scores, -1e+30)
    shifted = jnp.exp(scores - lax.optimization_barrier(jnp.max(scores, axis=-1, keepdims=True)))
    probabilities = low(shifted / lax.optimization_barrier(jnp.sum(shifted, axis=-1, keepdims=True)))
    heads_out = jnp.einsum('hqk,khd->qhd', probabilities, value_rows, precision=HIGHEST).reshape(length, D)
    heads_out = low_back(low(heads_out))
    hidden = inputs + low_back(product(heads_out, w_attn_out))
    ffn_in = low(layer_norm(hidden, gain_ffn))
    pre_act = low_back(product(ffn_in, w_up))
    activated = low(jax.nn.gelu(pre_act))
    return hidden + low_back(product(activated, w_down))

def expert_apply(seq_rows, weight_in, weight_out, centroid, norm_gain):
    sent_rows = low_back(low(seq_rows))
    gate_values = jax.nn.sigmoid(jnp.dot(sent_rows, centroid, precision=HIGHEST))
    expert_norm = low(layer_norm(sent_rows, norm_gain))
    expert_pre = low_back(product(expert_norm, weight_in))
    expert_act = low(jax.nn.gelu(expert_pre))
    expert_whole = sent_rows + low_back(product(expert_act, weight_out))
    return low_back(low(gate_values[:, None] * expert_whole))

def forward(inputs, route, w_qkv, w_attn_out, w_up, w_down, gain_attn, gain_ffn, expert_in, expert_out, centroids, expert_gain):
    dense_block = jax.checkpoint(dense_sequence)
    sequences = inputs.reshape(SEQS, TOK_DEV, D)
    dense_out = lax.map(lambda seq_rows: dense_block(seq_rows, w_qkv, w_attn_out, w_up, w_down, gain_attn, gain_ffn), sequences)
    ordered = jax.vmap(lambda seq_rows, route_order: seq_rows[route_order])(dense_out, route)
    grouped = ordered.reshape(N_EXPERT, N_REPLICA, N_EXPERT, PER_EXPERT, D).transpose(2, 0, 1, 3, 4)
    grouped = grouped.reshape(EXPERTS, SEQS * PER_EXPERT, D)
    expert_block = jax.checkpoint(expert_apply)
    returned = lax.map(lambda expert_item: expert_block(expert_item[0], expert_item[1], expert_item[2], expert_item[3], expert_item[4]), (grouped, expert_in, expert_out, centroids, expert_gain))
    back_rows = returned.reshape(N_EXPERT, N_EXPERT, N_REPLICA, PER_EXPERT, D).transpose(1, 2, 0, 3, 4)
    back_rows = back_rows.reshape(SEQS, TOK_DEV, D)
    placed = jax.vmap(lambda seq_rows, route_order: jnp.zeros_like(seq_rows).at[route_order].set(seq_rows))(back_rows, route)
    return (dense_out + placed).reshape(TOKENS, D)

def reference(tokens, route, w_qkv, w_attn_out, w_up, w_down, gain_attn, gain_ffn, expert_in, expert_out, centroids, expert_gain, cotangent):

    def run_forward(inputs, p_qkv, p_attn_out, p_up, p_down, p_gain_attn, p_gain_ffn, p_expert_in, p_expert_out, p_centroids, p_expert_gain):
        return forward(inputs, route, p_qkv, p_attn_out, p_up, p_down, p_gain_attn, p_gain_ffn, p_expert_in, p_expert_out, p_centroids, p_expert_gain)
    mixed, pullback = jax.vjp(run_forward, tokens.astype(jnp.float32), w_qkv.astype(jnp.float32), w_attn_out.astype(jnp.float32), w_up.astype(jnp.float32), w_down.astype(jnp.float32), gain_attn.astype(jnp.float32), gain_ffn.astype(jnp.float32), expert_in.astype(jnp.float32), expert_out.astype(jnp.float32), centroids.astype(jnp.float32), expert_gain.astype(jnp.float32))
    gradients = pullback(cotangent.astype(jnp.float32))
    return (mixed.astype(jnp.bfloat16), gradients[0], gradients[1], gradients[2], gradients[3], gradients[4], gradients[5], gradients[6], gradients[7], gradients[8], gradients[9], gradients[10])
```

```python
import math

import jax
import jax.numpy as jnp
from jax import lax
from jax.sharding import PartitionSpec as P

HEADS = 16


EPSILON = 1e-05


def layer_norm(values, norm_gain):
    centered = values - jnp.mean(values, axis=-1, keepdims=True)
    inverse = lax.rsqrt(jnp.mean(centered * centered, axis=-1, keepdims=True) + EPSILON)
    normed = centered * inverse
    return (normed * norm_gain, normed, inverse)


def layer_norm_back(grad_out, norm_gain, normed, inverse):
    grad_normed = grad_out * norm_gain
    grad_gain = jnp.sum(grad_out * normed, axis=0)
    grad_in = inverse * (
        grad_normed
        - jnp.mean(grad_normed, axis=-1, keepdims=True)
        - normed * jnp.mean(grad_normed * normed, axis=-1, keepdims=True)
    )
    return (grad_in, grad_gain)


def matmul_rows(left_rows, right_rows):
    return jnp.dot(left_rows, right_rows, preferred_element_type=jnp.float32)


def contract_rows(left_rows, right_rows):
    return lax.dot_general(
        left_rows, right_rows, (((0,), (0,)), ((), ())), preferred_element_type=jnp.float32
    )


def contract_cols(left_rows, right_rows):
    return lax.dot_general(
        left_rows, right_rows, (((1,), (1,)), ((), ())), preferred_element_type=jnp.float32
    )


def group_scores(head_item, causal, factor):
    scores = (
        jnp.einsum(
            "qhd,khd->hqk", head_item[:, 0], head_item[:, 1], preferred_element_type=jnp.float32
        )
        * factor
    )
    return jnp.where(causal, scores, -1e30)


def attend_group(head_item, causal, factor):
    scores = group_scores(head_item, causal, factor)
    largest = jnp.max(scores, axis=-1, keepdims=True)
    shifted = jnp.exp(scores - largest)
    totals = jnp.sum(shifted, axis=-1, keepdims=True)
    weights = (shifted / totals).astype(jnp.bfloat16)
    mixed_heads = jnp.einsum(
        "hqk,khd->qhd", weights, head_item[:, 2], preferred_element_type=jnp.float32
    )
    return (mixed_heads, largest + jnp.log(totals))


def attend_back(head_item, grad_heads, log_total, causal, factor):
    scores = group_scores(head_item, causal, factor)
    probabilities = jnp.exp(scores - log_total)
    weights = probabilities.astype(jnp.bfloat16)
    grad_value = jnp.einsum("hqk,qhd->khd", weights, grad_heads, preferred_element_type=jnp.float32)
    grad_probs = jnp.einsum(
        "qhd,khd->hqk", grad_heads, head_item[:, 2], preferred_element_type=jnp.float32
    )
    row_terms = jnp.sum(grad_probs * probabilities, axis=-1, keepdims=True)
    grad_scores = (probabilities * (grad_probs - row_terms)).astype(jnp.bfloat16)
    grad_query = (
        jnp.einsum("hqk,khd->qhd", grad_scores, head_item[:, 1], preferred_element_type=jnp.float32)
        * factor
    )
    grad_key = (
        jnp.einsum("hqk,qhd->khd", grad_scores, head_item[:, 0], preferred_element_type=jnp.float32)
        * factor
    )
    return jnp.stack([grad_query, grad_key, grad_value], axis=1)

ALL_AXES = ("expert", "replica")


def device_swap(values, bits):
    n_dev = lax.axis_size("expert") * lax.axis_size("replica")
    return lax.ppermute(values, ALL_AXES, [(d, d ^ bits) for d in range(n_dev)])


def swap_core(values):
    return device_swap(values, 1)


def swap_y(values):
    return device_swap(values, 2)


def swap_x(values):
    return device_swap(values, 4)


def plane_shift(values, step):
    n_dev = lax.axis_size("expert") * lax.axis_size("replica")
    return lax.ppermute(values, ALL_AXES, [(d, (d + 8 * step) % n_dev) for d in range(n_dev)])


def after(values, *earlier):
    return lax.optimization_barrier((values,) + earlier)[0]


def rows(*parts):
    return jnp.concatenate(parts, axis=0)


def cols(*parts):
    return jnp.concatenate(parts, axis=1)


def gather_own_core(planes, half):
    stacked = rows(*planes)
    left, right = stacked[:, :half], stacked[:, half:]
    n = left.shape[0]
    left_x = swap_x(left)
    right_y = swap_y(right)
    left_y = swap_y(rows(left, left_x))
    right_x = swap_x(rows(right, right_y))
    return cols(
        rows(left, left_x, left_y), rows(right, right_x[:n], right_y, right_x[n:])
    )


def scatter_sum(total, half, n_planes):
    n = total.shape[0] // 4
    low = total.astype(jnp.bfloat16)
    left, right = low[:, :half], low[:, half:]
    left_f, right_f = total[:, :half], total[:, half:]
    left_y = swap_y(left[2 * n :])
    right_x = swap_x(rows(right[n : 2 * n], right[3 * n :]))
    left_sum = left_f[: 2 * n] + left_y.astype(jnp.float32)
    right_sum = rows(right_f[:n], right_f[2 * n : 3 * n]) + right_x.astype(jnp.float32)
    left_x = swap_x(left_sum[n:].astype(jnp.bfloat16))
    right_y = swap_y(right_sum[n:].astype(jnp.bfloat16))
    both = cols(
        left_sum[:n] + left_x.astype(jnp.float32), right_sum[:n] + right_y.astype(jnp.float32)
    )
    m = n // n_planes
    low_both = both.astype(jnp.bfloat16)
    result = both[:m]
    for step in range(1, n_planes):
        moved = plane_shift(low_both[step * m : (step + 1) * m], step)
        result = result + moved.astype(jnp.float32)
    return result


def on_device(
    tokens,
    route,
    w_qkv,
    w_attn_out,
    w_up,
    w_down,
    gain_attn,
    gain_ffn,
    expert_in,
    expert_out,
    centroids,
    expert_gain,
    cotangent,
):
    length, features = tokens.shape
    per_group = min(HEADS, 4)
    groups = HEADS // per_group
    head_size = features // HEADS
    factor = 1.0 / math.sqrt(head_size)
    n_expert = lax.axis_size("expert")
    n_replica = lax.axis_size("replica")
    n_dev = n_expert * n_replica
    n_planes = n_dev // 8
    per_dest = length // n_expert
    bf16, f32 = jnp.bfloat16, jnp.float32
    replica = lax.axis_index("replica")
    me = lax.axis_index("expert") * n_replica + replica
    rel = lax.iota(jnp.int32, n_dev)
    rel_plane = rel % n_planes
    rel_x = (rel // n_planes) % 2
    rel_y = (rel // (2 * n_planes)) % 2
    rel_core = rel // (4 * n_planes)
    rel_dev = ((me // 8 + rel_plane) % n_planes) * 8 + (
        (me % 8) ^ (4 * rel_x + 2 * rel_y + rel_core)
    )
    shard = features // n_dev
    rel_feature = (rel_dev[:, None] * shard + lax.iota(jnp.int32, shard)[None]).reshape(features)
    to_rel = (lax.iota(jnp.int32, features)[:, None] == rel_feature[None]).astype(bf16)

    padded_gains = jnp.pad(
        jnp.stack([gain_attn, gain_ffn], axis=1), ((0, 0), (0, 126))
    )
    first = cols(w_qkv, w_attn_out, padded_gains)
    width_qkv = w_qkv.shape[1]
    hidden_size = w_up.shape[1]

    def planes_of(own):
        return [own] + [plane_shift(own, n_planes - step) for step in range(1, n_planes)]

    planes_first = planes_of(first)
    planes_up = planes_of(after(w_up, *planes_first[1:]))
    planes_down = planes_of(after(w_down, *planes_up[1:]))
    first_half = gather_own_core(planes_first, 2048)
    first_full = rows(first_half, swap_core(first_half))
    up_half = gather_own_core(planes_up, hidden_size // 2)
    down_half = gather_own_core(planes_down, features // 2)
    full_up = rows(up_half, swap_core(up_half))
    full_down = rows(down_half, swap_core(down_half))
    full_qkv = first_full[:, :width_qkv]
    full_out = first_full[:, width_qkv : width_qkv + features]
    gain_columns = first_full[:, width_qkv + features : width_qkv + features + 2]
    gains_plain = lax.dot_general(
        gain_columns, to_rel, (((0,), (1,)), ((), ())), preferred_element_type=f32
    )
    gains_rel = matmul_rows(gains_plain.astype(bf16), to_rel)
    gain_one = gains_rel[0]
    gain_two = gains_plain[1]
    gain_two_rel = gains_rel[1]

    def rel_order(low_values):
        return matmul_rows(low_values, to_rel).astype(bf16)

    inputs = tokens.astype(f32)
    inputs_rel = rel_order(tokens).astype(f32)
    attn_in, normed_one, inverse_one = layer_norm(inputs_rel, gain_one)
    attn_in = attn_in.astype(bf16)
    qkv_rows = matmul_rows(attn_in, full_qkv).astype(bf16)
    head_groups = jnp.moveaxis(qkv_rows.reshape(length, 3, groups, per_group, head_size), 2, 0)
    causal = (
        lax.broadcasted_iota(jnp.int32, (length, length), 0)
        >= lax.broadcasted_iota(jnp.int32, (length, length), 1)
    )[None]
    mixed_groups, log_totals = lax.map(
        lambda head_item: attend_group(head_item, causal, factor), head_groups
    )
    heads_out = jnp.moveaxis(mixed_groups, 0, 1).reshape(length, features).astype(bf16)
    heads_rel = rel_order(heads_out)
    hidden = inputs + matmul_rows(heads_rel, full_out)
    ffn_in, normed_two, inverse_two = layer_norm(hidden, gain_two)
    ffn_rel = rel_order(ffn_in.astype(bf16))
    pre_act = matmul_rows(ffn_rel, full_up)
    activated, gelu_back = jax.vjp(jax.nn.gelu, pre_act)
    activated = activated.astype(bf16)
    act_rel = jnp.take(activated.reshape(length, n_dev, -1), rel_dev, axis=1).reshape(length, -1)
    dense_out = hidden + matmul_rows(act_rel, full_down)

    route_pick = (route[0][:, None] == lax.iota(jnp.int32, length)[None]).astype(bf16)

    def to_expert(low_values):
        picked = matmul_rows(route_pick, low_values).astype(bf16)
        return lax.all_to_all(
            picked.reshape(n_expert, per_dest, features),
            "expert",
            split_axis=0,
            concat_axis=0,
            tiled=True,
        ).reshape(length, features)

    def to_home(low_values):
        back = lax.all_to_all(
            low_values.reshape(n_expert, per_dest, features),
            "expert",
            split_axis=0,
            concat_axis=0,
            tiled=True,
        ).reshape(length, features)
        return contract_rows(route_pick, back)

    arrived = to_expert(dense_out.astype(bf16))
    weight_in = expert_in[0]
    weight_out = expert_out[0]
    centroid = centroids[0]
    expert_norm_gain = expert_gain[0].astype(f32)
    expert_rows = arrived.astype(f32)
    gate_values = jax.nn.sigmoid(jnp.dot(arrived, centroid, preferred_element_type=f32))
    expert_norm, normed_three, inverse_three = layer_norm(expert_rows, expert_norm_gain)
    expert_norm = expert_norm.astype(bf16)
    expert_pre = matmul_rows(expert_norm, weight_in)
    expert_act, expert_gelu_back = jax.vjp(jax.nn.gelu, expert_pre)
    expert_act = expert_act.astype(bf16)
    expert_whole = expert_rows + matmul_rows(expert_act, weight_out)
    delta_rows = (gate_values[:, None] * expert_whole).astype(bf16)
    mixed = (dense_out + to_home(delta_rows)).astype(bf16)
    grad_delta = to_expert(cotangent).astype(f32)
    grad_gate = jnp.sum(grad_delta * expert_whole, axis=-1)
    grad_logit = grad_gate * gate_values * (1.0 - gate_values)
    grad_whole = gate_values[:, None] * grad_delta
    grad_whole_low = grad_whole.astype(bf16)
    grad_expert_act = contract_cols(grad_whole_low, weight_out)
    grad_expert_pre = expert_gelu_back(grad_expert_act)[0].astype(bf16)
    grad_expert_norm = contract_cols(grad_expert_pre, weight_in)
    grad_from_norm, grad_norm_gain = layer_norm_back(
        grad_expert_norm, expert_norm_gain, normed_three, inverse_three
    )
    grad_centroid = jnp.dot(grad_logit, expert_rows, precision=lax.Precision.HIGHEST)
    grad_rows = grad_whole + grad_logit[:, None] * centroid.astype(f32) + grad_from_norm
    grad_placed = to_home(grad_rows.astype(bf16))

    block = lax.iota(jnp.int32, n_replica)
    copy_order = replica ^ (2 * (block % 2) + block // 2)

    def copies_order(values):
        shape = values.shape[:-1]
        return jnp.take(values.reshape(*shape, n_replica, -1), copy_order, axis=-2).reshape(values.shape)

    def sum_copies(left, right, extra=None):
        left = copies_order(left)
        half = left.shape[1] // 2
        keep, send = contract_rows(left[:, :half], right), contract_rows(left[:, half:], right)
        if extra is not None:
            keep, send = cols(keep, extra[:half]), cols(send, extra[half:])
        total = keep + swap_core(send.astype(bf16)).astype(f32)
        n = half // 2
        return total[:n] + swap_y(total[n:].astype(bf16)).astype(f32)

    sum_expert_out = sum_copies(expert_act, grad_whole_low)
    vectors = jnp.pad(
        copies_order(jnp.stack([grad_centroid, grad_norm_gain])).T, ((0, 0), (0, 126))
    )
    sum_in_all = sum_copies(expert_norm, grad_expert_pre, vectors)
    sum_expert_in = sum_in_all[:, : weight_in.shape[1]]
    sum_vectors = sum_in_all[:, weight_in.shape[1] :]

    def sum_dense(left, right, extra=None):
        half = left.shape[1] // 2
        keep, send = contract_rows(left[:, :half], right), contract_rows(left[:, half:], right)
        if extra is not None:
            keep, send = cols(keep, extra[:half]), cols(send, extra[half:])
        total = keep + swap_core(send.astype(bf16)).astype(f32)
        return scatter_sum(total, right.shape[1] // 2, n_planes)

    grad_dense = cotangent.astype(f32) + grad_placed
    grad_dense_low = grad_dense.astype(bf16)
    sum_down = sum_dense(act_rel, grad_dense_low)
    grad_act_rel = contract_cols(grad_dense_low, full_down)
    plain_order = jnp.zeros((n_dev,), jnp.int32).at[rel_dev].set(lax.iota(jnp.int32, n_dev))
    grad_act = jnp.take(grad_act_rel.reshape(length, n_dev, -1), plain_order, axis=1).reshape(length, -1)
    grad_pre = gelu_back(grad_act)[0].astype(bf16)
    sum_up = sum_dense(ffn_rel, grad_pre)
    grad_ffn_rel = contract_cols(grad_pre, full_up)

    def plain_order_f32(values):
        high = values.astype(bf16)
        low = (values - high.astype(f32)).astype(bf16)
        return contract_cols(high, to_rel) + contract_cols(low, to_rel)

    grad_hidden_norm, grad_gain_ffn = layer_norm_back(
        plain_order_f32(grad_ffn_rel), gain_two, normed_two, inverse_two
    )
    grad_gain_ffn_rel = jnp.dot(grad_gain_ffn, to_rel.astype(f32), precision=lax.Precision.HIGHEST)
    grad_hidden = grad_dense + grad_hidden_norm
    grad_hidden_low = grad_hidden.astype(bf16)
    sum_out = sum_dense(heads_rel, grad_hidden_low)
    grad_heads_rel = contract_cols(grad_hidden_low, full_out).astype(bf16)
    grad_heads = contract_cols(grad_heads_rel, to_rel).astype(bf16)
    grad_groups = jnp.moveaxis(grad_heads.reshape(length, groups, per_group, head_size), 1, 0)
    grad_qkv_groups = lax.map(
        lambda group_item: attend_back(group_item[0], group_item[1], group_item[2], causal, factor),
        (head_groups, grad_groups, log_totals),
    )
    grad_qkv_rows = (
        jnp.moveaxis(grad_qkv_groups, 0, 2).reshape(length, 3 * features).astype(bf16)
    )
    grad_attn_rel = contract_cols(grad_qkv_rows, full_qkv)
    grad_input_norm, grad_gain_attn = layer_norm_back(
        grad_attn_rel, gain_one, normed_one, inverse_one
    )
    grad_tokens = grad_hidden + plain_order_f32(grad_input_norm)
    gain_grads = jnp.pad(jnp.stack([grad_gain_attn, grad_gain_ffn_rel], axis=1), ((0, 0), (0, 126)))
    sum_qkv_all = sum_dense(attn_in, grad_qkv_rows, gain_grads)
    sum_qkv = sum_qkv_all[:, :width_qkv]
    return (
        mixed,
        grad_tokens,
        sum_qkv,
        sum_out,
        sum_up,
        sum_down,
        sum_qkv_all[:, width_qkv],
        sum_qkv_all[:, width_qkv + 1],
        sum_expert_in[None],
        sum_expert_out[None],
        sum_vectors[None, :, 0],
        sum_vectors[None, :, 1],
    )


def solution(mesh):
    placed = (
        P(("expert", "replica"), None),
        P(("expert", "replica"), None),
        P(("expert", "replica"), None),
        P(("expert", "replica"), None),
        P(("expert", "replica"), None),
        P(("expert", "replica"), None),
        P(("expert", "replica")),
        P(("expert", "replica")),
        P("expert", None, None),
        P("expert", None, None),
        P("expert", None),
        P("expert", None),
        P(("expert", "replica"), None),
    )
    return jax.shard_map(
        on_device,
        mesh=mesh,
        in_specs=placed,
        out_specs=(
            P(("expert", "replica"), None),
            P(("expert", "replica"), None),
            P(("expert", "replica"), None),
            P(("expert", "replica"), None),
            P(("expert", "replica"), None),
            P(("expert", "replica"), None),
            P(("expert", "replica")),
            P(("expert", "replica")),
            P("expert", "replica", None),
            P("expert", "replica", None),
            P("expert", "replica"),
            P("expert", "replica"),
        ),
        check_vma=False,
    )
```

```python
import functools
import math

import jax
import jax.numpy as jnp
from jax import lax
from jax.experimental import pallas as pl
from jax.experimental.pallas import tpu as pltpu
from jax.sharding import PartitionSpec as P

HEADS = 16
EPSILON = 1e-05
ALL_AXES = ("expert", "replica")
VMEM_LIMIT = 58 * 2**20
GELU_SCALE = math.sqrt(2.0 / math.pi)
BF16, F32 = jnp.bfloat16, jnp.float32


def permuted(values, target):
    n_dev = lax.axis_size("expert") * lax.axis_size("replica")
    return lax.ppermute(values, ALL_AXES, [(d, target(d, n_dev)) for d in range(n_dev)])


def swap_core(values):
    return permuted(values, lambda d, n: d ^ 1)


def swap_first(values):
    return permuted(values, lambda d, n: d ^ (2 if d % 2 else 4))


def swap_second(values):
    return permuted(values, lambda d, n: d ^ (4 if d % 2 else 2))


def plane_shift(values, step):
    return permuted(values, lambda d, n: (d + 8 * step) % n)


def after(values, *earlier):
    return lax.optimization_barrier((values,) + earlier)[0]


def run_kernel(body, args, spaces, outs, scratch=(), flops=0, out_spaces=None):
    place = {
        "v": pl.BlockSpec(memory_space=pltpu.VMEM),
        "h": pl.BlockSpec(memory_space=pl.ANY),
        "s": pl.BlockSpec(memory_space=pltpu.SMEM),
    }
    moved = sum(a.size * a.dtype.itemsize for a in args)
    moved += sum(o.size * o.dtype.itemsize for o in outs)
    return pl.pallas_call(
        body,
        out_shape=list(outs),
        in_specs=[place[s] for s in spaces],
        out_specs=[place[s] for s in (out_spaces or "v" * len(outs))],
        scratch_shapes=list(scratch),
        cost_estimate=pl.CostEstimate(flops=flops, bytes_accessed=moved, transcendentals=0),
        compiler_params=pltpu.CompilerParams(vmem_limit_bytes=VMEM_LIMIT),
    )(*args)


def shaped(*shape, dtype=BF16):
    return jax.ShapeDtypeStruct(shape, dtype)


def dot_nn(left, right):
    return jnp.dot(left, right, preferred_element_type=F32)


def dot_nt(left, right):
    return lax.dot_general(left, right, (((1,), (1,)), ((), ())), preferred_element_type=F32)


def dot_tn(left, right):
    return lax.dot_general(left, right, (((0,), (0,)), ((), ())), preferred_element_type=F32)


def normed(values):
    centered = values - jnp.mean(values, axis=-1, keepdims=True)
    inverse = lax.rsqrt(jnp.mean(centered * centered, axis=-1, keepdims=True) + EPSILON)
    return centered * inverse, inverse


def norm_back(grad_normed, norm, inverse):
    return inverse * (
        grad_normed
        - jnp.mean(grad_normed, axis=-1, keepdims=True)
        - norm * jnp.mean(grad_normed * norm, axis=-1, keepdims=True)
    )


def gelu_both(values):
    square = values * values
    bent = jnp.tanh(GELU_SCALE * values * (1.0 + 0.044715 * square))
    half = 0.5 * (1.0 + bent)
    slope = half + 0.5 * values * (1.0 - bent * bent) * (
        GELU_SCALE * (1.0 + 3.0 * 0.044715 * square)
    )
    return values * half, slope


def row_start(pos, core, first, second, step, n_planes, block):
    x, y = pos[1], pos[2]
    flip = lambda v, on: 1 - v if on else v
    across = jnp.where(core == 0, flip(x, first), flip(x, second))
    along = jnp.where(core == 0, flip(y, second), flip(y, first))
    plane = lax.rem(pos[0] + step, n_planes)
    return pl.multiple_of(((plane * 2 + across) * 2 + along) * block, block)


PIECE_ORDER = ((0, 0), (1, 0), (0, 1), (1, 1))


def load_weight(pos, pieces, target, sem, n_planes):
    block = pieces[0].shape[0] // n_planes
    half = pieces[0].shape[1]
    for side in range(2):
        core = pos[3] if side == 0 else 1 - pos[3]
        lanes = pl.ds(pl.multiple_of(core * half, 128), half)
        for i, (first, second) in enumerate(PIECE_ORDER):
            for step in range(n_planes):
                row = row_start(pos, core, first, second, step, n_planes, block)
                pltpu.make_async_copy(
                    pieces[4 * side + i].at[pl.ds(step * block, block), :],
                    target.at[pl.ds(row, block), lanes],
                    sem,
                ).start()


def wait_whole(target, sem):
    pltpu.make_async_copy(target, target, sem).wait()


def causal_mask(length):
    return lax.broadcasted_iota(jnp.int32, (length, length), 0) >= lax.broadcasted_iota(
        jnp.int32, (length, length), 1
    )


def attend_kernel(n_planes, pos, tokens, *refs):
    pieces, refs = refs[:8], refs[8:]
    hidden, ffn_in, attn_in, qkv, heads, gains, weight, sem = refs
    length, width = tokens.shape
    load_weight(pos, pieces, weight, sem, n_planes)
    inputs = tokens[...].astype(F32)
    norm, _ = normed(inputs)
    wait_whole(weight, sem)
    columns = weight[:, 4 * width : 4 * width + 128].astype(F32)
    gains[...] = columns.T[:8]
    attn_in[...] = (norm * gains[0:1, :]).astype(BF16)
    for part in range(3):
        lanes = slice(part * width, (part + 1) * width)
        qkv[:, lanes] = dot_nn(attn_in[...], weight[:, lanes]).astype(BF16)
    head_size = width // HEADS
    causal = causal_mask(length)
    lane = lax.broadcasted_iota(jnp.int32, (1, 2 * head_size), 1)

    def pair(i, _):
        at = pl.multiple_of(i * 2 * head_size, 2 * head_size)
        query = qkv[:, pl.ds(at, 2 * head_size)] * (head_size**-0.5)
        key_rows = qkv[:, pl.ds(width + at, 2 * head_size)]
        value_rows = qkv[:, pl.ds(2 * width + at, 2 * head_size)]
        mixed = []
        for head in range(2):
            own = (lane // head_size) == head
            scores = dot_nt(jnp.where(own, query, 0).astype(BF16), key_rows)
            scores = jnp.where(causal, scores, -1e30)
            shifted = jnp.exp(scores - jnp.max(scores, axis=-1, keepdims=True))
            probs = shifted / jnp.sum(shifted, axis=-1, keepdims=True)
            mixed.append(dot_nn(probs.astype(BF16), value_rows))
        heads[:, pl.ds(at, 2 * head_size)] = jnp.where(lane < head_size, mixed[0], mixed[1]).astype(
            BF16
        )
        return 0

    lax.fori_loop(0, HEADS // 2, pair, 0)
    hidden[...] = inputs + dot_nn(heads[...], weight[:, 3 * width : 4 * width])
    norm_two, _ = normed(hidden[...])
    ffn_in[...] = (norm_two * gains[1:2, :]).astype(BF16)


def up_kernel(n_planes, pos, ffn_in, *refs):
    pieces, (act, slope, weight, sem) = refs[:8], refs[8:]
    load_weight(pos, pieces, weight, sem, n_planes)
    wait_whole(weight, sem)
    chunk = 512

    def step(i, _):
        lanes = pl.ds(pl.multiple_of(i * chunk, chunk), chunk)
        value, grad = gelu_both(dot_nn(ffn_in[...], weight[:, lanes]))
        act[:, lanes] = value.astype(BF16)
        slope[:, lanes] = grad
        return 0

    lax.fori_loop(0, weight.shape[1] // chunk, step, 0)


def down_kernel(n_planes, pos, act, hidden, pick, *refs):
    pieces, (dense_out, sent, weight, sem) = refs[:8], refs[8:]
    load_weight(pos, pieces, weight, sem, n_planes)
    wait_whole(weight, sem)
    dense_out[...] = hidden[...] + dot_nn(act[...], weight[...])
    sent[...] = dot_nn(pick[...], dense_out[...].astype(BF16)).astype(BF16)


def expert_kernel(
    arrived,
    grad_delta,
    centroid,
    norm_gain,
    weight_in,
    weight_out,
    delta,
    grad_rows,
    norm_low,
    act,
    grad_pre,
    whole_low,
    vectors,
    w_in,
    w_out,
    slope,
    sems,
):
    copy_in = pltpu.make_async_copy(weight_in.at[0], w_in, sems.at[0])
    copy_out = pltpu.make_async_copy(weight_out.at[0], w_out, sems.at[1])
    copy_in.start()
    copy_out.start()
    rows = arrived[...].astype(F32)
    center = centroid[...].astype(F32)
    gain = norm_gain[...].astype(F32)
    gate = jax.nn.sigmoid(jnp.sum(rows * center, axis=-1, keepdims=True))
    norm, inverse = normed(rows)
    norm_low[...] = (norm * gain).astype(BF16)
    grad_out = grad_delta[...].astype(F32)
    grad_whole = gate * grad_out
    whole_low[...] = grad_whole.astype(BF16)
    chunk = 512
    n_chunks = w_in.shape[1] // chunk
    copy_in.wait()

    def forward(i, _):
        lanes = pl.ds(pl.multiple_of(i * chunk, chunk), chunk)
        value, grad = gelu_both(dot_nn(norm_low[...], w_in[:, lanes]))
        act[:, lanes] = value.astype(BF16)
        slope[:, lanes] = grad
        return 0

    lax.fori_loop(0, n_chunks, forward, 0)
    copy_out.wait()
    whole = rows + dot_nn(act[...], w_out[...])
    delta[...] = (gate * whole).astype(BF16)
    grad_gate = jnp.sum(grad_out * whole, axis=-1, keepdims=True)
    grad_logit = grad_gate * gate * (1.0 - gate)

    def backward(i, _):
        lanes = pl.ds(pl.multiple_of(i * chunk, chunk), chunk)
        grad_act = dot_nt(whole_low[...], w_out[lanes, :])
        grad_pre[:, lanes] = (grad_act * slope[:, lanes]).astype(BF16)
        return 0

    lax.fori_loop(0, n_chunks, backward, 0)
    grad_norm = dot_nt(grad_pre[...], w_in[...])
    vectors[...] = jnp.zeros_like(vectors)
    vectors[0:1, :] = jnp.sum(grad_logit * rows, axis=0, keepdims=True)
    vectors[1:2, :] = jnp.sum(grad_norm * norm, axis=0, keepdims=True)
    back = norm_back(grad_norm * gain, norm, inverse)
    grad_rows[...] = (grad_whole + grad_logit * center + back).astype(BF16)


def copies_send_kernel(pos, left, right, sent):
    block = left.shape[1] // 4
    other = 1 - pos[3]
    tile = 256

    def step(i, _):
        outer, inner = lax.div(i, block // tile), lax.rem(i, block // tile)
        at = pl.multiple_of((2 * outer + other) * block + inner * tile, tile)
        sent[pl.ds(pl.multiple_of(i * tile, tile), tile), :] = dot_tn(
            left[:, pl.ds(at, tile)], right[...]
        ).astype(BF16)
        return 0

    lax.fori_loop(0, 2 * block // tile, step, 0)


def copies_keep_kernel(pos, left, right, received, sent, kept):
    block = left.shape[1] // 4
    core, y = pos[3], pos[2]
    tile = 256

    def step(i, _):
        rows = pl.ds(pl.multiple_of(i * tile, tile), tile)
        for turn, target in ((0, kept), (1, sent)):
            outer = 1 - y if turn else y
            at = pl.multiple_of((2 * outer + core) * block + i * tile, tile)
            there = pl.ds(pl.multiple_of(outer * block + i * tile, tile), tile)
            target[rows, :] = (
                dot_tn(left[:, pl.ds(at, tile)], right[...]) + received[there, :].astype(F32)
            ).astype(BF16)
        return 0

    lax.fori_loop(0, block // tile, step, 0)


def dense_grad_kernel(returned, cotangent, pick, grad_dense, grad_low):
    grad_dense[...] = cotangent[...].astype(F32) + dot_tn(pick[...], returned[...])
    grad_low[...] = grad_dense[...].astype(BF16)


def sum_send_kernel(pos, left, right, sent):
    half = right.shape[1] // 2
    lanes = pl.ds(pl.multiple_of((1 - pos[3]) * half, 128), half)
    tile = 256

    def step(i, _):
        rows = pl.ds(pl.multiple_of(i * tile, tile), tile)
        sent[rows, :] = dot_tn(left[:, rows], right[:, lanes]).astype(BF16)
        return 0

    lax.fori_loop(0, left.shape[1] // tile, step, 0)


def lay_out(pos, total, sent, kept, sems, n_planes):
    block = total.shape[0] // (4 * n_planes)
    for second in range(2):
        for step in range(n_planes):
            spot = pl.ds((second * n_planes + step) * block, block)
            for first, target in ((0, kept), (1, sent)):
                row = row_start(pos, pos[3], second, first, step, n_planes, block)
                pltpu.make_async_copy(
                    total.at[pl.ds(row, block), :], target.at[spot, :], sems.at[first]
                ).start()
    wait_whole(kept, sems.at[0])
    wait_whole(sent, sems.at[1])


def sum_keep_kernel(n_planes, pos, left, right, received, sent, kept, total, sems):
    half = right.shape[1] // 2
    lanes = pl.ds(pl.multiple_of(pos[3] * half, 128), half)
    tile = 256

    def step(i, _):
        rows = pl.ds(pl.multiple_of(i * tile, tile), tile)
        total[rows, :] = (
            dot_tn(left[:, rows], right[:, lanes]) + received[rows, :].astype(F32)
        ).astype(BF16)
        return 0

    lax.fori_loop(0, left.shape[1] // tile, step, 0)
    lay_out(pos, total, sent, kept, sems, n_planes)


def pre_back_kernel(n_planes, pos, grad_low, slope, *refs):
    pieces, (grad_pre, weight, sem) = refs[:8], refs[8:]
    load_weight(pos, pieces, weight, sem, n_planes)
    wait_whole(weight, sem)
    chunk = 512

    def step(i, _):
        lanes = pl.ds(pl.multiple_of(i * chunk, chunk), chunk)
        grad_pre[:, lanes] = (dot_nt(grad_low[...], weight[lanes, :]) * slope[:, lanes]).astype(
            BF16
        )
        return 0

    lax.fori_loop(0, weight.shape[0] // chunk, step, 0)


def hidden_back_kernel(n_planes, pos, grad_pre, hidden, grad_dense, gains, *refs):
    pieces, (grad_hidden, grad_low, grad_gain, weight, sem) = refs[:8], refs[8:]
    load_weight(pos, pieces, weight, sem, n_planes)
    norm, inverse = normed(hidden[...])
    wait_whole(weight, sem)
    grad_in = dot_nt(grad_pre[...], weight[...])
    grad_gain[...] = jnp.zeros_like(grad_gain)
    grad_gain[0:1, :] = jnp.sum(grad_in * norm, axis=0, keepdims=True)
    grad_hidden[...] = grad_dense[...] + norm_back(grad_in * gains[1:2, :], norm, inverse)
    grad_low[...] = grad_hidden[...].astype(BF16)


def attend_back_kernel(n_planes, pos, grad_low, qkv, tokens, grad_hidden, gains, *refs):
    pieces, refs = refs[:8], refs[8:]
    grad_qkv, grad_tokens, grad_gain, grad_heads, weight, sem = refs
    length, width = tokens.shape
    head_size = width // HEADS
    load_weight(pos, pieces, weight, sem, n_planes)
    inputs = tokens[...].astype(F32)
    norm, inverse = normed(inputs)
    causal = causal_mask(length)
    lane = lax.broadcasted_iota(jnp.int32, (1, 2 * head_size), 1)
    wait_whole(weight, sem)
    grad_heads[...] = dot_nt(grad_low[...], weight[:, 3 * width : 4 * width]).astype(BF16)
    factor = head_size**-0.5

    def pair(i, _):
        at = pl.multiple_of(i * 2 * head_size, 2 * head_size)
        query = qkv[:, pl.ds(at, 2 * head_size)]
        key_rows = qkv[:, pl.ds(width + at, 2 * head_size)]
        value_rows = qkv[:, pl.ds(2 * width + at, 2 * head_size)]
        grad_out = grad_heads[:, pl.ds(at, 2 * head_size)]
        sums = [0.0, 0.0, 0.0]
        for head in range(2):
            own = (lane // head_size) == head
            masked = lambda v: jnp.where(own, v, 0).astype(BF16)
            own_query, own_grad = masked(query), masked(grad_out)
            scores = dot_nt(own_query, key_rows) * factor
            scores = jnp.where(causal, scores, -1e30)
            shifted = jnp.exp(scores - jnp.max(scores, axis=-1, keepdims=True))
            probs = shifted / jnp.sum(shifted, axis=-1, keepdims=True)
            grad_probs = dot_nt(own_grad, value_rows)
            row_terms = jnp.sum(probs * grad_probs, axis=-1, keepdims=True)
            grad_scores = (probs * (grad_probs - row_terms)).astype(BF16)
            sums[0] = sums[0] + dot_nn(grad_scores, masked(key_rows)) * factor
            sums[1] = sums[1] + dot_tn(grad_scores, own_query) * factor
            sums[2] = sums[2] + dot_tn(probs.astype(BF16), own_grad)
        for part in range(3):
            grad_qkv[:, pl.ds(part * width + at, 2 * head_size)] = sums[part].astype(BF16)
        return 0

    lax.fori_loop(0, HEADS // 2, pair, 0)
    grad_in = dot_nt(grad_qkv[...], weight[:, : 3 * width])
    grad_gain[...] = jnp.zeros_like(grad_gain)
    grad_gain[0:1, :] = jnp.sum(grad_in * norm, axis=0, keepdims=True)
    grad_tokens[...] = grad_hidden[...] + norm_back(grad_in * gains[0:1, :], norm, inverse)


def first_send_kernel(pos, attn_in, heads, grad_qkv, grad_low, sent):
    first_columns(1 - pos[3], attn_in, heads, grad_qkv, grad_low, sent, None)


def first_columns(half, attn_in, heads, grad_qkv, grad_low, target, received):
    width = attn_in.shape[1]
    tile = 256

    def fill(lanes, left, right_of):
        def step(i, _):
            rows = pl.ds(pl.multiple_of(i * tile, tile), tile)
            value = dot_tn(left[:, rows], right_of())
            if received is not None:
                value = value + received[rows, lanes].astype(F32)
            target[rows, lanes] = value.astype(BF16)
            return 0

        lax.fori_loop(0, width // tile, step, 0)

    low, high = pl.ds(0, width), pl.ds(width, width)
    fill(
        low, attn_in, lambda: grad_qkv[:, pl.ds(pl.multiple_of(half * 2 * width, 128), width)]
    )

    @pl.when(half == 0)
    def _():
        fill(high, attn_in, lambda: grad_qkv[:, width : 2 * width])

    @pl.when(half == 1)
    def _():
        fill(high, heads, lambda: grad_low[...])


def first_keep_kernel(
    n_planes, pos, attn_in, heads, grad_qkv, grad_low, received, sent, kept, total, sems
):
    first_columns(pos[3], attn_in, heads, grad_qkv, grad_low, total, received)
    lay_out(pos, total, sent, kept, sems, n_planes)


def own_columns(values, core):
    half = values.shape[1] // 2
    mine = lax.dynamic_slice_in_dim(values, core * half, half, 1)
    other = lax.dynamic_slice_in_dim(values, (1 - core) * half, half, 1)
    got = swap_core(other)
    return jnp.where(
        core == 0, jnp.concatenate([mine, got], axis=0), jnp.concatenate([got, mine], axis=0)
    )


def finish_sum(sent, kept, core, n_planes):
    total = kept.astype(F32) + swap_second(sent).astype(F32)
    quarter = total.shape[0] // 2
    got = swap_first(total[quarter:].astype(BF16))
    total = total[:quarter] + got.astype(F32)
    block = quarter // n_planes
    result = total[:block]
    for step in range(1, n_planes):
        moved = plane_shift(total[step * block : (step + 1) * block].astype(BF16), step)
        result = result + moved.astype(F32)
    shard = block // 2
    mine = lax.dynamic_slice_in_dim(result, core * shard, shard, 0)
    other = lax.dynamic_slice_in_dim(result, (1 - core) * shard, shard, 0)
    got = swap_core(other.astype(BF16)).astype(F32)
    return jnp.where(
        core == 0, jnp.concatenate([mine, got], axis=1), jnp.concatenate([got, mine], axis=1)
    )


def on_device(
    tokens,
    route,
    w_qkv,
    w_attn_out,
    w_up,
    w_down,
    gain_attn,
    gain_ffn,
    expert_in,
    expert_out,
    centroids,
    expert_gain,
    cotangent,
):
    length, features = tokens.shape
    n_expert = lax.axis_size("expert")
    n_replica = lax.axis_size("replica")
    n_dev = n_expert * n_replica
    n_planes = n_dev // 8
    per_dest = length // n_expert
    hidden_size = w_up.shape[1]
    replica = lax.axis_index("replica")
    me = lax.axis_index("expert") * n_replica + replica
    core = me % 2
    pos = jnp.stack([me // 8, (me // 4) % 2, (me // 2) % 2, core]).astype(jnp.int32)
    route_pick = (route[0][:, None] == lax.iota(jnp.int32, length)[None]).astype(BF16)

    def to_expert(picked):
        return lax.all_to_all(
            picked.reshape(n_expert, per_dest, features),
            "expert",
            split_axis=0,
            concat_axis=0,
            tiled=True,
        ).reshape(length, features)

    padded_gains = jnp.pad(jnp.stack([gain_attn, gain_ffn], axis=1), ((0, 0), (0, 254)))
    first = jnp.concatenate([w_qkv, w_attn_out, padded_gains], axis=1)
    owned = [own_columns(v, core) for v in (first, w_up, w_down)]
    gathered = []
    shifts, earlier = (), [(), ()]
    for own in owned:
        start = after(own, *shifts) if shifts else own
        shifts = tuple(plane_shift(start, n_planes - step) for step in range(1, n_planes))
        stack = jnp.concatenate([own, *shifts], axis=0)
        one = swap_first(after(stack, *earlier[0]))
        two = swap_second(after(stack, *earlier[1]))
        both = swap_second(one)
        earlier = [(two,), (both,)]
        mine = [stack, one, two, both]
        gathered.append(mine + [swap_core(v) for v in mine])
    first_pieces, up_pieces, down_pieces = gathered
    grad_delta = to_expert(jnp.dot(route_pick, cotangent, preferred_element_type=F32).astype(BF16))

    wide = first.shape[1]
    planes = functools.partial
    weight_first = pltpu.VMEM((features, wide), BF16)
    weight_up = pltpu.VMEM((features, hidden_size), BF16)
    weight_down = pltpu.VMEM((hidden_size, features), BF16)
    sem, two_sems = pltpu.SemaphoreType.DMA, pltpu.SemaphoreType.DMA((2,))
    unit = 2 * length * features * features

    hidden, ffn_in, attn_in, qkv, heads, gains = run_kernel(
        planes(attend_kernel, n_planes),
        [pos, tokens, *first_pieces],
        "sv" + "h" * 8,
        [
            shaped(length, features, dtype=F32),
            shaped(length, features),
            shaped(length, features),
            shaped(length, 3 * features),
            shaped(length, features),
            shaped(8, features, dtype=F32),
        ],
        [weight_first, sem],
        flops=5 * unit,
    )
    act, slope = run_kernel(
        planes(up_kernel, n_planes),
        [pos, ffn_in, *up_pieces],
        "sv" + "h" * 8,
        [shaped(length, hidden_size), shaped(length, hidden_size, dtype=F32)],
        [weight_up, sem],
        flops=4 * unit,
    )
    dense_out, sent = run_kernel(
        planes(down_kernel, n_planes),
        [pos, act, hidden, route_pick, *down_pieces],
        "svvv" + "h" * 8,
        [shaped(length, features, dtype=F32), shaped(length, features)],
        [weight_down, sem],
        flops=4 * unit,
    )
    arrived = to_expert(after(sent, grad_delta))
    inner = expert_in.shape[2]
    delta, grad_rows, expert_norm, expert_act, expert_grad_pre, whole_low, vectors = run_kernel(
        expert_kernel,
        [arrived, grad_delta, centroids, expert_gain, expert_in, expert_out],
        "vvvvhh",
        [
            shaped(length, features),
            shaped(length, features),
            shaped(length, features),
            shaped(length, inner),
            shaped(length, inner),
            shaped(length, features),
            shaped(8, features, dtype=F32),
        ],
        [
            pltpu.VMEM((features, inner), BF16),
            pltpu.VMEM((inner, features), BF16),
            pltpu.VMEM((length, inner), F32),
            two_sems,
        ],
        flops=16 * unit,
    )
    returned = to_expert(grad_rows)
    delta_home = to_expert(after(delta, returned))
    mixed = (
        dense_out
        + lax.dot_general(
            route_pick, delta_home, (((0,), (0,)), ((), ())), preferred_element_type=F32
        )
    ).astype(BF16)

    def copies_sum(left, right):
        rows_out = left.shape[1]
        (send,) = run_kernel(
            copies_send_kernel,
            [pos, left, right],
            "svv",
            [shaped(rows_out // 2, right.shape[1])],
            flops=2 * unit,
        )
        got = swap_core(send)
        send, kept = run_kernel(
            copies_keep_kernel,
            [pos, left, right, got],
            "svvv",
            [shaped(rows_out // 4, right.shape[1])] * 2,
            flops=2 * unit,
        )
        return kept.astype(F32) + permuted(send, lambda d, n: d ^ 2).astype(F32)

    sum_expert_out = copies_sum(expert_act, whole_low)
    sum_expert_in = copies_sum(expert_norm, expert_grad_pre)
    vectors = vectors[:2]
    vectors = vectors + swap_core(vectors)
    vectors = vectors + permuted(vectors, lambda d, n: d ^ 2)
    part = features // n_replica
    vectors = lax.dynamic_slice_in_dim(vectors, replica * part, part, 1)

    def send_half(left, right):
        (send,) = run_kernel(
            sum_send_kernel,
            [pos, left, right],
            "svv",
            [shaped(left.shape[1], right.shape[1] // 2)],
            flops=2 * unit,
        )
        return swap_core(send)

    def keep_half(left, right, got):
        rows_out, half = got.shape
        send, kept = run_kernel(
            planes(sum_keep_kernel, n_planes),
            [pos, left, right, got],
            "svvv",
            [shaped(rows_out // 2, half)] * 2,
            [pltpu.VMEM((rows_out, half), BF16), two_sems],
            flops=2 * unit,
            out_spaces="hh",
        )
        return finish_sum(send, kept, core, n_planes)

    grad_dense, grad_dense_low = run_kernel(
        dense_grad_kernel,
        [returned, cotangent, route_pick],
        "vvv",
        [shaped(length, features, dtype=F32), shaped(length, features)],
        flops=unit // 4,
    )
    got_down = send_half(act, grad_dense_low)
    (grad_pre,) = run_kernel(
        planes(pre_back_kernel, n_planes),
        [pos, grad_dense_low, slope, *down_pieces],
        "svv" + "h" * 8,
        [shaped(length, hidden_size)],
        [weight_down, sem],
        flops=4 * unit,
    )
    got_up = send_half(ffn_in, grad_pre)
    sum_down = keep_half(act, grad_dense_low, got_down)
    grad_hidden, grad_hidden_low, grad_gain_two = run_kernel(
        planes(hidden_back_kernel, n_planes),
        [pos, grad_pre, hidden, grad_dense, gains, *up_pieces],
        "svvvv" + "h" * 8,
        [
            shaped(length, features, dtype=F32),
            shaped(length, features),
            shaped(8, features, dtype=F32),
        ],
        [weight_up, sem],
        flops=4 * unit,
    )
    sum_up = keep_half(ffn_in, grad_pre, got_up)
    grad_qkv, grad_tokens, grad_gain_one = run_kernel(
        planes(attend_back_kernel, n_planes),
        [pos, grad_hidden_low, qkv, tokens, grad_hidden, gains, *first_pieces],
        "svvvvv" + "h" * 8,
        [
            shaped(length, 3 * features),
            shaped(length, features, dtype=F32),
            shaped(8, features, dtype=F32),
        ],
        [pltpu.VMEM((length, features), BF16), weight_first, sem],
        flops=8 * unit,
    )
    lefts = [pos, attn_in, heads, grad_qkv, grad_hidden_low]
    (send,) = run_kernel(
        first_send_kernel,
        lefts,
        "svvvv",
        [shaped(features, 2 * features)],
        flops=2 * unit,
    )
    got_first = swap_core(send)
    send, kept = run_kernel(
        planes(first_keep_kernel, n_planes),
        [*lefts, got_first],
        "svvvvv",
        [shaped(features // 2, 2 * features)] * 2,
        [pltpu.VMEM((features, 2 * features), BF16), two_sems],
        flops=2 * unit,
        out_spaces="hh",
    )
    sum_first = finish_sum(send, kept, core, n_planes)
    gain_grads = jnp.concatenate([grad_gain_one[:1], grad_gain_two[:1]], axis=0)
    gain_grads = gain_grads + swap_core(gain_grads)
    gain_grads = gain_grads + swap_first(gain_grads)
    gain_grads = gain_grads + swap_second(gain_grads)
    gain_grads = gain_grads + sum(plane_shift(gain_grads, step) for step in range(1, n_planes))
    shard = features // n_dev
    gain_grads = lax.dynamic_slice_in_dim(gain_grads, me * shard, shard, 1)
    width_qkv = w_qkv.shape[1]
    return (
        mixed,
        grad_tokens,
        sum_first[:, :width_qkv],
        sum_first[:, width_qkv:],
        sum_up,
        sum_down,
        gain_grads[0],
        gain_grads[1],
        sum_expert_in[None],
        sum_expert_out[None],
        vectors[:1],
        vectors[1:],
    )


def solution(mesh):
    placed = (
        P(("expert", "replica"), None),
        P(("expert", "replica"), None),
        P(("expert", "replica"), None),
        P(("expert", "replica"), None),
        P(("expert", "replica"), None),
        P(("expert", "replica"), None),
        P(("expert", "replica")),
        P(("expert", "replica")),
        P("expert", None, None),
        P("expert", None, None),
        P("expert", None),
        P("expert", None),
        P(("expert", "replica"), None),
    )
    return jax.shard_map(
        on_device,
        mesh=mesh,
        in_specs=placed,
        out_specs=(
            P(("expert", "replica"), None),
            P(("expert", "replica"), None),
            P(("expert", "replica"), None),
            P(("expert", "replica"), None),
            P(("expert", "replica"), None),
            P(("expert", "replica"), None),
            P(("expert", "replica")),
            P(("expert", "replica")),
            P("expert", "replica", None),
            P("expert", "replica", None),
            P("expert", "replica"),
            P("expert", "replica"),
        ),
        check_vma=False,
    )
```

```python
import functools
import math

import jax
import jax.numpy as jnp
from jax import lax
from jax.experimental import pallas as pl
from jax.experimental.pallas import tpu as pltpu
from jax.sharding import PartitionSpec as P

HEADS = 16
EPSILON = 1e-05
ALL_AXES = ("expert", "replica")
VMEM_LIMIT = 58 * 2**20
GELU_SCALE = math.sqrt(2.0 / math.pi)
BF16, F32 = jnp.bfloat16, jnp.float32


def permuted(values, target):
    n_dev = lax.axis_size("expert") * lax.axis_size("replica")
    return lax.ppermute(values, ALL_AXES, [(d, target(d, n_dev)) for d in range(n_dev)])


def swap_core(values):
    return permuted(values, lambda d, n: d ^ 1)


def swap_first(values):
    return permuted(values, lambda d, n: d ^ (2 if d % 2 else 4))


def swap_second(values):
    return permuted(values, lambda d, n: d ^ (4 if d % 2 else 2))


def swap_x(values):
    return permuted(values, lambda d, n: d ^ 4)


def swap_y(values):
    return permuted(values, lambda d, n: d ^ 2)


def swap_plane(values, bit):
    return permuted(values, lambda d, n: d ^ (8 * bit))


def after(values, *earlier):
    return lax.optimization_barrier((values,) + earlier)[0]


HINT = 30


def body_name(body):
    return getattr(body, "func", body).__name__


def run_kernel(body, args, spaces, outs, scratch=(), flops=0, out_spaces=None):
    place = {
        "v": pl.BlockSpec(memory_space=pltpu.VMEM),
        "h": pl.BlockSpec(memory_space=pl.ANY),
        "s": pl.BlockSpec(memory_space=pltpu.SMEM),
    }
    moved = sum(a.size * a.dtype.itemsize for a in args)
    moved += sum(o.size * o.dtype.itemsize for o in outs)
    return pl.pallas_call(
        body,
        name=body_name(body),
        out_shape=list(outs),
        in_specs=[place[s] for s in spaces],
        out_specs=[place[s] for s in (out_spaces or "v" * len(outs))],
        scratch_shapes=list(scratch),
        cost_estimate=pl.CostEstimate(flops=int(flops * HINT), bytes_accessed=int(moved * HINT), transcendentals=0),
        compiler_params=pltpu.CompilerParams(vmem_limit_bytes=VMEM_LIMIT),
    )(*args)


def shaped(*shape, dtype=BF16):
    return jax.ShapeDtypeStruct(shape, dtype)


def dot_nn(left, right):
    return jnp.dot(left, right, preferred_element_type=F32)


def dot_nt(left, right):
    return lax.dot_general(left, right, (((1,), (1,)), ((), ())), preferred_element_type=F32)


def dot_tn(left, right):
    return lax.dot_general(left, right, (((0,), (0,)), ((), ())), preferred_element_type=F32)


def normed(values):
    centered = values - jnp.mean(values, axis=-1, keepdims=True)
    inverse = lax.rsqrt(jnp.mean(centered * centered, axis=-1, keepdims=True) + EPSILON)
    return centered * inverse, inverse


def norm_back(grad_normed, norm, inverse):
    return inverse * (
        grad_normed
        - jnp.mean(grad_normed, axis=-1, keepdims=True)
        - norm * jnp.mean(grad_normed * norm, axis=-1, keepdims=True)
    )


def gelu_both(values):
    square = values * values
    bent = jnp.tanh(GELU_SCALE * values * (1.0 + 0.044715 * square))
    half = 0.5 * (1.0 + bent)
    slope = half + 0.5 * values * (1.0 - bent * bent) * (
        GELU_SCALE * (1.0 + 3.0 * 0.044715 * square)
    )
    return values * half, slope


def row_start(pos, core, first, second, step, n_planes, block):
    x, y = pos[1], pos[2]
    flip = lambda v, on: 1 - v if on else v
    across = jnp.where(core == 0, flip(x, first), flip(x, second))
    along = jnp.where(core == 0, flip(y, second), flip(y, first))
    plane = pos[0] ^ step
    return pl.multiple_of(((plane * 2 + across) * 2 + along) * block, block)


PIECE_ORDER = ((0, 0), (1, 0), (0, 1), (1, 1))


def load_weight(pos, sides, target, sems, n_planes, by_plane):
    block = target.shape[0] // (4 * n_planes)
    part = n_planes // 2
    order = [(far, *chip) for far in range(2) for chip in PIECE_ORDER]
    copies = []
    for side, pieces in enumerate(sides):
        half = pieces[0].shape[1]
        core = pos[3] if side == 0 else 1 - pos[3]
        lanes = pl.ds(pl.multiple_of(core * half, 128), half)
        spots = [(piece, at) for piece in pieces for at in range(0, piece.shape[0], block * part)]
        for (far, first, second), (piece, at) in zip(order, spots, strict=True):
            for step in range(part):
                row = row_start(pos, core, first, second, far * part + step, n_planes, block)
                copies.append(
                    (
                        far * part + step if by_plane else side,
                        pltpu.make_async_copy(
                            piece.at[pl.ds(at + step * block, block), :],
                            target.at[pl.ds(row, block), lanes],
                            sems.at[far * part + step] if by_plane else sems.at[core],
                        ),
                    )
                )
    for _, copy in sorted(copies, key=lambda pair: pair[0]):
        copy.start()


def wait_half(target, core, sems):
    half = target.at[:, : target.shape[1] // 2]
    pltpu.make_async_copy(half, half, sems.at[core]).wait()


def wait_step(pos, target, sems, step, n_planes):
    rows = target.shape[0] // n_planes
    part = target.at[:rows, :]
    pltpu.make_async_copy(part, part, sems.at[step]).wait()
    return pl.multiple_of((pos[0] ^ step) * rows, rows)


def wait_whole(target, sem):
    pltpu.make_async_copy(target, target, sem).wait()


def causal_mask(length):
    return lax.broadcasted_iota(jnp.int32, (length, length), 0) >= lax.broadcasted_iota(
        jnp.int32, (length, length), 1
    )


def take_sides(refs, split):
    mine, both = split[0], sum(split)
    return (refs[:mine], refs[mine:both]), refs[both:]


def attend_kernel(n_planes, split, pos, tokens, *refs):
    sides, refs = take_sides(refs, split)
    hidden, ffn_in, attn_in, qkv, heads, gains, weight, sem = refs
    length, width = tokens.shape
    load_weight(pos, sides, weight, sem, n_planes, False)
    inputs = tokens[...].astype(F32)
    norm, _ = normed(inputs)
    wait_half(weight, 1, sem)
    columns = weight[:, 4 * width : 4 * width + 128].astype(F32)
    gains[...] = columns.T[:8]
    attn_in[...] = (norm * gains[0:1, :]).astype(BF16)
    wait_half(weight, 0, sem)
    for part in range(3):
        lanes = slice(part * width, (part + 1) * width)
        qkv[:, lanes] = dot_nn(attn_in[...], weight[:, lanes]).astype(BF16)
    head_size = width // HEADS
    causal = causal_mask(length)
    lane = lax.broadcasted_iota(jnp.int32, (1, 2 * head_size), 1)

    def pair(i, _):
        at = pl.multiple_of(i * 2 * head_size, 2 * head_size)
        query = qkv[:, pl.ds(at, 2 * head_size)] * (head_size**-0.5)
        key_rows = qkv[:, pl.ds(width + at, 2 * head_size)]
        value_rows = qkv[:, pl.ds(2 * width + at, 2 * head_size)]
        mixed = []
        for head in range(2):
            own = (lane // head_size) == head
            scores = dot_nt(jnp.where(own, query, 0).astype(BF16), key_rows)
            scores = jnp.where(causal, scores, -1e30)
            shifted = jnp.exp(scores - jnp.max(scores, axis=-1, keepdims=True))
            probs = shifted / jnp.sum(shifted, axis=-1, keepdims=True)
            mixed.append(dot_nn(probs.astype(BF16), value_rows))
        heads[:, pl.ds(at, 2 * head_size)] = jnp.where(lane < head_size, mixed[0], mixed[1]).astype(
            BF16
        )
        return 0

    lax.fori_loop(0, HEADS // 2, pair, 0)
    hidden[...] = inputs + dot_nn(heads[...], weight[:, 3 * width : 4 * width])
    norm_two, _ = normed(hidden[...])
    ffn_in[...] = (norm_two * gains[1:2, :]).astype(BF16)


def up_kernel(n_planes, split, pos, ffn_in, *refs):
    sides, (act, slope, weight, sem) = take_sides(refs, split)
    load_weight(pos, sides, weight, sem, n_planes, False)
    chunk = 512
    half = weight.shape[1] // 2
    for side in range(2):
        core = pos[3] if side == 0 else 1 - pos[3]
        wait_half(weight, core, sem)
        for i in range(half // chunk):
            lanes = pl.ds(pl.multiple_of(core * half + i * chunk, chunk), chunk)
            value, grad = gelu_both(dot_nn(ffn_in[...], weight[:, lanes]))
            act[:, lanes] = value.astype(BF16)
            slope[:, lanes] = grad


def down_kernel(n_planes, split, pos, act, hidden, pick, *refs):
    sides, (dense_out, sent, weight, sem) = take_sides(refs, split)
    load_weight(pos, sides, weight, sem, n_planes, True)
    rows = weight.shape[0] // n_planes
    total = hidden[...]
    for step in range(n_planes):
        at = pl.ds(wait_step(pos, weight, sem, step, n_planes), rows)
        total = total + dot_nn(act[:, at], weight[at, :])
    dense_out[...] = total
    sent[...] = dot_nn(pick[...], total.astype(BF16)).astype(BF16)


def expert_kernel(
    pos,
    arrived,
    grad_delta,
    centroid,
    norm_gain,
    weight_in,
    weight_out,
    delta,
    grad_rows,
    norm_low,
    kept,
    sent_low,
    sent_high,
    whole_low,
    grad_pre,
    vectors,
    w_in,
    w_out,
    act,
    slope,
    sems,
):
    chunk = 512
    n_chunks = w_in.shape[1] // chunk
    spans = [pl.ds(i * chunk, chunk) for i in range(n_chunks)]
    copies_in = [
        pltpu.make_async_copy(weight_in.at[0, :, span], w_in.at[:, span], sems.at[0, i])
        for i, span in enumerate(spans)
    ]
    copies_out = [
        pltpu.make_async_copy(weight_out.at[0, span, :], w_out.at[span, :], sems.at[1, i])
        for i, span in enumerate(spans)
    ]
    for copy in copies_in + copies_out:
        copy.start()
    rows = arrived[...].astype(F32)
    center = centroid[...].astype(F32)
    gain = norm_gain[...].astype(F32)
    gate = jax.nn.sigmoid(jnp.sum(rows * center, axis=-1, keepdims=True))
    norm, inverse = normed(rows)
    norm_low[...] = (norm * gain).astype(BF16)
    grad_out = grad_delta[...].astype(F32)
    grad_whole = gate * grad_out
    whole_low[...] = grad_whole.astype(BF16)
    for copy, span in zip(copies_in, spans):
        copy.wait()
        value, grad = gelu_both(dot_nn(norm_low[...], w_in[:, span]))
        act[:, span] = value.astype(BF16)
        slope[:, span] = grad
    half = act.shape[1] // 2
    kept[:, :half] = act[:, pl.ds(pl.multiple_of(pos[2] * half, 128), half)]
    other = pl.multiple_of((1 - pos[2]) * half, 128)
    sent_low[...] = act[:, pl.ds(other, half // 2)]
    sent_high[...] = act[:, pl.ds(pl.multiple_of(other + half // 2, 128), half // 2)]
    kept[:, half:] = whole_low[...]
    for copy in copies_out:
        copy.wait()
    whole = rows + dot_nn(act[...], w_out[...])
    delta[...] = (gate * whole).astype(BF16)
    grad_gate = jnp.sum(grad_out * whole, axis=-1, keepdims=True)
    grad_logit = grad_gate * gate * (1.0 - gate)

    for span in spans:
        grad_act = dot_nt(whole_low[...], w_out[span, :])
        grad_pre[:, span] = (grad_act * slope[:, span]).astype(BF16)
    grad_norm = dot_nt(grad_pre[...], w_in[...])
    vectors[...] = jnp.zeros_like(vectors)
    vectors[0:1, :] = jnp.sum(grad_logit * rows, axis=0, keepdims=True)
    vectors[1:2, :] = jnp.sum(grad_norm * norm, axis=0, keepdims=True)
    back = norm_back(grad_norm * gain, norm, inverse)
    grad_rows[...] = (grad_whole + grad_logit * center + back).astype(BF16)


VECTOR_ROWS = 16


def put_vectors(target, at, one, two):
    width = one.shape[1]
    row = lax.broadcasted_iota(jnp.int32, (VECTOR_ROWS, width), 0)
    both = jnp.where(row == 0, one, jnp.where(row == 1, two, 0.0))
    target[at : at + VECTOR_ROWS, :] = jnp.zeros((VECTOR_ROWS, target.shape[1]), BF16)
    target[at : at + VECTOR_ROWS, :width] = both.astype(BF16)


def copies_send_kernel(pos, left, right, vectors, sent):
    block = left.shape[1] // 4
    other = 1 - pos[3]
    tile = 256

    def step(i, _):
        outer, inner = lax.div(i, block // tile), lax.rem(i, block // tile)
        at = pl.multiple_of((2 * outer + other) * block + inner * tile, tile)
        sent[pl.ds(pl.multiple_of(i * tile, tile), tile), :] = dot_tn(
            left[:, pl.ds(at, tile)], right[...]
        ).astype(BF16)
        return 0

    lax.fori_loop(0, 2 * block // tile, step, 0)
    put_vectors(sent, 2 * block, vectors[:1, :], vectors[1:2, :])


def copies_keep_kernel(pos, left, right, vectors, received, sent, kept, vector_sums):
    block = left.shape[1] // 4
    core, y = pos[3], pos[2]
    tile = 256

    def step(i, _):
        rows = pl.ds(pl.multiple_of(i * tile, tile), tile)
        for turn, target in ((0, kept), (1, sent)):
            outer = 1 - y if turn else y
            at = pl.multiple_of((2 * outer + core) * block + i * tile, tile)
            there = pl.ds(pl.multiple_of(outer * block + i * tile, tile), tile)
            target[rows, :] = (
                dot_tn(left[:, pl.ds(at, tile)], right[...]) + received[there, :].astype(F32)
            ).astype(BF16)
        return 0

    lax.fori_loop(0, block // tile, step, 0)
    width = vectors.shape[1]
    got = received[2 * block : 2 * block + VECTOR_ROWS, :width].astype(F32)
    vector_sums[...] = vectors[...] + got[:8]
    put_vectors(sent, block, vector_sums[:1, :], vector_sums[1:2, :])


def copies_whole_kernel(pos, kept, low, high, whole, core_kept, core_rest, result):
    tile = 512
    rows = kept.shape[0]
    width = kept.shape[1] - result.shape[1]
    start = pos[3] * (width // 2)

    def step(i, _):
        at = pl.ds(pl.multiple_of(i * tile, tile), tile)
        mine = jnp.where(pos[3] == 0, low[:, at], high[:, at])
        other = jnp.where(pos[3] == 0, core_rest[:rows, at], core_rest[rows : 2 * rows, at])
        both = pl.ds(pl.multiple_of(start + i * tile, tile), tile)
        result[at, :] = (
            dot_tn(kept[:, both], kept[:, width:])
            + dot_tn(mine, whole[...])
            + dot_tn(core_kept[:, both], core_kept[:, width:])
            + dot_tn(other, core_rest[2 * rows :, :])
        )
        return 0

    lax.fori_loop(0, result.shape[0] // tile, step, 0)


def dense_grad_kernel(pos, returned, cotangent, pick, act, grad_dense, grad_low, sent):
    grad_dense[...] = cotangent[...].astype(F32) + dot_tn(pick[...], returned[...])
    grad_low[...] = grad_dense[...].astype(BF16)
    sum_send_kernel(pos, act, grad_low, sent)


def sum_send_kernel(pos, left, right, sent):
    half = right.shape[1] // 2
    lanes = pl.ds(pl.multiple_of((1 - pos[3]) * half, 128), half)
    tile = min(1024, left.shape[1] // 2)

    def step(i, _):
        rows = pl.ds(pl.multiple_of(i * tile, tile), tile)
        sent[rows, :] = dot_tn(left[:, rows], right[:, lanes]).astype(BF16)
        return 0

    lax.fori_loop(0, left.shape[1] // tile, step, 0)


def lay_out(pos, total, far, near, kept, sems, n_planes, vector=None):
    block = total.shape[0] // (4 * n_planes)
    for second in (1, 0):
        for step in range(n_planes):
            for first in (1, 0):
                row = row_start(pos, pos[3], second, first, step, n_planes, block)
                if first:
                    target, at, sem = (far if second else near), step, sems.at[1 + second]
                else:
                    target, at, sem = kept, second * n_planes + step, sems.at[0]
                pltpu.make_async_copy(
                    total.at[pl.ds(row, block), :], target.at[pl.ds(at * block, block), :], sem
                ).start()
    if vector is not None:
        pltpu.make_async_copy(
            vector, far.at[pl.ds(total.shape[0] // 4, VECTOR_ROWS), :], sems.at[2]
        ).start()
    for target, sem in ((kept, 0), (near, 1), (far, 2)):
        wait_whole(target, sems.at[sem])


def sum_keep_kernel(
    n_planes, pos, left, right, received, far, near, kept, total, sems, vector=None
):
    half = right.shape[1] // 2
    lanes = pl.ds(pl.multiple_of(pos[3] * half, 128), half)
    tile = min(1024, left.shape[1] // 2)

    def step(i, _):
        rows = pl.ds(pl.multiple_of(i * tile, tile), tile)
        total[rows, :] = (
            dot_tn(left[:, rows], right[:, lanes]) + received[rows, :].astype(F32)
        ).astype(BF16)
        return 0

    lax.fori_loop(0, left.shape[1] // tile, step, 0)
    lay_out(pos, total, far, near, kept, sems, n_planes, vector)


def pre_back_kernel(n_planes, split, pos, grad_low, slope, *refs):
    sides, (grad_pre, weight, sem) = take_sides(refs, split)
    load_weight(pos, sides, weight, sem, n_planes, True)
    rows = weight.shape[0] // n_planes
    chunk = min(512, rows)
    for step in range(n_planes):
        start = wait_step(pos, weight, sem, step, n_planes)
        for i in range(rows // chunk):
            at = pl.ds(pl.multiple_of(start + i * chunk, chunk), chunk)
            grad_pre[:, at] = (dot_nt(grad_low[...], weight[at, :]) * slope[:, at]).astype(BF16)


def hidden_back_kernel(n_planes, split, pos, grad_pre, hidden, grad_dense, gains, *refs):
    sides, (ffn_in, heads, grad_hidden, grad_low, grad_gain, send, weight, sem) = take_sides(refs, split)
    load_weight(pos, sides, weight, sem, n_planes, False)
    norm, inverse = normed(hidden[...])
    half = weight.shape[1] // 2
    grad_in = 0.0
    for side in range(2):
        core = pos[3] if side == 0 else 1 - pos[3]
        wait_half(weight, core, sem)
        lanes = pl.ds(pl.multiple_of(core * half, 128), half)
        grad_in = grad_in + dot_nt(grad_pre[:, lanes], weight[:, lanes])
    grad_gain[...] = jnp.zeros_like(grad_gain)
    grad_gain[0:1, :] = jnp.sum(grad_in * norm, axis=0, keepdims=True)
    grad_hidden[...] = grad_dense[...] + norm_back(grad_in * gains[1:2, :], norm, inverse)
    grad_low[...] = grad_hidden[...].astype(BF16)
    wide_columns(1 - pos[3], ffn_in, heads, grad_pre, grad_low, send, None)


def attend_back_kernel(n_planes, split, pos, grad_low, qkv, tokens, grad_hidden, gains, *refs):
    sides, refs = take_sides(refs, split)
    grad_qkv, grad_tokens, grad_gain, grad_heads, weight, sem = refs
    length, width = tokens.shape
    head_size = width // HEADS
    load_weight(pos, sides, weight, sem, n_planes, False)
    inputs = tokens[...].astype(F32)
    norm, inverse = normed(inputs)
    causal = causal_mask(length)
    lane = lax.broadcasted_iota(jnp.int32, (1, 2 * head_size), 1)
    wait_half(weight, 1, sem)
    grad_heads[...] = dot_nt(grad_low[...], weight[:, 3 * width : 4 * width]).astype(BF16)
    factor = head_size**-0.5

    def pair(i, _):
        at = pl.multiple_of(i * 2 * head_size, 2 * head_size)
        query = qkv[:, pl.ds(at, 2 * head_size)]
        key_rows = qkv[:, pl.ds(width + at, 2 * head_size)]
        value_rows = qkv[:, pl.ds(2 * width + at, 2 * head_size)]
        grad_out = grad_heads[:, pl.ds(at, 2 * head_size)]
        sums = [0.0, 0.0, 0.0]
        for head in range(2):
            own = (lane // head_size) == head
            masked = lambda v: jnp.where(own, v, 0).astype(BF16)
            own_query, own_grad = masked(query), masked(grad_out)
            scores = dot_nt(own_query, key_rows) * factor
            scores = jnp.where(causal, scores, -1e30)
            shifted = jnp.exp(scores - jnp.max(scores, axis=-1, keepdims=True))
            probs = shifted / jnp.sum(shifted, axis=-1, keepdims=True)
            grad_probs = dot_nt(own_grad, value_rows)
            row_terms = jnp.sum(probs * grad_probs, axis=-1, keepdims=True)
            grad_scores = (probs * (grad_probs - row_terms)).astype(BF16)
            sums[0] = sums[0] + dot_nn(grad_scores, masked(key_rows)) * factor
            sums[1] = sums[1] + dot_tn(grad_scores, own_query) * factor
            sums[2] = sums[2] + dot_tn(probs.astype(BF16), own_grad)
        for part in range(3):
            grad_qkv[:, pl.ds(part * width + at, 2 * head_size)] = sums[part].astype(BF16)
        return 0

    lax.fori_loop(0, HEADS // 2, pair, 0)
    wait_half(weight, 0, sem)
    grad_in = dot_nt(grad_qkv[...], weight[:, : 3 * width])
    grad_gain[...] = jnp.zeros_like(grad_gain)
    grad_gain[0:1, :] = jnp.sum(grad_in * norm, axis=0, keepdims=True)
    grad_tokens[...] = grad_hidden[...] + norm_back(grad_in * gains[0:1, :], norm, inverse)


def wide_columns(half, ffn_in, heads, grad_pre, grad_low, target, received):
    width = ffn_in.shape[1]
    columns = target.shape[1]
    rest = grad_pre.shape[1] - columns
    tile = 512

    def fill(lanes, left, right):
        def step(i, _):
            rows = pl.ds(pl.multiple_of(i * tile, tile), tile)
            value = dot_tn(left[:, rows], right())
            if received is not None:
                value = value + received[rows, lanes].astype(F32)
            target[rows, lanes] = value.astype(BF16)
            return 0

        lax.fori_loop(0, width // tile, step, 0)

    @pl.when(half == 0)
    def _():
        fill(slice(0, columns), ffn_in, lambda: grad_pre[:, :columns])

    @pl.when(half == 1)
    def _():
        fill(slice(0, rest), ffn_in, lambda: grad_pre[:, columns:])
        fill(slice(rest, columns), heads, lambda: grad_low[...])


def wide_keep_kernel(
    n_planes,
    pos,
    ffn_in,
    heads,
    grad_pre,
    grad_low,
    received,
    attn_in,
    grad_qkv,
    gain_one,
    gain_two,
    far,
    near,
    kept,
    send,
    total,
    sems,
):
    wide_columns(pos[3], ffn_in, heads, grad_pre, grad_low, total, received)
    lay_out(pos, total, far, near, kept, sems, n_planes)
    last_send_kernel(pos, attn_in, grad_qkv, gain_one, gain_two, send)


def last_send_kernel(pos, left, right, gain_one, gain_two, sent):
    put_vectors(sent, left.shape[1], gain_one[:1, :], gain_two[:1, :])
    sum_send_kernel(pos, left, right, sent)


def last_keep_kernel(
    n_planes,
    pos,
    left,
    right,
    gain_one,
    gain_two,
    received,
    far,
    near,
    kept,
    vector,
    total,
    vector_low,
    sems,
):
    at = received.shape[0] - VECTOR_ROWS
    width = gain_one.shape[1]
    vector[...] = jnp.zeros_like(vector)
    vector_low[...] = jnp.zeros_like(vector_low)
    for i, gain in enumerate((gain_one, gain_two)):
        row = slice(at, at + VECTOR_ROWS)
        summed = gain[:1, :] + received[row, :width].astype(F32)[i : i + 1]
        vector[i : i + 1, :width] = summed
    vector_low[:8, :] = vector[...].astype(BF16)
    sum_keep_kernel(
        n_planes, pos, left, right, received, far, near, kept, total, sems, vector_low
    )


def own_columns(values, core):
    half = values.shape[1] // 2
    mine = lax.dynamic_slice_in_dim(values, core * half, half, 1)
    other = lax.dynamic_slice_in_dim(values, (1 - core) * half, half, 1)
    got = swap_core(other)
    return jnp.where(
        core == 0, jnp.concatenate([mine, got], axis=0), jnp.concatenate([got, mine], axis=0)
    )


def exchange_rows(total, vector, swap):
    half = total.shape[0] // 2
    send = total[half:].astype(BF16)
    if vector is not None:
        send = jnp.concatenate(
            [send, jnp.pad(vector, ((0, VECTOR_ROWS - vector.shape[0]), (0, 0))).astype(BF16)], axis=0
        )
    got = swap(send).astype(F32)
    if vector is not None:
        vector = vector + got[half : half + vector.shape[0]]
    return total[:half] + got[:half], vector


def start_sum(got, kept):
    return kept.astype(F32) + got[: kept.shape[0]].astype(F32)


def second_sum(got_far, got_near, kept, vector=None, gate=()):
    half = kept.shape[0] // 2
    send = (kept[half:].astype(F32) + got_far[:half].astype(F32)).astype(BF16)
    if vector is not None:
        vector = vector + got_far[half : half + vector.shape[0]].astype(F32)
        low = jnp.pad(vector, ((0, VECTOR_ROWS - vector.shape[0]), (0, 0))).astype(BF16)
        send = jnp.concatenate([send, low], axis=0)
    got = swap_first(after(send, *gate) if gate else send).astype(F32)
    if vector is not None:
        vector = vector + got[half : half + vector.shape[0]]
    return kept[:half].astype(F32) + got_near.astype(F32) + got[:half], vector, (send,)


def whole_rows(total, core):
    shard = total.shape[0] // 2
    mine = lax.dynamic_slice_in_dim(total, core * shard, shard, 0)
    other = lax.dynamic_slice_in_dim(total, (1 - core) * shard, shard, 0)
    got = swap_core(other.astype(BF16)).astype(F32)
    return jnp.where(
        core == 0, jnp.concatenate([mine, got], axis=1), jnp.concatenate([got, mine], axis=1)
    )


def on_device(
    tokens,
    route,
    w_qkv,
    w_attn_out,
    w_up,
    w_down,
    gain_attn,
    gain_ffn,
    expert_in,
    expert_out,
    centroids,
    expert_gain,
    cotangent,
):
    length, features = tokens.shape
    n_expert = lax.axis_size("expert")
    n_replica = lax.axis_size("replica")
    n_dev = n_expert * n_replica
    n_planes = n_dev // 8
    per_dest = length // n_expert
    hidden_size = w_up.shape[1]
    replica = lax.axis_index("replica")
    me = lax.axis_index("expert") * n_replica + replica
    core = me % 2
    pos = jnp.stack([me // 8, (me // 4) % 2, (me // 2) % 2, core]).astype(jnp.int32)
    route_pick = (route[0][:, None] == lax.iota(jnp.int32, length)[None]).astype(BF16)

    def to_expert(picked):
        return lax.all_to_all(
            picked.reshape(n_expert, per_dest, features),
            "expert",
            split_axis=0,
            concat_axis=0,
            tiled=True,
        ).reshape(length, features)

    padded_gains = jnp.pad(jnp.stack([gain_attn, gain_ffn], axis=1), ((0, 0), (0, 254)))
    first = jnp.concatenate([w_qkv, w_attn_out, padded_gains], axis=1)
    owned = [own_columns(v, core) for v in (first, w_up, w_down)]
    join = lambda *v: jnp.concatenate(v, axis=0)
    far_bit = n_planes // 2

    def near_planes(own, *earlier):
        stack = after(own, *earlier) if earlier else own
        bit = 1
        while bit < far_bit:
            stack = join(stack, swap_plane(stack, bit))
            bit *= 2
        return stack

    own_a, own_b, own_c = owned
    near_a = near_planes(own_a)
    gate = (near_a,)
    far_a = swap_plane(near_a, far_bit)
    near_one_a = swap_first(near_a)
    near_b, near_c = near_planes(own_b, *gate), near_planes(own_c, *gate)
    gate = (far_a, near_one_a, near_b, near_c)
    far_b = swap_plane(after(near_b, *gate), far_bit)
    near_two_a = swap_second(after(join(near_a, near_one_a), *gate))
    one_a = swap_first(after(far_a, *gate))
    near_one_b = swap_first(after(near_b, *gate))
    gate = (far_b, near_two_a, one_a, near_one_b)
    far_c = swap_plane(after(near_c, *gate), far_bit)
    two_a = swap_second(after(join(far_a, one_a), *gate))
    near_two_b = swap_second(after(join(near_b, near_one_b), *gate))
    one_b = swap_first(after(far_b, *gate))
    core_near_a = swap_core(after(join(near_a, near_one_a, near_two_a), *gate))
    gate = (far_c, two_a, near_two_b, one_b, core_near_a)
    two_b = swap_second(after(join(far_b, one_b), *gate))
    near_one_c = swap_first(after(near_c, *gate))
    one_c = swap_first(after(far_c, *gate))
    core_far_a = swap_core(after(join(far_a, one_a, two_a), *gate))
    core_near_b = swap_core(after(join(near_b, near_one_b, near_two_b), *gate))
    first_pieces = [near_a, near_one_a, near_two_a, far_a, one_a, two_a, core_near_a, core_far_a]
    gate = (two_b, near_one_c, one_c, core_far_a, core_near_b)
    near_two_c = swap_second(after(join(near_c, near_one_c), *gate))
    two_c = swap_second(after(join(far_c, one_c), *gate))
    core_far_b = swap_core(after(join(far_b, one_b, two_b), *gate))
    up_pieces = [near_b, near_one_b, near_two_b, far_b, one_b, two_b, core_near_b, core_far_b]
    grad_delta = to_expert(jnp.dot(route_pick, cotangent, preferred_element_type=F32).astype(BF16))

    wide = first.shape[1]
    planes = functools.partial
    weight_first = pltpu.VMEM((features, wide), BF16)
    weight_up = pltpu.VMEM((features, hidden_size), BF16)
    weight_down = pltpu.VMEM((hidden_size, features), BF16)
    two_sems, three_sems, plane_sems = (pltpu.SemaphoreType.DMA((n,)) for n in (2, 3, n_planes))
    unit = 2 * length * features * features

    hidden, ffn_in, attn_in, qkv, heads, gains = run_kernel(
        planes(attend_kernel, n_planes, (6, 2)),
        [after(pos, grad_delta), tokens, *first_pieces],
        "sv" + "h" * 8,
        [
            shaped(length, features, dtype=F32),
            shaped(length, features),
            shaped(length, features),
            shaped(length, 3 * features),
            shaped(length, features),
            shaped(8, features, dtype=F32),
        ],
        [weight_first, two_sems],
        flops=5 * unit,
    )
    gate = (near_two_c, two_c, core_far_b, hidden)
    core_near_c = swap_core(after(join(near_c, near_one_c, near_two_c), *gate))
    core_far_c = swap_core(after(join(far_c, one_c, two_c), *gate))
    act, slope = run_kernel(
        planes(up_kernel, n_planes, (6, 2)),
        [pos, ffn_in, *up_pieces],
        "sv" + "h" * 8,
        [shaped(length, hidden_size), shaped(length, hidden_size, dtype=F32)],
        [weight_up, two_sems],
        flops=4 * unit,
    )
    down_pieces = [near_c, near_one_c, near_two_c, far_c, one_c, two_c, core_near_c, core_far_c]
    dense_out, sent = run_kernel(
        planes(down_kernel, n_planes, (6, 2)),
        [pos, act, hidden, route_pick, *down_pieces],
        "svvv" + "h" * 8,
        [shaped(length, features, dtype=F32), shaped(length, features)],
        [weight_down, plane_sems],
        flops=4 * unit,
    )
    arrived = to_expert(after(sent, grad_delta))
    inner = expert_in.shape[2]
    (
        delta,
        grad_rows,
        expert_norm,
        pair,
        sent_low,
        sent_high,
        whole_low,
        expert_grad_pre,
        vectors,
    ) = run_kernel(
        expert_kernel,
        [pos, arrived, grad_delta, centroids, expert_gain, expert_in, expert_out],
        "svvvvhh",
        [
            shaped(length, features),
            shaped(length, features),
            shaped(length, features),
            shaped(length, inner // 2 + features),
            shaped(length, inner // 4),
            shaped(length, inner // 4),
            shaped(length, features),
            shaped(length, inner),
            shaped(8, features, dtype=F32),
        ],
        [
            pltpu.VMEM((features, inner), BF16),
            pltpu.VMEM((inner, features), BF16),
            pltpu.VMEM((length, inner), BF16),
            pltpu.VMEM((length, inner), F32),
            pltpu.SemaphoreType.DMA((2, inner // 512)),
        ],
        flops=16 * unit,
    )
    returned = to_expert(grad_rows)
    got_low = swap_y(sent_low)
    got_high = swap_y(after(sent_high, got_low))
    got_whole = swap_y(after(whole_low, got_high))

    (send_in,) = run_kernel(
        copies_send_kernel,
        [pos, expert_norm, expert_grad_pre, vectors],
        "svvv",
        [shaped(features // 2 + VECTOR_ROWS, inner)],
        flops=2 * unit,
    )
    got_in = swap_core(send_in)

    grad_dense, grad_dense_low, send_down = run_kernel(
        dense_grad_kernel,
        [after(pos, send_in, got_low), returned, cotangent, route_pick, act],
        "svvvv",
        [
            shaped(length, features, dtype=F32),
            shaped(length, features),
            shaped(hidden_size, features // 2),
        ],
        flops=4 * unit,
    )
    got_down = swap_core(send_down)
    (grad_pre,) = run_kernel(
        planes(pre_back_kernel, n_planes, (6, 2)),
        [after(pos, send_down, got_in, got_high), grad_dense_low, slope, *down_pieces],
        "svv" + "h" * 8,
        [shaped(length, hidden_size)],
        [weight_down, plane_sems],
        flops=4 * unit,
    )
    core_kept = swap_core(pair)
    far_down, near_down, kept_down = run_kernel(
        planes(sum_keep_kernel, n_planes),
        [after(pos, grad_pre, got_whole, core_kept), act, grad_dense_low, got_down],
        "svvv",
        [shaped(hidden_size // 4, features // 2)] * 2 + [shaped(hidden_size // 2, features // 2)],
        [pltpu.VMEM((hidden_size, features // 2), BF16), three_sems],
        flops=4 * unit,
        out_spaces="hhh",
    )
    got_far_down, got_near_down = swap_second(far_down), swap_second(near_down)
    send_in, kept_in, vectors = run_kernel(
        copies_keep_kernel,
        [after(pos, kept_down), expert_norm, expert_grad_pre, vectors, got_in],
        "svvvv",
        [
            shaped(features // 4 + VECTOR_ROWS, inner),
            shaped(features // 4, inner),
            shaped(8, features, dtype=F32),
        ],
        flops=2 * unit,
    )
    core_rest = swap_core(join(got_low, got_high, got_whole))
    wide_half = (hidden_size + features) // 2
    grad_hidden, grad_hidden_low, grad_gain_two, send_up = run_kernel(
        planes(hidden_back_kernel, n_planes, (6, 2)),
        [
            after(pos, send_in),
            grad_pre,
            hidden,
            grad_dense,
            gains,
            *up_pieces,
            ffn_in,
            heads,
        ],
        "svvvv" + "h" * 8 + "vv",
        [
            shaped(length, features, dtype=F32),
            shaped(length, features),
            shaped(8, features, dtype=F32),
            shaped(features, wide_half),
        ],
        [weight_up, two_sems],
        flops=7 * unit,
    )
    got_up = swap_core(send_up)
    grad_qkv, grad_tokens, grad_gain_one = run_kernel(
        planes(attend_back_kernel, n_planes, (6, 2)),
        [
            after(pos, got_far_down, got_near_down, send_up, core_rest),
            grad_hidden_low,
            qkv,
            tokens,
            grad_hidden,
            gains,
            *first_pieces,
        ],
        "svvvvv" + "h" * 8,
        [
            shaped(length, 3 * features),
            shaped(length, features, dtype=F32),
            shaped(8, features, dtype=F32),
        ],
        [pltpu.VMEM((length, features), BF16), weight_first, two_sems],
        flops=8 * unit,
    )
    in_low = swap_y(after(send_in[: features // 16], grad_qkv))
    down_2 = second_sum(got_far_down, got_near_down, kept_down)
    last_half = 3 * features // 2
    far_up, near_up, kept_up, send_last = run_kernel(
        planes(wide_keep_kernel, n_planes),
        [
            after(pos, grad_qkv, down_2[0]),
            ffn_in,
            heads,
            grad_pre,
            grad_hidden_low,
            got_up,
            attn_in,
            grad_qkv,
            grad_gain_one,
            grad_gain_two,
        ],
        "s" + "v" * 9,
        [shaped(features // 4, wide_half)] * 2
        + [shaped(features // 2, wide_half), shaped(features + VECTOR_ROWS, last_half)],
        [pltpu.VMEM((features, wide_half), BF16), three_sems],
        flops=5 * unit,
        out_spaces="hhhv",
    )
    swaps = [
        functools.partial(swap_plane, bit=bit)
        for bit in (1 << i for i in reversed(range(n_planes.bit_length() - 1)))
    ]
    got_far_up = swap_second(far_up)
    down_3, _ = exchange_rows(after(down_2[0], kept_up), None, swaps[0])
    got_near_up = swap_second(after(near_up, got_far_up))
    got_last = swap_core(send_last)
    delta_home = to_expert(after(delta, send_last))
    (sum_expert_out,) = run_kernel(
        copies_whole_kernel,
        [
            after(pos, send_last, delta_home, in_low),
            pair,
            got_low,
            got_high,
            got_whole,
            core_kept,
            core_rest,
        ],
        "s" + "v" * 6,
        [shaped(inner // n_replica, features, dtype=F32)],
        flops=4 * unit,
    )
    far, near, kept, vector = run_kernel(
        planes(last_keep_kernel, n_planes),
        [
            after(pos, sum_expert_out, got_far_up, down_3),
            attn_in,
            grad_qkv,
            grad_gain_one,
            grad_gain_two,
            got_last,
        ],
        "s" + "v" * 5,
        [
            shaped(features // 4 + VECTOR_ROWS, last_half),
            shaped(features // 4, last_half),
            shaped(features // 2, last_half),
            shaped(8, last_half, dtype=F32),
        ],
        [
            pltpu.VMEM((features, last_half), BF16),
            pltpu.VMEM((VECTOR_ROWS, last_half), BF16),
            three_sems,
        ],
        flops=2 * unit,
        out_spaces="hhhv",
    )
    up_2 = second_sum(got_far_up, got_near_up, kept_up, gate=(kept,))
    last_2 = second_sum(swap_second(far), swap_second(near), kept, vector)
    in_high = swap_y(after(send_in[features // 16 :], up_2[0]))
    sums = []
    for total, vector, left in (
        (after(down_3, up_2[0]), None, swaps[1:]),
        (*up_2[:2], swaps),
        (*last_2[:2], swaps),
    ):
        for swap in left:
            total, vector = exchange_rows(total, vector, swap)
        sums.append(whole_rows(total, core))
    sum_down, sum_up, sum_last = sums
    mixed = (
        dense_out
        + lax.dot_general(
            route_pick, delta_home, (((0,), (0,)), ((), ())), preferred_element_type=F32
        )
    ).astype(BF16)
    part = features // n_replica
    sum_expert_in = kept_in.astype(F32) + join(in_low, in_high[: 3 * features // 16]).astype(F32)
    vectors = vectors[:2] + in_high[3 * features // 16 : 3 * features // 16 + 2, :features].astype(F32)
    vectors = lax.dynamic_slice_in_dim(vectors, replica * part, part, 1)
    shard = features // n_dev
    gain_grads = lax.dynamic_slice_in_dim(vector[:2, :features], me * shard, shard, 1)
    return (
        mixed,
        grad_tokens,
        sum_last,
        sum_up[:, hidden_size:],
        sum_up[:, :hidden_size],
        sum_down,
        gain_grads[0],
        gain_grads[1],
        sum_expert_in[None],
        sum_expert_out[None],
        vectors[:1],
        vectors[1:],
    )


def solution(mesh):
    placed = (
        P(("expert", "replica"), None),
        P(("expert", "replica"), None),
        P(("expert", "replica"), None),
        P(("expert", "replica"), None),
        P(("expert", "replica"), None),
        P(("expert", "replica"), None),
        P(("expert", "replica")),
        P(("expert", "replica")),
        P("expert", None, None),
        P("expert", None, None),
        P("expert", None),
        P("expert", None),
        P(("expert", "replica"), None),
    )
    return jax.shard_map(
        on_device,
        mesh=mesh,
        in_specs=placed,
        out_specs=(
            P(("expert", "replica"), None),
            P(("expert", "replica"), None),
            P(("expert", "replica"), None),
            P(("expert", "replica"), None),
            P(("expert", "replica"), None),
            P(("expert", "replica"), None),
            P(("expert", "replica")),
            P(("expert", "replica")),
            P("expert", "replica", None),
            P("expert", "replica", None),
            P("expert", "replica"),
            P("expert", "replica"),
        ),
        check_vma=False,
    )
```

```python
import functools
import math

import jax
import jax.numpy as jnp
from jax import lax
from jax.experimental import pallas as pl
from jax.experimental.pallas import tpu as pltpu
from jax.sharding import PartitionSpec as P

HEADS = 16
EPSILON = 1e-05
ALL_AXES = ("expert", "replica")
VMEM_LIMIT = 58 * 2**20
GELU_SCALE = math.sqrt(2.0 / math.pi)
BF16, F32 = jnp.bfloat16, jnp.float32


def permuted(values, target):
    n_dev = lax.axis_size("expert") * lax.axis_size("replica")
    return lax.ppermute(values, ALL_AXES, [(d, target(d, n_dev)) for d in range(n_dev)])


def swap_core(values):
    return permuted(values, lambda d, n: d ^ 1)


def swap_first(values):
    return permuted(values, lambda d, n: d ^ (2 if d % 2 else 4))


def swap_second(values):
    return permuted(values, lambda d, n: d ^ (4 if d % 2 else 2))


def swap_x(values):
    return permuted(values, lambda d, n: d ^ 4)


def swap_y(values):
    return permuted(values, lambda d, n: d ^ 2)


def swap_plane(values, bit):
    return permuted(values, lambda d, n: d ^ (8 * bit))


def after(values, *earlier):
    return lax.optimization_barrier((values,) + earlier)[0]


HINT = 30


def body_name(body):
    return getattr(body, "func", body).__name__


def run_kernel(body, args, spaces, outs, scratch=(), flops=0, out_spaces=None):
    place = {
        "v": pl.BlockSpec(memory_space=pltpu.VMEM),
        "h": pl.BlockSpec(memory_space=pl.ANY),
        "s": pl.BlockSpec(memory_space=pltpu.SMEM),
    }
    moved = sum(a.size * a.dtype.itemsize for a in args)
    moved += sum(o.size * o.dtype.itemsize for o in outs)
    return pl.pallas_call(
        body,
        name=body_name(body),
        out_shape=list(outs),
        in_specs=[place[s] for s in spaces],
        out_specs=[place[s] for s in (out_spaces or "v" * len(outs))],
        scratch_shapes=list(scratch),
        cost_estimate=pl.CostEstimate(flops=int(flops * HINT), bytes_accessed=int(moved * HINT), transcendentals=0),
        compiler_params=pltpu.CompilerParams(vmem_limit_bytes=VMEM_LIMIT),
    )(*args)


def shaped(*shape, dtype=BF16):
    return jax.ShapeDtypeStruct(shape, dtype)


def dot_nn(left, right):
    return jnp.dot(left, right, preferred_element_type=F32)


def dot_nt(left, right):
    return lax.dot_general(left, right, (((1,), (1,)), ((), ())), preferred_element_type=F32)


def dot_tn(left, right):
    return lax.dot_general(left, right, (((0,), (0,)), ((), ())), preferred_element_type=F32)


def normed(values):
    centered = values - jnp.mean(values, axis=-1, keepdims=True)
    inverse = lax.rsqrt(jnp.mean(centered * centered, axis=-1, keepdims=True) + EPSILON)
    return centered * inverse, inverse


def norm_back(grad_normed, norm, inverse):
    return inverse * (
        grad_normed
        - jnp.mean(grad_normed, axis=-1, keepdims=True)
        - norm * jnp.mean(grad_normed * norm, axis=-1, keepdims=True)
    )


def gelu_both(values):
    square = values * values
    bent = jnp.tanh(GELU_SCALE * values * (1.0 + 0.044715 * square))
    half = 0.5 * (1.0 + bent)
    slope = half + 0.5 * values * (1.0 - bent * bent) * (
        GELU_SCALE * (1.0 + 3.0 * 0.044715 * square)
    )
    return values * half, slope


def row_start(pos, core, first, second, step, n_planes, block):
    x, y = pos[1], pos[2]
    flip = lambda v, on: 1 - v if on else v
    across = jnp.where(core == 0, flip(x, first), flip(x, second))
    along = jnp.where(core == 0, flip(y, second), flip(y, first))
    plane = pos[0] ^ step
    return pl.multiple_of(((plane * 2 + across) * 2 + along) * block, block)


PIECE_ORDER = ((0, 0), (1, 0), (0, 1), (1, 1))


def load_weight(pos, sides, target, sems, n_planes, by_plane):
    block = target.shape[0] // (4 * n_planes)
    part = n_planes // 2
    order = [(far, *chip) for far in range(2) for chip in PIECE_ORDER]
    copies = []
    for side, pieces in enumerate(sides):
        half = pieces[0].shape[1]
        core = pos[3] if side == 0 else 1 - pos[3]
        lanes = pl.ds(pl.multiple_of(core * half, 128), half)
        spots = [(piece, at) for piece in pieces for at in range(0, piece.shape[0], block * part)]
        for (far, first, second), (piece, at) in zip(order, spots, strict=True):
            for step in range(part):
                row = row_start(pos, core, first, second, far * part + step, n_planes, block)
                copies.append(
                    (
                        far * part + step if by_plane else side,
                        pltpu.make_async_copy(
                            piece.at[pl.ds(at + step * block, block), :],
                            target.at[pl.ds(row, block), lanes],
                            sems.at[far * part + step] if by_plane else sems.at[core],
                        ),
                    )
                )
    for _, copy in sorted(copies, key=lambda pair: pair[0]):
        copy.start()


def wait_half(target, core, sems):
    half = target.at[:, : target.shape[1] // 2]
    pltpu.make_async_copy(half, half, sems.at[core]).wait()


def wait_step(pos, target, sems, step, n_planes):
    rows = target.shape[0] // n_planes
    part = target.at[:rows, :]
    pltpu.make_async_copy(part, part, sems.at[step]).wait()
    return pl.multiple_of((pos[0] ^ step) * rows, rows)


def wait_whole(target, sem):
    pltpu.make_async_copy(target, target, sem).wait()


def causal_mask(length):
    return lax.broadcasted_iota(jnp.int32, (length, length), 0) >= lax.broadcasted_iota(
        jnp.int32, (length, length), 1
    )


def take_sides(refs, split):
    mine, both = split[0], sum(split)
    return (refs[:mine], refs[mine:both]), refs[both:]


def attend_kernel(n_planes, split, pos, tokens, *refs):
    sides, refs = take_sides(refs, split)
    hidden, ffn_in, attn_in, qkv, heads, gains, weight, sem = refs
    length, width = tokens.shape
    load_weight(pos, sides, weight, sem, n_planes, False)
    inputs = tokens[...].astype(F32)
    norm, _ = normed(inputs)
    wait_half(weight, 1, sem)
    columns = weight[:, 4 * width : 4 * width + 128].astype(F32)
    gains[...] = columns.T[:8]
    attn_in[...] = (norm * gains[0:1, :]).astype(BF16)
    wait_half(weight, 0, sem)
    for part in range(3):
        lanes = slice(part * width, (part + 1) * width)
        qkv[:, lanes] = dot_nn(attn_in[...], weight[:, lanes]).astype(BF16)
    head_size = width // HEADS
    causal = causal_mask(length)
    lane = lax.broadcasted_iota(jnp.int32, (1, 2 * head_size), 1)

    def pair(i, _):
        at = pl.multiple_of(i * 2 * head_size, 2 * head_size)
        query = qkv[:, pl.ds(at, 2 * head_size)] * (head_size**-0.5)
        key_rows = qkv[:, pl.ds(width + at, 2 * head_size)]
        value_rows = qkv[:, pl.ds(2 * width + at, 2 * head_size)]
        mixed = []
        for head in range(2):
            own = (lane // head_size) == head
            scores = dot_nt(jnp.where(own, query, 0).astype(BF16), key_rows)
            scores = jnp.where(causal, scores, -1e30)
            shifted = jnp.exp(scores - jnp.max(scores, axis=-1, keepdims=True))
            probs = shifted / jnp.sum(shifted, axis=-1, keepdims=True)
            mixed.append(dot_nn(probs.astype(BF16), value_rows))
        heads[:, pl.ds(at, 2 * head_size)] = jnp.where(lane < head_size, mixed[0], mixed[1]).astype(
            BF16
        )
        return 0

    lax.fori_loop(0, HEADS // 2, pair, 0, unroll=True)
    hidden[...] = inputs + dot_nn(heads[...], weight[:, 3 * width : 4 * width])
    norm_two, _ = normed(hidden[...])
    ffn_in[...] = (norm_two * gains[1:2, :]).astype(BF16)


def up_kernel(n_planes, split, pos, ffn_in, *refs):
    sides, (act, slope, weight, sem) = take_sides(refs, split)
    load_weight(pos, sides, weight, sem, n_planes, False)
    chunk = 512
    half = weight.shape[1] // 2
    for side in range(2):
        core = pos[3] if side == 0 else 1 - pos[3]
        wait_half(weight, core, sem)
        for i in range(half // chunk):
            lanes = pl.ds(pl.multiple_of(core * half + i * chunk, chunk), chunk)
            value, grad = gelu_both(dot_nn(ffn_in[...], weight[:, lanes]))
            act[:, lanes] = value.astype(BF16)
            slope[:, lanes] = grad


def down_kernel(n_planes, split, pos, act, hidden, pick, *refs):
    sides, (dense_out, sent, weight, sem) = take_sides(refs, split)
    load_weight(pos, sides, weight, sem, n_planes, True)
    rows = weight.shape[0] // n_planes
    total = hidden[...]
    for step in range(n_planes):
        at = pl.ds(wait_step(pos, weight, sem, step, n_planes), rows)
        total = total + dot_nn(act[:, at], weight[at, :])
    dense_out[...] = total
    sent[...] = dot_nn(pick[...], total.astype(BF16)).astype(BF16)


def expert_kernel(
    pos,
    arrived,
    grad_delta,
    centroid,
    norm_gain,
    weight_in,
    weight_out,
    delta,
    grad_rows,
    norm_low,
    kept,
    sent_low,
    sent_high,
    whole_low,
    grad_pre,
    vectors,
    w_in,
    w_out,
    act,
    slope,
    sems,
):
    chunk = 512
    n_chunks = w_in.shape[1] // chunk
    spans = [pl.ds(i * chunk, chunk) for i in range(n_chunks)]
    copies_in = [
        pltpu.make_async_copy(weight_in.at[0, :, span], w_in.at[:, span], sems.at[0, i])
        for i, span in enumerate(spans)
    ]
    copies_out = [
        pltpu.make_async_copy(weight_out.at[0, span, :], w_out.at[span, :], sems.at[1, i])
        for i, span in enumerate(spans)
    ]
    for copy in copies_in + copies_out:
        copy.start()
    rows = arrived[...].astype(F32)
    center = centroid[...].astype(F32)
    gain = norm_gain[...].astype(F32)
    gate = jax.nn.sigmoid(jnp.sum(rows * center, axis=-1, keepdims=True))
    norm, inverse = normed(rows)
    norm_low[...] = (norm * gain).astype(BF16)
    grad_out = grad_delta[...].astype(F32)
    grad_whole = gate * grad_out
    whole_low[...] = grad_whole.astype(BF16)
    for copy, span in zip(copies_in, spans):
        copy.wait()
        value, grad = gelu_both(dot_nn(norm_low[...], w_in[:, span]))
        act[:, span] = value.astype(BF16)
        slope[:, span] = grad
    half = act.shape[1] // 2
    kept[:, :half] = act[:, pl.ds(pl.multiple_of(pos[2] * half, 128), half)]
    other = pl.multiple_of((1 - pos[2]) * half, 128)
    sent_low[...] = act[:, pl.ds(other, half // 2)]
    sent_high[...] = act[:, pl.ds(pl.multiple_of(other + half // 2, 128), half // 2)]
    kept[:, half:] = whole_low[...]
    for copy in copies_out:
        copy.wait()
    whole = rows + dot_nn(act[...], w_out[...])
    delta[...] = (gate * whole).astype(BF16)
    grad_gate = jnp.sum(grad_out * whole, axis=-1, keepdims=True)
    grad_logit = grad_gate * gate * (1.0 - gate)

    for span in spans:
        grad_act = dot_nt(whole_low[...], w_out[span, :])
        grad_pre[:, span] = (grad_act * slope[:, span]).astype(BF16)
    grad_norm = dot_nt(grad_pre[...], w_in[...])
    vectors[...] = jnp.zeros_like(vectors)
    vectors[0:1, :] = jnp.sum(grad_logit * rows, axis=0, keepdims=True)
    vectors[1:2, :] = jnp.sum(grad_norm * norm, axis=0, keepdims=True)
    back = norm_back(grad_norm * gain, norm, inverse)
    grad_rows[...] = (grad_whole + grad_logit * center + back).astype(BF16)


VECTOR_ROWS = 16


def put_vectors(target, at, one, two):
    width = one.shape[1]
    row = lax.broadcasted_iota(jnp.int32, (VECTOR_ROWS, width), 0)
    both = jnp.where(row == 0, one, jnp.where(row == 1, two, 0.0))
    target[at : at + VECTOR_ROWS, :] = jnp.zeros((VECTOR_ROWS, target.shape[1]), BF16)
    target[at : at + VECTOR_ROWS, :width] = both.astype(BF16)


def copies_send_kernel(pos, left, right, vectors, sent):
    block = left.shape[1] // 4
    other = 1 - pos[3]
    tile = 256

    def step(i, _):
        outer, inner = lax.div(i, block // tile), lax.rem(i, block // tile)
        at = pl.multiple_of((2 * outer + other) * block + inner * tile, tile)
        sent[pl.ds(pl.multiple_of(i * tile, tile), tile), :] = dot_tn(
            left[:, pl.ds(at, tile)], right[...]
        ).astype(BF16)
        return 0

    lax.fori_loop(0, 2 * block // tile, step, 0)
    put_vectors(sent, 2 * block, vectors[:1, :], vectors[1:2, :])


def copies_keep_kernel(
    pos, left, right, vectors, received, sent_first, sent, kept, vector_sums
):
    block = left.shape[1] // 4
    core, y = pos[3], pos[2]
    early = sent_first.shape[0]
    for turn in range(2):
        outer = 1 - y if turn else y
        at = pl.ds(pl.multiple_of((2 * outer + core) * block, 128), block)
        there = pl.ds(pl.multiple_of(outer * block, 16), block)
        value = dot_tn(left[:, at], right[...]) + received[there, :].astype(F32)
        if turn:
            sent_first[...] = value[:early].astype(BF16)
            sent[: block - early, :] = value[early:].astype(BF16)
        else:
            kept[...] = value.astype(BF16)
    width = vectors.shape[1]
    got = received[2 * block : 2 * block + VECTOR_ROWS, :width].astype(F32)
    vector_sums[...] = vectors[...] + got[:8]
    put_vectors(sent, block - early, vector_sums[:1, :], vector_sums[1:2, :])


def copies_whole_kernel(pos, kept, low, high, whole, core_kept, core_rest, result):
    tile = 512
    rows = kept.shape[0]
    width = kept.shape[1] - result.shape[1]
    start = pos[3] * (width // 2)

    def step(i, _):
        at = pl.ds(pl.multiple_of(i * tile, tile), tile)
        mine = jnp.where(pos[3] == 0, low[:, at], high[:, at])
        other = jnp.where(pos[3] == 0, core_rest[:rows, at], core_rest[rows : 2 * rows, at])
        both = pl.ds(pl.multiple_of(start + i * tile, tile), tile)
        result[at, :] = (
            dot_tn(kept[:, both], kept[:, width:])
            + dot_tn(mine, whole[...])
            + dot_tn(core_kept[:, both], core_kept[:, width:])
            + dot_tn(other, core_rest[2 * rows :, :])
        )
        return 0

    lax.fori_loop(0, result.shape[0] // tile, step, 0)


def dense_grad_kernel(pos, returned, cotangent, pick, act, grad_dense, grad_low, sent):
    grad_dense[...] = cotangent[...].astype(F32) + dot_tn(pick[...], returned[...])
    grad_low[...] = grad_dense[...].astype(BF16)
    sum_send_kernel(pos, act, grad_low, sent)


def sum_send_kernel(pos, left, right, sent):
    half = right.shape[1] // 2
    lanes = pl.ds(pl.multiple_of((1 - pos[3]) * half, 128), half)
    tile = min(1024, left.shape[1] // 2)

    def step(i, _):
        rows = pl.ds(pl.multiple_of(i * tile, tile), tile)
        sent[rows, :] = dot_tn(left[:, rows], right[:, lanes]).astype(BF16)
        return 0

    lax.fori_loop(0, left.shape[1] // tile, step, 0)


def lay_out(pos, total, far, near, kept, sems, n_planes, vector=None):
    block = total.shape[0] // (4 * n_planes)
    for second in (1, 0):
        for step in range(n_planes):
            for first in (1, 0):
                row = row_start(pos, pos[3], second, first, step, n_planes, block)
                if first:
                    target, at, sem = (far if second else near), step, sems.at[1 + second]
                else:
                    target, at, sem = kept, second * n_planes + step, sems.at[0]
                pltpu.make_async_copy(
                    total.at[pl.ds(row, block), :], target.at[pl.ds(at * block, block), :], sem
                ).start()
    if vector is not None:
        pltpu.make_async_copy(
            vector, far.at[pl.ds(total.shape[0] // 4, VECTOR_ROWS), :], sems.at[2]
        ).start()
    for target, sem in ((kept, 0), (near, 1), (far, 2)):
        wait_whole(target, sems.at[sem])


def sum_keep_kernel(
    n_planes, pos, left, right, received, far, near, kept, total, sems, vector=None
):
    half = right.shape[1] // 2
    lanes = pl.ds(pl.multiple_of(pos[3] * half, 128), half)
    tile = min(1024, left.shape[1] // 2)

    def step(i, _):
        rows = pl.ds(pl.multiple_of(i * tile, tile), tile)
        total[rows, :] = (
            dot_tn(left[:, rows], right[:, lanes]) + received[rows, :].astype(F32)
        ).astype(BF16)
        return 0

    lax.fori_loop(0, left.shape[1] // tile, step, 0)
    lay_out(pos, total, far, near, kept, sems, n_planes, vector)


def pre_back_kernel(n_planes, split, pos, grad_low, slope, *refs):
    sides, (grad_pre, weight, sem) = take_sides(refs, split)
    load_weight(pos, sides, weight, sem, n_planes, True)
    rows = weight.shape[0] // n_planes
    chunk = min(512, rows)
    for step in range(n_planes):
        start = wait_step(pos, weight, sem, step, n_planes)
        for i in range(rows // chunk):
            at = pl.ds(pl.multiple_of(start + i * chunk, chunk), chunk)
            grad_pre[:, at] = (dot_nt(grad_low[...], weight[at, :]) * slope[:, at]).astype(BF16)


def hidden_back_kernel(n_planes, split, pos, grad_pre, hidden, grad_dense, gains, *refs):
    sides, (ffn_in, heads, grad_hidden, grad_low, grad_gain, send, weight, sem) = take_sides(refs, split)
    load_weight(pos, sides, weight, sem, n_planes, False)
    norm, inverse = normed(hidden[...])
    half = weight.shape[1] // 2
    grad_in = 0.0
    for side in range(2):
        core = pos[3] if side == 0 else 1 - pos[3]
        wait_half(weight, core, sem)
        lanes = pl.ds(pl.multiple_of(core * half, 128), half)
        grad_in = grad_in + dot_nt(grad_pre[:, lanes], weight[:, lanes])
    grad_gain[...] = jnp.zeros_like(grad_gain)
    grad_gain[0:1, :] = jnp.sum(grad_in * norm, axis=0, keepdims=True)
    grad_hidden[...] = grad_dense[...] + norm_back(grad_in * gains[1:2, :], norm, inverse)
    grad_low[...] = grad_hidden[...].astype(BF16)
    wide_columns(1 - pos[3], ffn_in, heads, grad_pre, grad_low, send, None)


def attend_back_kernel(n_planes, split, pos, grad_low, qkv, tokens, grad_hidden, gains, *refs):
    sides, refs = take_sides(refs, split)
    grad_qkv, grad_tokens, grad_gain, grad_heads, weight, sem = refs
    length, width = tokens.shape
    head_size = width // HEADS
    load_weight(pos, sides, weight, sem, n_planes, False)
    inputs = tokens[...].astype(F32)
    norm, inverse = normed(inputs)
    causal = causal_mask(length)
    lane = lax.broadcasted_iota(jnp.int32, (1, 2 * head_size), 1)
    wait_half(weight, 1, sem)
    grad_heads[...] = dot_nt(grad_low[...], weight[:, 3 * width : 4 * width]).astype(BF16)
    factor = head_size**-0.5

    def pair(i, _):
        at = pl.multiple_of(i * 2 * head_size, 2 * head_size)
        query = qkv[:, pl.ds(at, 2 * head_size)]
        key_rows = qkv[:, pl.ds(width + at, 2 * head_size)]
        value_rows = qkv[:, pl.ds(2 * width + at, 2 * head_size)]
        grad_out = grad_heads[:, pl.ds(at, 2 * head_size)]
        sums = [0.0, 0.0, 0.0]
        for head in range(2):
            own = (lane // head_size) == head
            masked = lambda v: jnp.where(own, v, 0).astype(BF16)
            own_query, own_grad = masked(query), masked(grad_out)
            scores = dot_nt(own_query, key_rows) * factor
            scores = jnp.where(causal, scores, -1e30)
            shifted = jnp.exp(scores - jnp.max(scores, axis=-1, keepdims=True))
            probs = shifted / jnp.sum(shifted, axis=-1, keepdims=True)
            grad_probs = dot_nt(own_grad, value_rows)
            row_terms = jnp.sum(probs * grad_probs, axis=-1, keepdims=True)
            grad_scores = (probs * (grad_probs - row_terms)).astype(BF16)
            sums[0] = sums[0] + dot_nn(grad_scores, masked(key_rows)) * factor
            sums[1] = sums[1] + dot_tn(grad_scores, own_query) * factor
            sums[2] = sums[2] + dot_tn(probs.astype(BF16), own_grad)
        for part in range(3):
            grad_qkv[:, pl.ds(part * width + at, 2 * head_size)] = sums[part].astype(BF16)
        return 0

    lax.fori_loop(0, HEADS // 2, pair, 0, unroll=True)
    wait_half(weight, 0, sem)
    grad_in = dot_nt(grad_qkv[...], weight[:, : 3 * width])
    grad_gain[...] = jnp.zeros_like(grad_gain)
    grad_gain[0:1, :] = jnp.sum(grad_in * norm, axis=0, keepdims=True)
    grad_tokens[...] = grad_hidden[...] + norm_back(grad_in * gains[0:1, :], norm, inverse)


def wide_columns(half, ffn_in, heads, grad_pre, grad_low, target, received):
    width = ffn_in.shape[1]
    columns = target.shape[1]
    rest = grad_pre.shape[1] - columns
    tile = 512

    def fill(lanes, left, right):
        def step(i, _):
            rows = pl.ds(pl.multiple_of(i * tile, tile), tile)
            value = dot_tn(left[:, rows], right())
            if received is not None:
                value = value + received[rows, lanes].astype(F32)
            target[rows, lanes] = value.astype(BF16)
            return 0

        lax.fori_loop(0, width // tile, step, 0)

    @pl.when(half == 0)
    def _():
        fill(slice(0, columns), ffn_in, lambda: grad_pre[:, :columns])

    @pl.when(half == 1)
    def _():
        fill(slice(0, rest), ffn_in, lambda: grad_pre[:, columns:])
        fill(slice(rest, columns), heads, lambda: grad_low[...])


def wide_keep_kernel(
    n_planes,
    pos,
    ffn_in,
    heads,
    grad_pre,
    grad_low,
    received,
    attn_in,
    grad_qkv,
    gain_one,
    gain_two,
    far,
    near,
    kept,
    send,
    total,
    sems,
):
    wide_columns(pos[3], ffn_in, heads, grad_pre, grad_low, total, received)
    lay_out(pos, total, far, near, kept, sems, n_planes)
    last_send_kernel(pos, attn_in, grad_qkv, gain_one, gain_two, send)


def last_send_kernel(pos, left, right, gain_one, gain_two, sent):
    put_vectors(sent, left.shape[1], gain_one[:1, :], gain_two[:1, :])
    sum_send_kernel(pos, left, right, sent)


def last_keep_kernel(
    n_planes,
    pos,
    left,
    right,
    gain_one,
    gain_two,
    received,
    far,
    near,
    kept,
    vector,
    total,
    vector_low,
    sems,
):
    at = received.shape[0] - VECTOR_ROWS
    width = gain_one.shape[1]
    vector[...] = jnp.zeros_like(vector)
    vector_low[...] = jnp.zeros_like(vector_low)
    for i, gain in enumerate((gain_one, gain_two)):
        row = slice(at, at + VECTOR_ROWS)
        summed = gain[:1, :] + received[row, :width].astype(F32)[i : i + 1]
        vector[i : i + 1, :width] = summed
    vector_low[:8, :] = vector[...].astype(BF16)
    sum_keep_kernel(
        n_planes, pos, left, right, received, far, near, kept, total, sems, vector_low
    )


def own_columns(values, core):
    half = values.shape[1] // 2
    mine = lax.dynamic_slice_in_dim(values, core * half, half, 1)
    other = lax.dynamic_slice_in_dim(values, (1 - core) * half, half, 1)
    got = swap_core(other)
    return jnp.where(
        core == 0, jnp.concatenate([mine, got], axis=0), jnp.concatenate([got, mine], axis=0)
    )


def exchange_rows(total, vector, swap):
    half = total.shape[0] // 2
    send = total[half:].astype(BF16)
    if vector is not None:
        send = jnp.concatenate(
            [send, jnp.pad(vector, ((0, VECTOR_ROWS - vector.shape[0]), (0, 0))).astype(BF16)], axis=0
        )
    got = swap(send).astype(F32)
    if vector is not None:
        vector = vector + got[half : half + vector.shape[0]]
    return total[:half] + got[:half], vector


def start_sum(got, kept):
    return kept.astype(F32) + got[: kept.shape[0]].astype(F32)


def plane_sum(total, vector, n_planes):
    block = total.shape[0] // n_planes
    result, sums = total[:block], vector
    for step in range(1, n_planes):
        send = total[step * block : (step + 1) * block].astype(BF16)
        if vector is not None:
            low = jnp.pad(vector, ((0, VECTOR_ROWS - vector.shape[0]), (0, 0))).astype(BF16)
            send = jnp.concatenate([send, low], axis=0)
        got = swap_plane(send, step).astype(F32)
        result = result + got[:block]
        if vector is not None:
            sums = sums + got[block : block + vector.shape[0]]
    return result, sums


def second_sum(got_far, got_near, kept, vector=None, gate=()):
    half = kept.shape[0] // 2
    send = (kept[half:].astype(F32) + got_far[:half].astype(F32)).astype(BF16)
    if vector is not None:
        vector = vector + got_far[half : half + vector.shape[0]].astype(F32)
        low = jnp.pad(vector, ((0, VECTOR_ROWS - vector.shape[0]), (0, 0))).astype(BF16)
        send = jnp.concatenate([send, low], axis=0)
    got = swap_first(after(send, *gate) if gate else send).astype(F32)
    if vector is not None:
        vector = vector + got[half : half + vector.shape[0]]
    return kept[:half].astype(F32) + got_near.astype(F32) + got[:half], vector, (send,)


def whole_rows(total, core):
    shard = total.shape[0] // 2
    mine = lax.dynamic_slice_in_dim(total, core * shard, shard, 0)
    other = lax.dynamic_slice_in_dim(total, (1 - core) * shard, shard, 0)
    got = swap_core(other.astype(BF16)).astype(F32)
    return jnp.where(
        core == 0, jnp.concatenate([mine, got], axis=1), jnp.concatenate([got, mine], axis=1)
    )


def on_device(
    tokens,
    route,
    w_qkv,
    w_attn_out,
    w_up,
    w_down,
    gain_attn,
    gain_ffn,
    expert_in,
    expert_out,
    centroids,
    expert_gain,
    cotangent,
):
    length, features = tokens.shape
    n_expert = lax.axis_size("expert")
    n_replica = lax.axis_size("replica")
    n_dev = n_expert * n_replica
    n_planes = n_dev // 8
    per_dest = length // n_expert
    hidden_size = w_up.shape[1]
    replica = lax.axis_index("replica")
    me = lax.axis_index("expert") * n_replica + replica
    core = me % 2
    pos = jnp.stack([me // 8, (me // 4) % 2, (me // 2) % 2, core]).astype(jnp.int32)
    route_pick = (route[0][:, None] == lax.iota(jnp.int32, length)[None]).astype(BF16)

    def to_expert(picked):
        return lax.all_to_all(
            picked.reshape(n_expert, per_dest, features),
            "expert",
            split_axis=0,
            concat_axis=0,
            tiled=True,
        ).reshape(length, features)

    padded_gains = jnp.pad(jnp.stack([gain_attn, gain_ffn], axis=1), ((0, 0), (0, 254)))
    first = jnp.concatenate([w_qkv, w_attn_out, padded_gains], axis=1)
    owned = [own_columns(v, core) for v in (first, w_up, w_down)]
    join = lambda *v: jnp.concatenate(v, axis=0)
    far_bit = n_planes // 2

    def near_planes(own, *earlier):
        stack = after(own, *earlier) if earlier else own
        bit = 1
        while bit < far_bit:
            stack = join(stack, swap_plane(stack, bit))
            bit *= 2
        return stack

    own_a, own_b, own_c = owned
    near_a = near_planes(own_a)
    gate = (near_a,)
    far_a = swap_plane(near_a, far_bit)
    near_one_a = swap_first(near_a)
    near_b, near_c = near_planes(own_b, *gate), near_planes(own_c, *gate)
    gate = (far_a, near_one_a, near_b, near_c)
    far_b = swap_plane(after(near_b, *gate), far_bit)
    near_two_a = swap_second(after(join(near_a, near_one_a), *gate))
    one_a = swap_first(after(far_a, *gate))
    near_one_b = swap_first(after(near_b, *gate))
    gate = (far_b, near_two_a, one_a, near_one_b)
    far_c = swap_plane(after(near_c, *gate), far_bit)
    two_a = swap_second(after(join(far_a, one_a), *gate))
    near_two_b = swap_second(after(join(near_b, near_one_b), *gate))
    one_b = swap_first(after(far_b, *gate))
    core_near_a = swap_core(after(join(near_a, near_one_a, near_two_a), *gate))
    gate = (far_c, two_a, near_two_b, one_b, core_near_a)
    two_b = swap_second(after(join(far_b, one_b), *gate))
    near_one_c = swap_first(after(near_c, *gate))
    one_c = swap_first(after(far_c, *gate))
    core_far_a = swap_core(after(join(far_a, one_a, two_a), *gate))
    core_near_b = swap_core(after(join(near_b, near_one_b, near_two_b), *gate))
    first_pieces = [near_a, near_one_a, near_two_a, far_a, one_a, two_a, core_near_a, core_far_a]
    gate = (two_b, near_one_c, one_c, core_far_a, core_near_b)
    near_two_c = swap_second(after(join(near_c, near_one_c), *gate))
    two_c = swap_second(after(join(far_c, one_c), *gate))
    core_far_b = swap_core(after(join(far_b, one_b, two_b), *gate))
    core_one_c = swap_core(after(join(far_c, one_c), *gate))
    up_pieces = [near_b, near_one_b, near_two_b, far_b, one_b, two_b, core_near_b, core_far_b]

    wide = first.shape[1]
    planes = functools.partial
    weight_first = pltpu.VMEM((features, wide), BF16)
    weight_up = pltpu.VMEM((features, hidden_size), BF16)
    weight_down = pltpu.VMEM((hidden_size, features), BF16)
    two_sems, three_sems, plane_sems = (pltpu.SemaphoreType.DMA((n,)) for n in (2, 3, n_planes))
    unit = 2 * length * features * features

    hidden, ffn_in, attn_in, qkv, heads, gains = run_kernel(
        planes(attend_kernel, n_planes, (6, 2)),
        [pos, tokens, *first_pieces],
        "sv" + "h" * 8,
        [
            shaped(length, features, dtype=F32),
            shaped(length, features),
            shaped(length, features),
            shaped(length, 3 * features),
            shaped(length, features),
            shaped(8, features, dtype=F32),
        ],
        [weight_first, two_sems],
        flops=5 * unit,
    )
    gate = (near_two_c, two_c, core_far_b, hidden)
    core_near_c = swap_core(after(join(near_c, near_one_c, near_two_c), *gate))
    core_two_c = swap_core(after(two_c, *gate))
    grad_delta = to_expert(
        after(
            jnp.dot(route_pick, cotangent, preferred_element_type=F32).astype(BF16), hidden
        )
    )
    act, slope = run_kernel(
        planes(up_kernel, n_planes, (6, 2)),
        [pos, ffn_in, *up_pieces],
        "sv" + "h" * 8,
        [shaped(length, hidden_size), shaped(length, hidden_size, dtype=F32)],
        [weight_up, two_sems],
        flops=4 * unit,
    )
    down_pieces = [near_c, near_one_c, near_two_c, far_c, one_c, two_c, core_near_c, core_one_c, core_two_c]
    dense_out, sent = run_kernel(
        planes(down_kernel, n_planes, (6, 3)),
        [pos, act, hidden, route_pick, *down_pieces],
        "svvv" + "h" * 9,
        [shaped(length, features, dtype=F32), shaped(length, features)],
        [weight_down, plane_sems],
        flops=4 * unit,
    )
    arrived = to_expert(after(sent, grad_delta))
    inner = expert_in.shape[2]
    (
        delta,
        grad_rows,
        expert_norm,
        pair,
        sent_low,
        sent_high,
        whole_low,
        expert_grad_pre,
        vectors,
    ) = run_kernel(
        expert_kernel,
        [pos, arrived, grad_delta, centroids, expert_gain, expert_in, expert_out],
        "svvvvhh",
        [
            shaped(length, features),
            shaped(length, features),
            shaped(length, features),
            shaped(length, inner // 2 + features),
            shaped(length, inner // 4),
            shaped(length, inner // 4),
            shaped(length, features),
            shaped(length, inner),
            shaped(8, features, dtype=F32),
        ],
        [
            pltpu.VMEM((features, inner), BF16),
            pltpu.VMEM((inner, features), BF16),
            pltpu.VMEM((length, inner), BF16),
            pltpu.VMEM((length, inner), F32),
            pltpu.SemaphoreType.DMA((2, inner // 512)),
        ],
        flops=16 * unit,
    )
    returned = to_expert(grad_rows)
    got_low = swap_y(sent_low)

    (send_in,) = run_kernel(
        copies_send_kernel,
        [pos, expert_norm, expert_grad_pre, vectors],
        "svvv",
        [shaped(features // 2 + VECTOR_ROWS, inner)],
        flops=2 * unit,
    )
    got_in = swap_core(send_in)

    grad_dense, grad_dense_low, send_down = run_kernel(
        dense_grad_kernel,
        [after(pos, send_in), returned, cotangent, route_pick, act],
        "svvvv",
        [
            shaped(length, features, dtype=F32),
            shaped(length, features),
            shaped(hidden_size, features // 2),
        ],
        flops=4 * unit,
    )
    got_down = swap_core(send_down)
    got_high = swap_y(after(sent_high, send_down))
    (grad_pre,) = run_kernel(
        planes(pre_back_kernel, n_planes, (6, 3)),
        [after(pos, send_down, got_in, got_low), grad_dense_low, slope, *down_pieces],
        "svv" + "h" * 9,
        [shaped(length, hidden_size)],
        [weight_down, plane_sems],
        flops=4 * unit,
    )
    core_kept = swap_core(pair)
    got_whole = swap_y(after(whole_low, grad_pre))
    far_down, near_down, kept_down = run_kernel(
        planes(sum_keep_kernel, n_planes),
        [after(pos, grad_pre, got_high, core_kept), act, grad_dense_low, got_down],
        "svvv",
        [shaped(hidden_size // 4, features // 2)] * 2 + [shaped(hidden_size // 2, features // 2)],
        [pltpu.VMEM((hidden_size, features // 2), BF16), three_sems],
        flops=4 * unit,
        out_spaces="hhh",
    )
    got_far_down = swap_second(far_down)
    got_near_down = swap_second(after(near_down, got_far_down))
    first_in, send_in, kept_in, vectors = run_kernel(
        copies_keep_kernel,
        [after(pos, kept_down), expert_norm, expert_grad_pre, vectors, got_in],
        "svvvv",
        [
            shaped(features // 16, inner),
            shaped(3 * features // 16 + VECTOR_ROWS, inner),
            shaped(features // 4, inner),
            shaped(8, features, dtype=F32),
        ],
        flops=2 * unit,
    )
    wide_half = (hidden_size + features) // 2
    grad_hidden, grad_hidden_low, grad_gain_two, send_up = run_kernel(
        planes(hidden_back_kernel, n_planes, (6, 2)),
        [
            after(pos, send_in, got_whole),
            grad_pre,
            hidden,
            grad_dense,
            gains,
            *up_pieces,
            ffn_in,
            heads,
        ],
        "svvvv" + "h" * 8 + "vv",
        [
            shaped(length, features, dtype=F32),
            shaped(length, features),
            shaped(8, features, dtype=F32),
            shaped(features, wide_half),
        ],
        [weight_up, two_sems],
        flops=7 * unit,
    )
    got_up = swap_core(send_up)
    core_rest = swap_core(join(*(after(v, send_up) for v in (got_low, got_high, got_whole))))
    grad_qkv, grad_tokens, grad_gain_one = run_kernel(
        planes(attend_back_kernel, n_planes, (6, 2)),
        [
            after(pos, got_far_down, send_up),
            grad_hidden_low,
            qkv,
            tokens,
            grad_hidden,
            gains,
            *first_pieces,
        ],
        "svvvvv" + "h" * 8,
        [
            shaped(length, 3 * features),
            shaped(length, features, dtype=F32),
            shaped(8, features, dtype=F32),
        ],
        [pltpu.VMEM((length, features), BF16), weight_first, two_sems],
        flops=8 * unit,
    )
    in_low = swap_y(after(first_in, grad_qkv))
    down_2 = second_sum(got_far_down, got_near_down, kept_down, gate=(send_up,))
    last_half = 3 * features // 2
    far_up, near_up, kept_up, send_last = run_kernel(
        planes(wide_keep_kernel, n_planes),
        [
            after(pos, grad_qkv, down_2[0], core_rest),
            ffn_in,
            heads,
            grad_pre,
            grad_hidden_low,
            got_up,
            attn_in,
            grad_qkv,
            grad_gain_one,
            grad_gain_two,
        ],
        "s" + "v" * 9,
        [shaped(features // 4, wide_half)] * 2
        + [shaped(features // 2, wide_half), shaped(features + VECTOR_ROWS, last_half)],
        [pltpu.VMEM((features, wide_half), BF16), three_sems],
        flops=5 * unit,
        out_spaces="hhhv",
    )
    swaps = [
        functools.partial(swap_plane, bit=bit)
        for bit in (1 << i for i in reversed(range(n_planes.bit_length() - 1)))
    ]
    got_far_up = swap_second(far_up)
    got_near_up = swap_second(after(near_up, got_far_up))
    got_last = swap_core(send_last)
    (sum_expert_out,) = run_kernel(
        copies_whole_kernel,
        [
            after(pos, send_last, in_low),
            pair,
            got_low,
            got_high,
            got_whole,
            core_kept,
            core_rest,
        ],
        "s" + "v" * 6,
        [shaped(inner // n_replica, features, dtype=F32)],
        flops=4 * unit,
    )
    far, near, kept, vector = run_kernel(
        planes(last_keep_kernel, n_planes),
        [
            after(pos, sum_expert_out, got_far_up),
            attn_in,
            grad_qkv,
            grad_gain_one,
            grad_gain_two,
            got_last,
        ],
        "s" + "v" * 5,
        [
            shaped(features // 4 + VECTOR_ROWS, last_half),
            shaped(features // 4, last_half),
            shaped(features // 2, last_half),
            shaped(8, last_half, dtype=F32),
        ],
        [
            pltpu.VMEM((features, last_half), BF16),
            pltpu.VMEM((VECTOR_ROWS, last_half), BF16),
            three_sems,
        ],
        flops=2 * unit,
        out_spaces="hhhv",
    )
    up_2 = second_sum(got_far_up, got_near_up, kept_up, gate=(kept,))
    last_2 = second_sum(swap_second(far), swap_second(after(near, up_2[0])), kept, vector)
    in_high = swap_y(after(send_in, up_2[0]))
    down_3, _ = exchange_rows(after(down_2[0], kept), None, swaps[0])
    delta_home = to_expert(after(delta, down_3))
    down_3 = after(down_3, last_2[0])
    for swap in swaps[1:]:
        down_3, _ = exchange_rows(down_3, None, swap)
    up_3, _ = plane_sum(after(up_2[0], *last_2[2]), None, n_planes)
    last_3, vector = plane_sum(*last_2[:2], n_planes)
    sum_down, sum_up, sum_last = (whole_rows(v, core) for v in (down_3, up_3, last_3))
    mixed = (
        dense_out
        + lax.dot_general(
            route_pick, delta_home, (((0,), (0,)), ((), ())), preferred_element_type=F32
        )
    ).astype(BF16)
    part = features // n_replica
    sum_expert_in = kept_in.astype(F32) + join(in_low, in_high[: 3 * features // 16]).astype(F32)
    vectors = vectors[:2] + in_high[3 * features // 16 : 3 * features // 16 + 2, :features].astype(F32)
    vectors = lax.dynamic_slice_in_dim(vectors, replica * part, part, 1)
    shard = features // n_dev
    gain_grads = lax.dynamic_slice_in_dim(vector[:2, :features], me * shard, shard, 1)
    return (
        mixed,
        grad_tokens,
        sum_last,
        sum_up[:, hidden_size:],
        sum_up[:, :hidden_size],
        sum_down,
        gain_grads[0],
        gain_grads[1],
        sum_expert_in[None],
        sum_expert_out[None],
        vectors[:1],
        vectors[1:],
    )


def solution(mesh):
    placed = (
        P(("expert", "replica"), None),
        P(("expert", "replica"), None),
        P(("expert", "replica"), None),
        P(("expert", "replica"), None),
        P(("expert", "replica"), None),
        P(("expert", "replica"), None),
        P(("expert", "replica")),
        P(("expert", "replica")),
        P("expert", None, None),
        P("expert", None, None),
        P("expert", None),
        P("expert", None),
        P(("expert", "replica"), None),
    )
    return jax.shard_map(
        on_device,
        mesh=mesh,
        in_specs=placed,
        out_specs=(
            P(("expert", "replica"), None),
            P(("expert", "replica"), None),
            P(("expert", "replica"), None),
            P(("expert", "replica"), None),
            P(("expert", "replica"), None),
            P(("expert", "replica"), None),
            P(("expert", "replica")),
            P(("expert", "replica")),
            P("expert", "replica", None),
            P("expert", "replica", None),
            P("expert", "replica"),
            P("expert", "replica"),
        ),
        check_vma=False,
    )
```

```python
import functools
import math

import jax
import jax.numpy as jnp
from jax import lax
from jax.experimental import pallas as pl
from jax.experimental.pallas import tpu as pltpu
from jax.sharding import PartitionSpec as P

HEADS = 16
EPSILON = 1e-05
ALL_AXES = ("expert", "replica")
VMEM_LIMIT = 58 * 2**20
GELU_SCALE = math.sqrt(2.0 / math.pi)
BF16, F32 = jnp.bfloat16, jnp.float32


def permuted(values, target):
    n_dev = lax.axis_size("expert") * lax.axis_size("replica")
    return lax.ppermute(values, ALL_AXES, [(d, target(d, n_dev)) for d in range(n_dev)])


def swap_core(values):
    return permuted(values, lambda d, n: d ^ 1)


def swap_first(values):
    return permuted(values, lambda d, n: d ^ (2 if d % 2 else 4))


def swap_second(values):
    return permuted(values, lambda d, n: d ^ (4 if d % 2 else 2))


def swap_x(values):
    return permuted(values, lambda d, n: d ^ 4)


def swap_y(values):
    return permuted(values, lambda d, n: d ^ 2)


def swap_plane(values, bit):
    return permuted(values, lambda d, n: d ^ (8 * bit))


def after(values, *earlier):
    return lax.optimization_barrier((values,) + earlier)[0]


HINT = 30


def body_name(body):
    return getattr(body, "func", body).__name__


def run_kernel(body, args, spaces, outs, scratch=(), flops=0, out_spaces=None):
    place = {
        "v": pl.BlockSpec(memory_space=pltpu.VMEM),
        "h": pl.BlockSpec(memory_space=pl.ANY),
        "s": pl.BlockSpec(memory_space=pltpu.SMEM),
    }
    moved = sum(a.size * a.dtype.itemsize for a in args)
    moved += sum(o.size * o.dtype.itemsize for o in outs)
    return pl.pallas_call(
        body,
        name=body_name(body),
        out_shape=list(outs),
        in_specs=[place[s] for s in spaces],
        out_specs=[place[s] for s in (out_spaces or "v" * len(outs))],
        scratch_shapes=list(scratch),
        cost_estimate=pl.CostEstimate(flops=int(flops * HINT), bytes_accessed=int(moved * HINT), transcendentals=0),
        compiler_params=pltpu.CompilerParams(vmem_limit_bytes=VMEM_LIMIT),
    )(*args)


def shaped(*shape, dtype=BF16):
    return jax.ShapeDtypeStruct(shape, dtype)


def dot_nn(left, right):
    return jnp.dot(left, right, preferred_element_type=F32)


def dot_nt(left, right):
    return lax.dot_general(left, right, (((1,), (1,)), ((), ())), preferred_element_type=F32)


def dot_tn(left, right):
    return lax.dot_general(left, right, (((0,), (0,)), ((), ())), preferred_element_type=F32)


def normed(values):
    centered = values - jnp.mean(values, axis=-1, keepdims=True)
    inverse = lax.rsqrt(jnp.mean(centered * centered, axis=-1, keepdims=True) + EPSILON)
    return centered * inverse, inverse


def norm_back(grad_normed, norm, inverse):
    return inverse * (
        grad_normed
        - jnp.mean(grad_normed, axis=-1, keepdims=True)
        - norm * jnp.mean(grad_normed * norm, axis=-1, keepdims=True)
    )


def gelu_both(values):
    square = values * values
    bent = jnp.tanh(GELU_SCALE * values * (1.0 + 0.044715 * square))
    half = 0.5 * (1.0 + bent)
    slope = half + 0.5 * values * (1.0 - bent * bent) * (
        GELU_SCALE * (1.0 + 3.0 * 0.044715 * square)
    )
    return values * half, slope


def row_start(pos, core, first, second, step, n_planes, block):
    x, y = pos[1], pos[2]
    flip = lambda v, on: 1 - v if on else v
    across = jnp.where(core == 0, flip(x, first), flip(x, second))
    along = jnp.where(core == 0, flip(y, second), flip(y, first))
    plane = pos[0] ^ step
    return pl.multiple_of(((plane * 2 + across) * 2 + along) * block, block)


PIECE_ORDER = ((0, 0), (1, 0), (0, 1), (1, 1))


def load_weight(pos, sides, target, sems, n_planes, by_plane):
    block = target.shape[0] // (4 * n_planes)
    part = n_planes // 2
    order = [(far, *chip) for far in range(2) for chip in PIECE_ORDER]
    copies = []
    for side, pieces in enumerate(sides):
        half = pieces[0].shape[1]
        core = pos[3] if side == 0 else 1 - pos[3]
        lanes = pl.ds(pl.multiple_of(core * half, 128), half)
        spots = [(piece, at) for piece in pieces for at in range(0, piece.shape[0], block * part)]
        for (far, first, second), (piece, at) in zip(order, spots, strict=True):
            for step in range(part):
                row = row_start(pos, core, first, second, far * part + step, n_planes, block)
                copies.append(
                    (
                        far * part + step if by_plane else side,
                        pltpu.make_async_copy(
                            piece.at[pl.ds(at + step * block, block), :],
                            target.at[pl.ds(row, block), lanes],
                            sems.at[far * part + step] if by_plane else sems.at[core],
                        ),
                    )
                )
    for _, copy in sorted(copies, key=lambda pair: pair[0]):
        copy.start()


def wait_half(target, core, sems):
    half = target.at[:, : target.shape[1] // 2]
    pltpu.make_async_copy(half, half, sems.at[core]).wait()


def wait_step(pos, target, sems, step, n_planes):
    rows = target.shape[0] // n_planes
    part = target.at[:rows, :]
    pltpu.make_async_copy(part, part, sems.at[step]).wait()
    return pl.multiple_of((pos[0] ^ step) * rows, rows)


def wait_whole(target, sem):
    pltpu.make_async_copy(target, target, sem).wait()


def causal_mask(length):
    return lax.broadcasted_iota(jnp.int32, (length, length), 0) >= lax.broadcasted_iota(
        jnp.int32, (length, length), 1
    )


def take_sides(refs, split):
    mine, both = split[0], sum(split)
    return (refs[:mine], refs[mine:both]), refs[both:]


def attend_kernel(n_planes, split, pos, tokens, *refs):
    sides, refs = take_sides(refs, split)
    hidden, ffn_in, attn_in, qkv, heads, gains, weight, sem = refs
    length, width = tokens.shape
    load_weight(pos, sides, weight, sem, n_planes, False)
    inputs = tokens[...].astype(F32)
    norm, _ = normed(inputs)
    wait_half(weight, 1, sem)
    columns = weight[:, 4 * width : 4 * width + 128].astype(F32)
    gains[...] = columns.T[:8]
    attn_in[...] = (norm * gains[0:1, :]).astype(BF16)
    wait_half(weight, 0, sem)
    for part in range(3):
        lanes = slice(part * width, (part + 1) * width)
        qkv[:, lanes] = dot_nn(attn_in[...], weight[:, lanes]).astype(BF16)
    head_size = width // HEADS
    causal = causal_mask(length)
    lane = lax.broadcasted_iota(jnp.int32, (1, 2 * head_size), 1)

    def pair(i, _):
        at = pl.multiple_of(i * 2 * head_size, 2 * head_size)
        query = qkv[:, pl.ds(at, 2 * head_size)] * (head_size**-0.5)
        key_rows = qkv[:, pl.ds(width + at, 2 * head_size)]
        value_rows = qkv[:, pl.ds(2 * width + at, 2 * head_size)]
        mixed = []
        for head in range(2):
            own = (lane // head_size) == head
            scores = dot_nt(jnp.where(own, query, 0).astype(BF16), key_rows)
            scores = jnp.where(causal, scores, -1e30)
            shifted = jnp.exp(scores - jnp.max(scores, axis=-1, keepdims=True))
            probs = shifted / jnp.sum(shifted, axis=-1, keepdims=True)
            mixed.append(dot_nn(probs.astype(BF16), value_rows))
        heads[:, pl.ds(at, 2 * head_size)] = jnp.where(lane < head_size, mixed[0], mixed[1]).astype(
            BF16
        )
        return 0

    lax.fori_loop(0, HEADS // 2, pair, 0)
    hidden[...] = inputs + dot_nn(heads[...], weight[:, 3 * width : 4 * width])
    norm_two, _ = normed(hidden[...])
    ffn_in[...] = (norm_two * gains[1:2, :]).astype(BF16)


def up_kernel(n_planes, split, pos, ffn_in, *refs):
    sides, (act, slope, weight, sem) = take_sides(refs, split)
    load_weight(pos, sides, weight, sem, n_planes, False)
    chunk = 512
    half = weight.shape[1] // 2
    for side in range(2):
        core = pos[3] if side == 0 else 1 - pos[3]
        wait_half(weight, core, sem)
        for i in range(half // chunk):
            lanes = pl.ds(pl.multiple_of(core * half + i * chunk, chunk), chunk)
            value, grad = gelu_both(dot_nn(ffn_in[...], weight[:, lanes]))
            act[:, lanes] = value.astype(BF16)
            slope[:, lanes] = grad


def down_kernel(n_planes, split, pos, act, hidden, pick, *refs):
    sides, (dense_out, sent, weight, sem) = take_sides(refs, split)
    load_weight(pos, sides, weight, sem, n_planes, True)
    rows = weight.shape[0] // n_planes
    total = hidden[...]
    for step in range(n_planes):
        at = pl.ds(wait_step(pos, weight, sem, step, n_planes), rows)
        total = total + dot_nn(act[:, at], weight[at, :])
    dense_out[...] = total
    sent[...] = dot_nn(pick[...], total.astype(BF16)).astype(BF16)


def expert_kernel(
    pos,
    arrived,
    grad_delta,
    centroid,
    norm_gain,
    weight_in,
    weight_out,
    delta,
    grad_rows,
    norm_low,
    kept,
    sent_low,
    sent_high,
    whole_low,
    grad_pre,
    vectors,
    w_in,
    w_out,
    act,
    slope,
    sems,
):
    chunk = 512
    n_chunks = w_in.shape[1] // chunk
    spans = [pl.ds(i * chunk, chunk) for i in range(n_chunks)]
    copies_in = [
        pltpu.make_async_copy(weight_in.at[0, :, span], w_in.at[:, span], sems.at[0, i])
        for i, span in enumerate(spans)
    ]
    copies_out = [
        pltpu.make_async_copy(weight_out.at[0, span, :], w_out.at[span, :], sems.at[1, i])
        for i, span in enumerate(spans)
    ]
    for copy in copies_in + copies_out:
        copy.start()
    rows = arrived[...].astype(F32)
    center = centroid[...].astype(F32)
    gain = norm_gain[...].astype(F32)
    gate = jax.nn.sigmoid(jnp.sum(rows * center, axis=-1, keepdims=True))
    norm, inverse = normed(rows)
    norm_low[...] = (norm * gain).astype(BF16)
    grad_out = grad_delta[...].astype(F32)
    grad_whole = gate * grad_out
    whole_low[...] = grad_whole.astype(BF16)
    for copy, span in zip(copies_in, spans):
        copy.wait()
        value, grad = gelu_both(dot_nn(norm_low[...], w_in[:, span]))
        act[:, span] = value.astype(BF16)
        slope[:, span] = grad
    half = act.shape[1] // 2
    kept[:, :half] = act[:, pl.ds(pl.multiple_of(pos[2] * half, 128), half)]
    other = pl.multiple_of((1 - pos[2]) * half, 128)
    sent_low[...] = act[:, pl.ds(other, half // 2)]
    sent_high[...] = act[:, pl.ds(pl.multiple_of(other + half // 2, 128), half // 2)]
    kept[:, half:] = whole_low[...]
    for copy in copies_out:
        copy.wait()
    whole = rows + dot_nn(act[...], w_out[...])
    delta[...] = (gate * whole).astype(BF16)
    grad_gate = jnp.sum(grad_out * whole, axis=-1, keepdims=True)
    grad_logit = grad_gate * gate * (1.0 - gate)

    for span in spans:
        grad_act = dot_nt(whole_low[...], w_out[span, :])
        grad_pre[:, span] = (grad_act * slope[:, span]).astype(BF16)
    grad_norm = dot_nt(grad_pre[...], w_in[...])
    vectors[...] = jnp.zeros_like(vectors)
    vectors[0:1, :] = jnp.sum(grad_logit * rows, axis=0, keepdims=True)
    vectors[1:2, :] = jnp.sum(grad_norm * norm, axis=0, keepdims=True)
    back = norm_back(grad_norm * gain, norm, inverse)
    grad_rows[...] = (grad_whole + grad_logit * center + back).astype(BF16)


VECTOR_ROWS = 16


def put_vectors(target, at, one, two):
    width = one.shape[1]
    row = lax.broadcasted_iota(jnp.int32, (VECTOR_ROWS, width), 0)
    both = jnp.where(row == 0, one, jnp.where(row == 1, two, 0.0))
    target[at : at + VECTOR_ROWS, :] = jnp.zeros((VECTOR_ROWS, target.shape[1]), BF16)
    target[at : at + VECTOR_ROWS, :width] = both.astype(BF16)


def copies_send_kernel(pos, left, right, vectors, sent):
    block = left.shape[1] // 4
    other = 1 - pos[3]
    tile = 256

    def step(i, _):
        outer, inner = lax.div(i, block // tile), lax.rem(i, block // tile)
        at = pl.multiple_of((2 * outer + other) * block + inner * tile, tile)
        sent[pl.ds(pl.multiple_of(i * tile, tile), tile), :] = dot_tn(
            left[:, pl.ds(at, tile)], right[...]
        ).astype(BF16)
        return 0

    lax.fori_loop(0, 2 * block // tile, step, 0)
    put_vectors(sent, 2 * block, vectors[:1, :], vectors[1:2, :])


def copies_keep_kernel(
    pos, left, right, vectors, received, sent_first, sent, kept, vector_sums
):
    block = left.shape[1] // 4
    core, y = pos[3], pos[2]
    early = sent_first.shape[0]
    for turn in range(2):
        outer = 1 - y if turn else y
        at = pl.ds(pl.multiple_of((2 * outer + core) * block, 128), block)
        there = pl.ds(pl.multiple_of(outer * block, 16), block)
        value = dot_tn(left[:, at], right[...]) + received[there, :].astype(F32)
        if turn:
            sent_first[...] = value[:early].astype(BF16)
            sent[: block - early, :] = value[early:].astype(BF16)
        else:
            kept[...] = value.astype(BF16)
    width = vectors.shape[1]
    got = received[2 * block : 2 * block + VECTOR_ROWS, :width].astype(F32)
    vector_sums[...] = vectors[...] + got[:8]
    put_vectors(sent, block - early, vector_sums[:1, :], vector_sums[1:2, :])


def copies_whole_kernel(pos, kept, low, high, whole, core_kept, core_rest, result):
    tile = 512
    rows = kept.shape[0]
    width = kept.shape[1] - result.shape[1]
    start = pos[3] * (width // 2)

    def step(i, _):
        at = pl.ds(pl.multiple_of(i * tile, tile), tile)
        mine = jnp.where(pos[3] == 0, low[:, at], high[:, at])
        other = jnp.where(pos[3] == 0, core_rest[:rows, at], core_rest[rows : 2 * rows, at])
        both = pl.ds(pl.multiple_of(start + i * tile, tile), tile)
        result[at, :] = (
            dot_tn(kept[:, both], kept[:, width:])
            + dot_tn(mine, whole[...])
            + dot_tn(core_kept[:, both], core_kept[:, width:])
            + dot_tn(other, core_rest[2 * rows :, :])
        )
        return 0

    lax.fori_loop(0, result.shape[0] // tile, step, 0)


def dense_grad_kernel(pos, returned, cotangent, pick, act, grad_dense, grad_low, sent):
    grad_dense[...] = cotangent[...].astype(F32) + dot_tn(pick[...], returned[...])
    grad_low[...] = grad_dense[...].astype(BF16)
    sum_send_kernel(pos, act, grad_low, sent)


def sum_send_kernel(pos, left, right, sent):
    half = right.shape[1] // 2
    lanes = pl.ds(pl.multiple_of((1 - pos[3]) * half, 128), half)
    tile = min(1024, left.shape[1] // 2)

    def step(i, _):
        rows = pl.ds(pl.multiple_of(i * tile, tile), tile)
        sent[rows, :] = dot_tn(left[:, rows], right[:, lanes]).astype(BF16)
        return 0

    lax.fori_loop(0, left.shape[1] // tile, step, 0)


def lay_out(pos, total, far, near, kept, sems, n_planes, vector=None):
    block = total.shape[0] // (4 * n_planes)
    for second in (1, 0):
        for step in range(n_planes):
            for first in (1, 0):
                row = row_start(pos, pos[3], second, first, step, n_planes, block)
                if first:
                    target, at, sem = (far if second else near), step, sems.at[1 + second]
                else:
                    target, at, sem = kept, second * n_planes + step, sems.at[0]
                pltpu.make_async_copy(
                    total.at[pl.ds(row, block), :], target.at[pl.ds(at * block, block), :], sem
                ).start()
    if vector is not None:
        pltpu.make_async_copy(
            vector, far.at[pl.ds(total.shape[0] // 4, VECTOR_ROWS), :], sems.at[2]
        ).start()
    for target, sem in ((kept, 0), (near, 1), (far, 2)):
        wait_whole(target, sems.at[sem])


def sum_keep_kernel(
    n_planes, pos, left, right, received, far, near, kept, total, sems, vector=None
):
    half = right.shape[1] // 2
    lanes = pl.ds(pl.multiple_of(pos[3] * half, 128), half)
    tile = min(1024, left.shape[1] // 2)

    def step(i, _):
        rows = pl.ds(pl.multiple_of(i * tile, tile), tile)
        total[rows, :] = (
            dot_tn(left[:, rows], right[:, lanes]) + received[rows, :].astype(F32)
        ).astype(BF16)
        return 0

    lax.fori_loop(0, left.shape[1] // tile, step, 0)
    lay_out(pos, total, far, near, kept, sems, n_planes, vector)


def pre_back_kernel(n_planes, split, pos, grad_low, slope, *refs):
    sides, (grad_pre, weight, sem) = take_sides(refs, split)
    load_weight(pos, sides, weight, sem, n_planes, True)
    rows = weight.shape[0] // n_planes
    chunk = min(512, rows)
    for step in range(n_planes):
        start = wait_step(pos, weight, sem, step, n_planes)
        for i in range(rows // chunk):
            at = pl.ds(pl.multiple_of(start + i * chunk, chunk), chunk)
            grad_pre[:, at] = (dot_nt(grad_low[...], weight[at, :]) * slope[:, at]).astype(BF16)


def hidden_back_kernel(n_planes, split, pos, grad_pre, hidden, grad_dense, gains, *refs):
    sides, (ffn_in, heads, grad_hidden, grad_low, grad_gain, send, weight, sem) = take_sides(refs, split)
    load_weight(pos, sides, weight, sem, n_planes, False)
    norm, inverse = normed(hidden[...])
    half = weight.shape[1] // 2
    grad_in = 0.0
    for side in range(2):
        core = pos[3] if side == 0 else 1 - pos[3]
        wait_half(weight, core, sem)
        lanes = pl.ds(pl.multiple_of(core * half, 128), half)
        grad_in = grad_in + dot_nt(grad_pre[:, lanes], weight[:, lanes])
    grad_gain[...] = jnp.zeros_like(grad_gain)
    grad_gain[0:1, :] = jnp.sum(grad_in * norm, axis=0, keepdims=True)
    grad_hidden[...] = grad_dense[...] + norm_back(grad_in * gains[1:2, :], norm, inverse)
    grad_low[...] = grad_hidden[...].astype(BF16)
    wide_columns(1 - pos[3], ffn_in, heads, grad_pre, grad_low, send, None)


def attend_back_kernel(n_planes, split, pos, grad_low, qkv, tokens, grad_hidden, gains, *refs):
    sides, refs = take_sides(refs, split)
    grad_qkv, grad_tokens, grad_gain, grad_heads, weight, sem = refs
    length, width = tokens.shape
    head_size = width // HEADS
    load_weight(pos, sides, weight, sem, n_planes, False)
    inputs = tokens[...].astype(F32)
    norm, inverse = normed(inputs)
    causal = causal_mask(length)
    lane = lax.broadcasted_iota(jnp.int32, (1, 2 * head_size), 1)
    wait_half(weight, 1, sem)
    grad_heads[...] = dot_nt(grad_low[...], weight[:, 3 * width : 4 * width]).astype(BF16)
    factor = head_size**-0.5

    def pair(i, _):
        at = pl.multiple_of(i * 2 * head_size, 2 * head_size)
        query = qkv[:, pl.ds(at, 2 * head_size)]
        key_rows = qkv[:, pl.ds(width + at, 2 * head_size)]
        value_rows = qkv[:, pl.ds(2 * width + at, 2 * head_size)]
        grad_out = grad_heads[:, pl.ds(at, 2 * head_size)]
        sums = [0.0, 0.0, 0.0]
        for head in range(2):
            own = (lane // head_size) == head
            masked = lambda v: jnp.where(own, v, 0).astype(BF16)
            own_query, own_grad = masked(query), masked(grad_out)
            scores = dot_nt(own_query, key_rows) * factor
            scores = jnp.where(causal, scores, -1e30)
            shifted = jnp.exp(scores - jnp.max(scores, axis=-1, keepdims=True))
            probs = shifted / jnp.sum(shifted, axis=-1, keepdims=True)
            grad_probs = dot_nt(own_grad, value_rows)
            row_terms = jnp.sum(probs * grad_probs, axis=-1, keepdims=True)
            grad_scores = (probs * (grad_probs - row_terms)).astype(BF16)
            sums[0] = sums[0] + dot_nn(grad_scores, masked(key_rows)) * factor
            sums[1] = sums[1] + dot_tn(grad_scores, own_query) * factor
            sums[2] = sums[2] + dot_tn(probs.astype(BF16), own_grad)
        for part in range(3):
            grad_qkv[:, pl.ds(part * width + at, 2 * head_size)] = sums[part].astype(BF16)
        return 0

    lax.fori_loop(0, HEADS // 2, pair, 0, unroll=True)
    wait_half(weight, 0, sem)
    grad_in = dot_nt(grad_qkv[...], weight[:, : 3 * width])
    grad_gain[...] = jnp.zeros_like(grad_gain)
    grad_gain[0:1, :] = jnp.sum(grad_in * norm, axis=0, keepdims=True)
    grad_tokens[...] = grad_hidden[...] + norm_back(grad_in * gains[0:1, :], norm, inverse)


def wide_columns(half, ffn_in, heads, grad_pre, grad_low, target, received):
    width = ffn_in.shape[1]
    columns = target.shape[1]
    rest = grad_pre.shape[1] - columns
    tile = 512

    def fill(lanes, left, right):
        def step(i, _):
            rows = pl.ds(pl.multiple_of(i * tile, tile), tile)
            value = dot_tn(left[:, rows], right())
            if received is not None:
                value = value + received[rows, lanes].astype(F32)
            target[rows, lanes] = value.astype(BF16)
            return 0

        lax.fori_loop(0, width // tile, step, 0)

    @pl.when(half == 0)
    def _():
        fill(slice(0, columns), ffn_in, lambda: grad_pre[:, :columns])

    @pl.when(half == 1)
    def _():
        fill(slice(0, rest), ffn_in, lambda: grad_pre[:, columns:])
        fill(slice(rest, columns), heads, lambda: grad_low[...])


def wide_keep_kernel(
    n_planes,
    pos,
    ffn_in,
    heads,
    grad_pre,
    grad_low,
    received,
    attn_in,
    grad_qkv,
    gain_one,
    gain_two,
    far,
    near,
    kept,
    send,
    total,
    sems,
):
    wide_columns(pos[3], ffn_in, heads, grad_pre, grad_low, total, received)
    lay_out(pos, total, far, near, kept, sems, n_planes)
    last_send_kernel(pos, attn_in, grad_qkv, gain_one, gain_two, send)


def last_send_kernel(pos, left, right, gain_one, gain_two, sent):
    put_vectors(sent, left.shape[1], gain_one[:1, :], gain_two[:1, :])
    sum_send_kernel(pos, left, right, sent)


def last_keep_kernel(
    n_planes,
    pos,
    left,
    right,
    gain_one,
    gain_two,
    received,
    far,
    near,
    kept,
    vector,
    total,
    vector_low,
    sems,
):
    at = received.shape[0] - VECTOR_ROWS
    width = gain_one.shape[1]
    vector[...] = jnp.zeros_like(vector)
    vector_low[...] = jnp.zeros_like(vector_low)
    for i, gain in enumerate((gain_one, gain_two)):
        row = slice(at, at + VECTOR_ROWS)
        summed = gain[:1, :] + received[row, :width].astype(F32)[i : i + 1]
        vector[i : i + 1, :width] = summed
    vector_low[:8, :] = vector[...].astype(BF16)
    sum_keep_kernel(
        n_planes, pos, left, right, received, far, near, kept, total, sems, vector_low
    )


def own_columns(values, core):
    half = values.shape[1] // 2
    mine = lax.dynamic_slice_in_dim(values, core * half, half, 1)
    other = lax.dynamic_slice_in_dim(values, (1 - core) * half, half, 1)
    got = swap_core(other)
    return jnp.where(
        core == 0, jnp.concatenate([mine, got], axis=0), jnp.concatenate([got, mine], axis=0)
    )


def exchange_rows(total, vector, swap):
    half = total.shape[0] // 2
    send = total[half:].astype(BF16)
    if vector is not None:
        send = jnp.concatenate(
            [send, jnp.pad(vector, ((0, VECTOR_ROWS - vector.shape[0]), (0, 0))).astype(BF16)], axis=0
        )
    got = swap(send).astype(F32)
    if vector is not None:
        vector = vector + got[half : half + vector.shape[0]]
    return total[:half] + got[:half], vector


def start_sum(got, kept):
    return kept.astype(F32) + got[: kept.shape[0]].astype(F32)


def plane_sum(total, vector, n_planes):
    block = total.shape[0] // n_planes
    result, sums = total[:block], vector
    for step in range(1, n_planes):
        send = total[step * block : (step + 1) * block].astype(BF16)
        if vector is not None:
            low = jnp.pad(vector, ((0, VECTOR_ROWS - vector.shape[0]), (0, 0))).astype(BF16)
            send = jnp.concatenate([send, low], axis=0)
        got = swap_plane(send, step).astype(F32)
        result = result + got[:block]
        if vector is not None:
            sums = sums + got[block : block + vector.shape[0]]
    return result, sums


def second_sum(got_far, got_near, kept, vector=None, gate=()):
    half = kept.shape[0] // 2
    send = (kept[half:].astype(F32) + got_far[:half].astype(F32)).astype(BF16)
    if vector is not None:
        vector = vector + got_far[half : half + vector.shape[0]].astype(F32)
        low = jnp.pad(vector, ((0, VECTOR_ROWS - vector.shape[0]), (0, 0))).astype(BF16)
        send = jnp.concatenate([send, low], axis=0)
    got = swap_first(after(send, *gate) if gate else send).astype(F32)
    if vector is not None:
        vector = vector + got[half : half + vector.shape[0]]
    return kept[:half].astype(F32) + got_near.astype(F32) + got[:half], vector, (send,)


def whole_rows(total, core):
    shard = total.shape[0] // 2
    mine = lax.dynamic_slice_in_dim(total, core * shard, shard, 0)
    other = lax.dynamic_slice_in_dim(total, (1 - core) * shard, shard, 0)
    got = swap_core(other.astype(BF16)).astype(F32)
    return jnp.where(
        core == 0, jnp.concatenate([mine, got], axis=1), jnp.concatenate([got, mine], axis=1)
    )


def on_device(
    tokens,
    route,
    w_qkv,
    w_attn_out,
    w_up,
    w_down,
    gain_attn,
    gain_ffn,
    expert_in,
    expert_out,
    centroids,
    expert_gain,
    cotangent,
):
    length, features = tokens.shape
    n_expert = lax.axis_size("expert")
    n_replica = lax.axis_size("replica")
    n_dev = n_expert * n_replica
    n_planes = n_dev // 8
    per_dest = length // n_expert
    hidden_size = w_up.shape[1]
    replica = lax.axis_index("replica")
    me = lax.axis_index("expert") * n_replica + replica
    core = me % 2
    pos = jnp.stack([me // 8, (me // 4) % 2, (me // 2) % 2, core]).astype(jnp.int32)
    route_pick = (route[0][:, None] == lax.iota(jnp.int32, length)[None]).astype(BF16)

    def to_expert(picked):
        return lax.all_to_all(
            picked.reshape(n_expert, per_dest, features),
            "expert",
            split_axis=0,
            concat_axis=0,
            tiled=True,
        ).reshape(length, features)

    padded_gains = jnp.pad(jnp.stack([gain_attn, gain_ffn], axis=1), ((0, 0), (0, 254)))
    first = jnp.concatenate([w_qkv, w_attn_out, padded_gains], axis=1)
    owned = [own_columns(v, core) for v in (first, w_up, w_down)]
    join = lambda *v: jnp.concatenate(v, axis=0)
    far_bit = n_planes // 2

    def near_planes(own, *earlier):
        stack = after(own, *earlier) if earlier else own
        bit = 1
        while bit < far_bit:
            stack = join(stack, swap_plane(stack, bit))
            bit *= 2
        return stack

    own_a, own_b, own_c = owned
    near_a = near_planes(own_a)
    gate = (near_a,)
    far_a = swap_plane(near_a, far_bit)
    near_one_a = swap_first(near_a)
    near_b, near_c = near_planes(own_b, *gate), near_planes(own_c, *gate)
    gate = (far_a, near_one_a, near_b, near_c)
    far_b = swap_plane(after(near_b, *gate), far_bit)
    near_two_a = swap_second(after(join(near_a, near_one_a), *gate))
    one_a = swap_first(after(far_a, *gate))
    near_one_b = swap_first(after(near_b, *gate))
    gate = (far_b, near_two_a, one_a, near_one_b)
    far_c = swap_plane(after(near_c, *gate), far_bit)
    two_a = swap_second(after(join(far_a, one_a), *gate))
    near_two_b = swap_second(after(join(near_b, near_one_b), *gate))
    one_b = swap_first(after(far_b, *gate))
    core_near_a = swap_core(after(join(near_a, near_one_a, near_two_a), *gate))
    gate = (far_c, two_a, near_two_b, one_b, core_near_a)
    two_b = swap_second(after(join(far_b, one_b), *gate))
    near_one_c = swap_first(after(near_c, *gate))
    one_c = swap_first(after(far_c, *gate))
    core_far_a = swap_core(after(join(far_a, one_a, two_a), *gate))
    core_near_b = swap_core(after(join(near_b, near_one_b, near_two_b), *gate))
    first_pieces = [near_a, near_one_a, near_two_a, far_a, one_a, two_a, core_near_a, core_far_a]
    gate = (two_b, near_one_c, one_c, core_far_a, core_near_b)
    near_two_c = swap_second(after(join(near_c, near_one_c), *gate))
    two_c = swap_second(after(join(far_c, one_c), *gate))
    core_far_b = swap_core(after(join(far_b, one_b, two_b), *gate))
    core_one_c = swap_core(after(join(far_c, one_c), *gate))
    up_pieces = [near_b, near_one_b, near_two_b, far_b, one_b, two_b, core_near_b, core_far_b]

    wide = first.shape[1]
    planes = functools.partial
    weight_first = pltpu.VMEM((features, wide), BF16)
    weight_up = pltpu.VMEM((features, hidden_size), BF16)
    weight_down = pltpu.VMEM((hidden_size, features), BF16)
    two_sems, three_sems, plane_sems = (pltpu.SemaphoreType.DMA((n,)) for n in (2, 3, n_planes))
    unit = 2 * length * features * features

    hidden, ffn_in, attn_in, qkv, heads, gains = run_kernel(
        planes(attend_kernel, n_planes, (6, 2)),
        [pos, tokens, *first_pieces],
        "sv" + "h" * 8,
        [
            shaped(length, features, dtype=F32),
            shaped(length, features),
            shaped(length, features),
            shaped(length, 3 * features),
            shaped(length, features),
            shaped(8, features, dtype=F32),
        ],
        [weight_first, two_sems],
        flops=5 * unit,
    )
    gate = (near_two_c, two_c, core_far_b, hidden)
    core_near_c = swap_core(after(join(near_c, near_one_c, near_two_c), *gate))
    core_two_c = swap_core(after(two_c, *gate))
    grad_delta = to_expert(
        after(
            jnp.dot(route_pick, cotangent, preferred_element_type=F32).astype(BF16), hidden
        )
    )
    act, slope = run_kernel(
        planes(up_kernel, n_planes, (6, 2)),
        [pos, ffn_in, *up_pieces],
        "sv" + "h" * 8,
        [shaped(length, hidden_size), shaped(length, hidden_size, dtype=F32)],
        [weight_up, two_sems],
        flops=4 * unit,
    )
    down_pieces = [near_c, near_one_c, near_two_c, far_c, one_c, two_c, core_near_c, core_one_c, core_two_c]
    dense_out, sent = run_kernel(
        planes(down_kernel, n_planes, (6, 3)),
        [pos, act, hidden, route_pick, *down_pieces],
        "svvv" + "h" * 9,
        [shaped(length, features, dtype=F32), shaped(length, features)],
        [weight_down, plane_sems],
        flops=4 * unit,
    )
    arrived = to_expert(after(sent, grad_delta))
    inner = expert_in.shape[2]
    (
        delta,
        grad_rows,
        expert_norm,
        pair,
        sent_low,
        sent_high,
        whole_low,
        expert_grad_pre,
        vectors,
    ) = run_kernel(
        expert_kernel,
        [pos, arrived, grad_delta, centroids, expert_gain, expert_in, expert_out],
        "svvvvhh",
        [
            shaped(length, features),
            shaped(length, features),
            shaped(length, features),
            shaped(length, inner // 2 + features),
            shaped(length, inner // 4),
            shaped(length, inner // 4),
            shaped(length, features),
            shaped(length, inner),
            shaped(8, features, dtype=F32),
        ],
        [
            pltpu.VMEM((features, inner), BF16),
            pltpu.VMEM((inner, features), BF16),
            pltpu.VMEM((length, inner), BF16),
            pltpu.VMEM((length, inner), F32),
            pltpu.SemaphoreType.DMA((2, inner // 512)),
        ],
        flops=16 * unit,
    )
    returned = to_expert(grad_rows)
    got_low = swap_y(sent_low)

    (send_in,) = run_kernel(
        copies_send_kernel,
        [pos, expert_norm, expert_grad_pre, vectors],
        "svvv",
        [shaped(features // 2 + VECTOR_ROWS, inner)],
        flops=2 * unit,
    )
    got_in = swap_core(send_in)

    grad_dense, grad_dense_low, send_down = run_kernel(
        dense_grad_kernel,
        [after(pos, send_in), returned, cotangent, route_pick, act],
        "svvvv",
        [
            shaped(length, features, dtype=F32),
            shaped(length, features),
            shaped(hidden_size, features // 2),
        ],
        flops=4 * unit,
    )
    got_down = swap_core(send_down)
    got_high = swap_y(after(sent_high, send_down))
    (grad_pre,) = run_kernel(
        planes(pre_back_kernel, n_planes, (6, 3)),
        [after(pos, send_down, got_in, got_low), grad_dense_low, slope, *down_pieces],
        "svv" + "h" * 9,
        [shaped(length, hidden_size)],
        [weight_down, plane_sems],
        flops=4 * unit,
    )
    core_kept = swap_core(pair)
    got_whole = swap_y(after(whole_low, grad_pre))
    far_down, near_down, kept_down = run_kernel(
        planes(sum_keep_kernel, n_planes),
        [after(pos, grad_pre, got_high, core_kept), act, grad_dense_low, got_down],
        "svvv",
        [shaped(hidden_size // 4, features // 2)] * 2 + [shaped(hidden_size // 2, features // 2)],
        [pltpu.VMEM((hidden_size, features // 2), BF16), three_sems],
        flops=4 * unit,
        out_spaces="hhh",
    )
    got_far_down = swap_second(far_down)
    got_near_down = swap_second(after(near_down, got_far_down))
    first_in, send_in, kept_in, vectors = run_kernel(
        copies_keep_kernel,
        [after(pos, kept_down), expert_norm, expert_grad_pre, vectors, got_in],
        "svvvv",
        [
            shaped(features // 16, inner),
            shaped(3 * features // 16 + VECTOR_ROWS, inner),
            shaped(features // 4, inner),
            shaped(8, features, dtype=F32),
        ],
        flops=2 * unit,
    )
    wide_half = (hidden_size + features) // 2
    grad_hidden, grad_hidden_low, grad_gain_two, send_up = run_kernel(
        planes(hidden_back_kernel, n_planes, (6, 2)),
        [
            after(pos, send_in, got_whole),
            grad_pre,
            hidden,
            grad_dense,
            gains,
            *up_pieces,
            ffn_in,
            heads,
        ],
        "svvvv" + "h" * 8 + "vv",
        [
            shaped(length, features, dtype=F32),
            shaped(length, features),
            shaped(8, features, dtype=F32),
            shaped(features, wide_half),
        ],
        [weight_up, two_sems],
        flops=7 * unit,
    )
    got_up = swap_core(send_up)
    core_rest = swap_core(join(*(after(v, send_up) for v in (got_low, got_high, got_whole))))
    grad_qkv, grad_tokens, grad_gain_one = run_kernel(
        planes(attend_back_kernel, n_planes, (6, 2)),
        [
            after(pos, got_far_down, send_up),
            grad_hidden_low,
            qkv,
            tokens,
            grad_hidden,
            gains,
            *first_pieces,
        ],
        "svvvvv" + "h" * 8,
        [
            shaped(length, 3 * features),
            shaped(length, features, dtype=F32),
            shaped(8, features, dtype=F32),
        ],
        [pltpu.VMEM((length, features), BF16), weight_first, two_sems],
        flops=8 * unit,
    )
    in_low = swap_y(after(first_in, grad_qkv))
    down_2 = second_sum(got_far_down, got_near_down, kept_down, gate=(send_up,))
    last_half = 3 * features // 2
    far_up, near_up, kept_up, send_last = run_kernel(
        planes(wide_keep_kernel, n_planes),
        [
            after(pos, grad_qkv, down_2[0], core_rest),
            ffn_in,
            heads,
            grad_pre,
            grad_hidden_low,
            got_up,
            attn_in,
            grad_qkv,
            grad_gain_one,
            grad_gain_two,
        ],
        "s" + "v" * 9,
        [shaped(features // 4, wide_half)] * 2
        + [shaped(features // 2, wide_half), shaped(features + VECTOR_ROWS, last_half)],
        [pltpu.VMEM((features, wide_half), BF16), three_sems],
        flops=5 * unit,
        out_spaces="hhhv",
    )
    swaps = [
        functools.partial(swap_plane, bit=bit)
        for bit in (1 << i for i in reversed(range(n_planes.bit_length() - 1)))
    ]
    got_far_up = swap_second(far_up)
    got_near_up = swap_second(after(near_up, got_far_up))
    got_last = swap_core(send_last)
    (sum_expert_out,) = run_kernel(
        copies_whole_kernel,
        [
            after(pos, send_last, in_low),
            pair,
            got_low,
            got_high,
            got_whole,
            core_kept,
            core_rest,
        ],
        "s" + "v" * 6,
        [shaped(inner // n_replica, features, dtype=F32)],
        flops=4 * unit,
    )
    far, near, kept, vector = run_kernel(
        planes(last_keep_kernel, n_planes),
        [
            after(pos, sum_expert_out, got_far_up),
            attn_in,
            grad_qkv,
            grad_gain_one,
            grad_gain_two,
            got_last,
        ],
        "s" + "v" * 5,
        [
            shaped(features // 4 + VECTOR_ROWS, last_half),
            shaped(features // 4, last_half),
            shaped(features // 2, last_half),
            shaped(8, last_half, dtype=F32),
        ],
        [
            pltpu.VMEM((features, last_half), BF16),
            pltpu.VMEM((VECTOR_ROWS, last_half), BF16),
            three_sems,
        ],
        flops=2 * unit,
        out_spaces="hhhv",
    )
    up_2 = second_sum(got_far_up, got_near_up, kept_up, gate=(kept,))
    last_2 = second_sum(swap_second(far), swap_second(after(near, up_2[0])), kept, vector)
    in_high = swap_y(after(send_in, up_2[0]))
    down_3, _ = exchange_rows(after(down_2[0], kept), None, swaps[0])
    delta_home = to_expert(after(delta, down_3))
    down_3 = after(down_3, last_2[0])
    for swap in swaps[1:]:
        down_3, _ = exchange_rows(down_3, None, swap)
    up_3, _ = plane_sum(after(up_2[0], *last_2[2]), None, n_planes)
    last_3, vector = plane_sum(*last_2[:2], n_planes)
    sum_down, sum_up, sum_last = (whole_rows(v, core) for v in (down_3, up_3, last_3))
    mixed = (
        dense_out
        + lax.dot_general(
            route_pick, delta_home, (((0,), (0,)), ((), ())), preferred_element_type=F32
        )
    ).astype(BF16)
    part = features // n_replica
    sum_expert_in = kept_in.astype(F32) + join(in_low, in_high[: 3 * features // 16]).astype(F32)
    vectors = vectors[:2] + in_high[3 * features // 16 : 3 * features // 16 + 2, :features].astype(F32)
    vectors = lax.dynamic_slice_in_dim(vectors, replica * part, part, 1)
    shard = features // n_dev
    gain_grads = lax.dynamic_slice_in_dim(vector[:2, :features], me * shard, shard, 1)
    return (
        mixed,
        grad_tokens,
        sum_last,
        sum_up[:, hidden_size:],
        sum_up[:, :hidden_size],
        sum_down,
        gain_grads[0],
        gain_grads[1],
        sum_expert_in[None],
        sum_expert_out[None],
        vectors[:1],
        vectors[1:],
    )


def solution(mesh):
    placed = (
        P(("expert", "replica"), None),
        P(("expert", "replica"), None),
        P(("expert", "replica"), None),
        P(("expert", "replica"), None),
        P(("expert", "replica"), None),
        P(("expert", "replica"), None),
        P(("expert", "replica")),
        P(("expert", "replica")),
        P("expert", None, None),
        P("expert", None, None),
        P("expert", None),
        P("expert", None),
        P(("expert", "replica"), None),
    )
    return jax.shard_map(
        on_device,
        mesh=mesh,
        in_specs=placed,
        out_specs=(
            P(("expert", "replica"), None),
            P(("expert", "replica"), None),
            P(("expert", "replica"), None),
            P(("expert", "replica"), None),
            P(("expert", "replica"), None),
            P(("expert", "replica"), None),
            P(("expert", "replica")),
            P(("expert", "replica")),
            P("expert", "replica", None),
            P("expert", "replica", None),
            P("expert", "replica"),
            P("expert", "replica"),
        ),
        check_vma=False,
    )
```

```python
import functools
import math

import jax
import jax.numpy as jnp
from jax import lax
from jax.experimental import pallas as pl
from jax.experimental.pallas import tpu as pltpu
from jax.sharding import PartitionSpec as P

HEADS = 16
EPSILON = 1e-05
ALL_AXES = ("expert", "replica")
VMEM_LIMIT = 58 * 2**20
GELU_SCALE = math.sqrt(2.0 / math.pi)
BF16, F32 = jnp.bfloat16, jnp.float32


def permuted(values, target):
    n_dev = lax.axis_size("expert") * lax.axis_size("replica")
    return lax.ppermute(values, ALL_AXES, [(d, target(d, n_dev)) for d in range(n_dev)])


def swap_core(values):
    return permuted(values, lambda d, n: d ^ 1)


def swap_first(values):
    return permuted(values, lambda d, n: d ^ (2 if d % 2 else 4))


def swap_second(values):
    return permuted(values, lambda d, n: d ^ (4 if d % 2 else 2))


def swap_x(values):
    return permuted(values, lambda d, n: d ^ 4)


def swap_y(values):
    return permuted(values, lambda d, n: d ^ 2)


def swap_plane(values, bit):
    return permuted(values, lambda d, n: d ^ (8 * bit))


def after(values, *earlier):
    return lax.optimization_barrier((values,) + earlier)[0]


HINT = 30


def body_name(body):
    return getattr(body, "func", body).__name__


def run_kernel(body, args, spaces, outs, scratch=(), flops=0, out_spaces=None):
    place = {
        "v": pl.BlockSpec(memory_space=pltpu.VMEM),
        "h": pl.BlockSpec(memory_space=pl.ANY),
        "s": pl.BlockSpec(memory_space=pltpu.SMEM),
    }
    moved = sum(a.size * a.dtype.itemsize for a in args)
    moved += sum(o.size * o.dtype.itemsize for o in outs)
    return pl.pallas_call(
        body,
        name=body_name(body),
        out_shape=list(outs),
        in_specs=[place[s] for s in spaces],
        out_specs=[place[s] for s in (out_spaces or "v" * len(outs))],
        scratch_shapes=list(scratch),
        cost_estimate=pl.CostEstimate(flops=int(flops * HINT), bytes_accessed=int(moved * HINT), transcendentals=0),
        compiler_params=pltpu.CompilerParams(vmem_limit_bytes=VMEM_LIMIT),
    )(*args)


def shaped(*shape, dtype=BF16):
    return jax.ShapeDtypeStruct(shape, dtype)


def dot_nn(left, right):
    return jnp.dot(left, right, preferred_element_type=F32)


def dot_nt(left, right):
    return lax.dot_general(left, right, (((1,), (1,)), ((), ())), preferred_element_type=F32)


def dot_tn(left, right):
    return lax.dot_general(left, right, (((0,), (0,)), ((), ())), preferred_element_type=F32)


def normed(values):
    centered = values - jnp.mean(values, axis=-1, keepdims=True)
    inverse = lax.rsqrt(jnp.mean(centered * centered, axis=-1, keepdims=True) + EPSILON)
    return centered * inverse, inverse


def norm_back(grad_normed, norm, inverse):
    return inverse * (
        grad_normed
        - jnp.mean(grad_normed, axis=-1, keepdims=True)
        - norm * jnp.mean(grad_normed * norm, axis=-1, keepdims=True)
    )


def gelu_both(values):
    square = values * values
    bent = jnp.tanh(GELU_SCALE * values * (1.0 + 0.044715 * square))
    half = 0.5 * (1.0 + bent)
    slope = half + 0.5 * values * (1.0 - bent * bent) * (
        GELU_SCALE * (1.0 + 3.0 * 0.044715 * square)
    )
    return values * half, slope


def row_start(pos, core, first, second, step, n_planes, block):
    x, y = pos[1], pos[2]
    flip = lambda v, on: 1 - v if on else v
    across = jnp.where(core == 0, flip(x, first), flip(x, second))
    along = jnp.where(core == 0, flip(y, second), flip(y, first))
    plane = pos[0] ^ step
    return pl.multiple_of(((plane * 2 + across) * 2 + along) * block, block)


PIECE_ORDER = ((0, 0), (1, 0), (0, 1), (1, 1))


def load_weight(pos, sides, target, sems, n_planes, by_plane):
    block = target.shape[0] // (4 * n_planes)
    part = n_planes // 2
    order = [(far, *chip) for far in range(2) for chip in PIECE_ORDER]
    copies = []
    for side, pieces in enumerate(sides):
        half = pieces[0].shape[1]
        core = pos[3] if side == 0 else 1 - pos[3]
        lanes = pl.ds(pl.multiple_of(core * half, 128), half)
        spots = [(piece, at) for piece in pieces for at in range(0, piece.shape[0], block * part)]
        for (far, first, second), (piece, at) in zip(order, spots, strict=True):
            for step in range(part):
                row = row_start(pos, core, first, second, far * part + step, n_planes, block)
                copies.append(
                    (
                        far * part + step if by_plane else side,
                        pltpu.make_async_copy(
                            piece.at[pl.ds(at + step * block, block), :],
                            target.at[pl.ds(row, block), lanes],
                            sems.at[far * part + step] if by_plane else sems.at[core],
                        ),
                    )
                )
    for _, copy in sorted(copies, key=lambda pair: pair[0]):
        copy.start()


def wait_half(target, core, sems):
    half = target.at[:, : target.shape[1] // 2]
    pltpu.make_async_copy(half, half, sems.at[core]).wait()


def wait_step(pos, target, sems, step, n_planes):
    rows = target.shape[0] // n_planes
    part = target.at[:rows, :]
    pltpu.make_async_copy(part, part, sems.at[step]).wait()
    return pl.multiple_of((pos[0] ^ step) * rows, rows)


def wait_whole(target, sem):
    pltpu.make_async_copy(target, target, sem).wait()


def causal_mask(length):
    return lax.broadcasted_iota(jnp.int32, (length, length), 0) >= lax.broadcasted_iota(
        jnp.int32, (length, length), 1
    )


def take_sides(refs, split):
    mine, both = split[0], sum(split)
    return (refs[:mine], refs[mine:both]), refs[both:]


def attend_kernel(n_planes, split, pos, tokens, *refs):
    sides, refs = take_sides(refs, split)
    hidden, ffn_in, attn_in, qkv, heads, gains, weight, sem = refs
    length, width = tokens.shape
    load_weight(pos, sides, weight, sem, n_planes, False)
    inputs = tokens[...].astype(F32)
    norm, _ = normed(inputs)
    wait_half(weight, 1, sem)
    columns = weight[:, 4 * width : 4 * width + 128].astype(F32)
    gains[...] = columns.T[:8]
    attn_in[...] = (norm * gains[0:1, :]).astype(BF16)
    wait_half(weight, 0, sem)
    for part in range(3):
        lanes = slice(part * width, (part + 1) * width)
        qkv[:, lanes] = dot_nn(attn_in[...], weight[:, lanes]).astype(BF16)
    head_size = width // HEADS
    causal = causal_mask(length)
    lane = lax.broadcasted_iota(jnp.int32, (1, 2 * head_size), 1)

    def pair(i, _):
        at = pl.multiple_of(i * 2 * head_size, 2 * head_size)
        query = qkv[:, pl.ds(at, 2 * head_size)] * (head_size**-0.5)
        key_rows = qkv[:, pl.ds(width + at, 2 * head_size)]
        value_rows = qkv[:, pl.ds(2 * width + at, 2 * head_size)]
        mixed = []
        for head in range(2):
            own = (lane // head_size) == head
            scores = dot_nt(jnp.where(own, query, 0).astype(BF16), key_rows)
            scores = jnp.where(causal, scores, -1e30)
            shifted = jnp.exp(scores - jnp.max(scores, axis=-1, keepdims=True))
            probs = shifted / jnp.sum(shifted, axis=-1, keepdims=True)
            mixed.append(dot_nn(probs.astype(BF16), value_rows))
        heads[:, pl.ds(at, 2 * head_size)] = jnp.where(lane < head_size, mixed[0], mixed[1]).astype(
            BF16
        )
        return 0

    lax.fori_loop(0, HEADS // 2, pair, 0)
    hidden[...] = inputs + dot_nn(heads[...], weight[:, 3 * width : 4 * width])
    norm_two, _ = normed(hidden[...])
    ffn_in[...] = (norm_two * gains[1:2, :]).astype(BF16)


def up_kernel(n_planes, split, pos, ffn_in, *refs):
    sides, (act, slope, weight, sem) = take_sides(refs, split)
    load_weight(pos, sides, weight, sem, n_planes, False)
    chunk = 512
    half = weight.shape[1] // 2
    for side in range(2):
        core = pos[3] if side == 0 else 1 - pos[3]
        wait_half(weight, core, sem)
        for i in range(half // chunk):
            lanes = pl.ds(pl.multiple_of(core * half + i * chunk, chunk), chunk)
            value, grad = gelu_both(dot_nn(ffn_in[...], weight[:, lanes]))
            act[:, lanes] = value.astype(BF16)
            slope[:, lanes] = grad


def down_kernel(n_planes, split, pos, act, hidden, pick, *refs):
    sides, (dense_out, sent, weight, sem) = take_sides(refs, split)
    load_weight(pos, sides, weight, sem, n_planes, True)
    rows = weight.shape[0] // n_planes
    total = hidden[...]
    for step in range(n_planes):
        at = pl.ds(wait_step(pos, weight, sem, step, n_planes), rows)
        total = total + dot_nn(act[:, at], weight[at, :])
    dense_out[...] = total
    sent[...] = dot_nn(pick[...], total.astype(BF16)).astype(BF16)


def expert_kernel(
    pos,
    arrived,
    grad_delta,
    centroid,
    norm_gain,
    weight_in,
    weight_out,
    delta,
    grad_rows,
    norm_low,
    kept,
    sent_low,
    sent_high,
    whole_low,
    grad_pre,
    vectors,
    w_in,
    w_out,
    act,
    slope,
    sems,
):
    chunk = 512
    n_chunks = w_in.shape[1] // chunk
    spans = [pl.ds(i * chunk, chunk) for i in range(n_chunks)]
    copies_in = [
        pltpu.make_async_copy(weight_in.at[0, :, span], w_in.at[:, span], sems.at[0, i])
        for i, span in enumerate(spans)
    ]
    copies_out = [
        pltpu.make_async_copy(weight_out.at[0, span, :], w_out.at[span, :], sems.at[1, i])
        for i, span in enumerate(spans)
    ]
    for copy in copies_in + copies_out:
        copy.start()
    rows = arrived[...].astype(F32)
    center = centroid[...].astype(F32)
    gain = norm_gain[...].astype(F32)
    gate = jax.nn.sigmoid(jnp.sum(rows * center, axis=-1, keepdims=True))
    norm, inverse = normed(rows)
    norm_low[...] = (norm * gain).astype(BF16)
    grad_out = grad_delta[...].astype(F32)
    grad_whole = gate * grad_out
    whole_low[...] = grad_whole.astype(BF16)
    for copy, span in zip(copies_in, spans):
        copy.wait()
        value, grad = gelu_both(dot_nn(norm_low[...], w_in[:, span]))
        act[:, span] = value.astype(BF16)
        slope[:, span] = grad
    half = act.shape[1] // 2
    kept[:, :half] = act[:, pl.ds(pl.multiple_of(pos[2] * half, 128), half)]
    other = pl.multiple_of((1 - pos[2]) * half, 128)
    sent_low[...] = act[:, pl.ds(other, half // 2)]
    sent_high[...] = act[:, pl.ds(pl.multiple_of(other + half // 2, 128), half // 2)]
    kept[:, half:] = whole_low[...]
    for copy in copies_out:
        copy.wait()
    whole = rows + dot_nn(act[...], w_out[...])
    delta[...] = (gate * whole).astype(BF16)
    grad_gate = jnp.sum(grad_out * whole, axis=-1, keepdims=True)
    grad_logit = grad_gate * gate * (1.0 - gate)

    for span in spans:
        grad_act = dot_nt(whole_low[...], w_out[span, :])
        grad_pre[:, span] = (grad_act * slope[:, span]).astype(BF16)
    grad_norm = dot_nt(grad_pre[...], w_in[...])
    vectors[...] = jnp.zeros_like(vectors)
    vectors[0:1, :] = jnp.sum(grad_logit * rows, axis=0, keepdims=True)
    vectors[1:2, :] = jnp.sum(grad_norm * norm, axis=0, keepdims=True)
    back = norm_back(grad_norm * gain, norm, inverse)
    grad_rows[...] = (grad_whole + grad_logit * center + back).astype(BF16)


VECTOR_ROWS = 16


def put_vectors(target, at, one, two):
    width = one.shape[1]
    row = lax.broadcasted_iota(jnp.int32, (VECTOR_ROWS, width), 0)
    both = jnp.where(row == 0, one, jnp.where(row == 1, two, 0.0))
    target[at : at + VECTOR_ROWS, :] = jnp.zeros((VECTOR_ROWS, target.shape[1]), BF16)
    target[at : at + VECTOR_ROWS, :width] = both.astype(BF16)


def copies_send_kernel(pos, left, right, vectors, sent):
    block = left.shape[1] // 4
    other = 1 - pos[3]
    tile = 256

    def step(i, _):
        outer, inner = lax.div(i, block // tile), lax.rem(i, block // tile)
        at = pl.multiple_of((2 * outer + other) * block + inner * tile, tile)
        sent[pl.ds(pl.multiple_of(i * tile, tile), tile), :] = dot_tn(
            left[:, pl.ds(at, tile)], right[...]
        ).astype(BF16)
        return 0

    lax.fori_loop(0, 2 * block // tile, step, 0)
    put_vectors(sent, 2 * block, vectors[:1, :], vectors[1:2, :])


def copies_keep_kernel(
    pos, left, right, vectors, received, sent_first, sent, kept, vector_sums
):
    block = left.shape[1] // 4
    core, y = pos[3], pos[2]
    early = sent_first.shape[0]
    for turn in range(2):
        outer = 1 - y if turn else y
        at = pl.ds(pl.multiple_of((2 * outer + core) * block, 128), block)
        there = pl.ds(pl.multiple_of(outer * block, 16), block)
        value = dot_tn(left[:, at], right[...]) + received[there, :].astype(F32)
        if turn:
            sent_first[...] = value[:early].astype(BF16)
            sent[: block - early, :] = value[early:].astype(BF16)
        else:
            kept[...] = value.astype(BF16)
    width = vectors.shape[1]
    got = received[2 * block : 2 * block + VECTOR_ROWS, :width].astype(F32)
    vector_sums[...] = vectors[...] + got[:8]
    put_vectors(sent, block - early, vector_sums[:1, :], vector_sums[1:2, :])


def copies_whole_kernel(pos, kept, low, high, whole, core_kept, core_rest, result):
    tile = 512
    rows = kept.shape[0]
    width = kept.shape[1] - result.shape[1]
    start = pos[3] * (width // 2)

    def step(i, _):
        at = pl.ds(pl.multiple_of(i * tile, tile), tile)
        mine = jnp.where(pos[3] == 0, low[:, at], high[:, at])
        other = jnp.where(pos[3] == 0, core_rest[:rows, at], core_rest[rows : 2 * rows, at])
        both = pl.ds(pl.multiple_of(start + i * tile, tile), tile)
        result[at, :] = (
            dot_tn(kept[:, both], kept[:, width:])
            + dot_tn(mine, whole[...])
            + dot_tn(core_kept[:, both], core_kept[:, width:])
            + dot_tn(other, core_rest[2 * rows :, :])
        )
        return 0

    lax.fori_loop(0, result.shape[0] // tile, step, 0)


def dense_grad_kernel(pos, returned, cotangent, pick, act, grad_dense, grad_low, sent):
    grad_dense[...] = cotangent[...].astype(F32) + dot_tn(pick[...], returned[...])
    grad_low[...] = grad_dense[...].astype(BF16)
    sum_send_kernel(pos, act, grad_low, sent)


def sum_send_kernel(pos, left, right, sent):
    half = right.shape[1] // 2
    lanes = pl.ds(pl.multiple_of((1 - pos[3]) * half, 128), half)
    tile = min(1024, left.shape[1] // 2)

    def step(i, _):
        rows = pl.ds(pl.multiple_of(i * tile, tile), tile)
        sent[rows, :] = dot_tn(left[:, rows], right[:, lanes]).astype(BF16)
        return 0

    lax.fori_loop(0, left.shape[1] // tile, step, 0)


def lay_out(pos, total, far, near, kept, sems, n_planes, vector=None):
    block = total.shape[0] // (4 * n_planes)
    for second in (1, 0):
        for step in range(n_planes):
            for first in (1, 0):
                row = row_start(pos, pos[3], second, first, step, n_planes, block)
                if first:
                    target, at, sem = (far if second else near), step, sems.at[1 + second]
                else:
                    target, at, sem = kept, second * n_planes + step, sems.at[0]
                pltpu.make_async_copy(
                    total.at[pl.ds(row, block), :], target.at[pl.ds(at * block, block), :], sem
                ).start()
    if vector is not None:
        pltpu.make_async_copy(
            vector, far.at[pl.ds(total.shape[0] // 4, VECTOR_ROWS), :], sems.at[2]
        ).start()
    for target, sem in ((kept, 0), (near, 1), (far, 2)):
        wait_whole(target, sems.at[sem])


def sum_keep_kernel(
    n_planes, pos, left, right, received, far, near, kept, total, sems, vector=None
):
    half = right.shape[1] // 2
    lanes = pl.ds(pl.multiple_of(pos[3] * half, 128), half)
    tile = min(1024, left.shape[1] // 2)

    def step(i, _):
        rows = pl.ds(pl.multiple_of(i * tile, tile), tile)
        total[rows, :] = (
            dot_tn(left[:, rows], right[:, lanes]) + received[rows, :].astype(F32)
        ).astype(BF16)
        return 0

    lax.fori_loop(0, left.shape[1] // tile, step, 0)
    lay_out(pos, total, far, near, kept, sems, n_planes, vector)


def pre_back_kernel(n_planes, split, pos, grad_low, slope, *refs):
    sides, (grad_pre, weight, sem) = take_sides(refs, split)
    load_weight(pos, sides, weight, sem, n_planes, True)
    rows = weight.shape[0] // n_planes
    chunk = min(512, rows)
    for step in range(n_planes):
        start = wait_step(pos, weight, sem, step, n_planes)
        for i in range(rows // chunk):
            at = pl.ds(pl.multiple_of(start + i * chunk, chunk), chunk)
            grad_pre[:, at] = (dot_nt(grad_low[...], weight[at, :]) * slope[:, at]).astype(BF16)


def hidden_back_kernel(n_planes, split, pos, grad_pre, hidden, grad_dense, gains, *refs):
    sides, (ffn_in, heads, grad_hidden, grad_low, grad_gain, send, weight, sem) = take_sides(refs, split)
    load_weight(pos, sides, weight, sem, n_planes, False)
    norm, inverse = normed(hidden[...])
    half = weight.shape[1] // 2
    grad_in = 0.0
    for side in range(2):
        core = pos[3] if side == 0 else 1 - pos[3]
        wait_half(weight, core, sem)
        lanes = pl.ds(pl.multiple_of(core * half, 128), half)
        grad_in = grad_in + dot_nt(grad_pre[:, lanes], weight[:, lanes])
    grad_gain[...] = jnp.zeros_like(grad_gain)
    grad_gain[0:1, :] = jnp.sum(grad_in * norm, axis=0, keepdims=True)
    grad_hidden[...] = grad_dense[...] + norm_back(grad_in * gains[1:2, :], norm, inverse)
    grad_low[...] = grad_hidden[...].astype(BF16)
    wide_columns(1 - pos[3], ffn_in, heads, grad_pre, grad_low, send, None)


def attend_back_kernel(n_planes, split, pos, grad_low, qkv, tokens, grad_hidden, gains, *refs):
    sides, refs = take_sides(refs, split)
    grad_qkv, grad_tokens, grad_gain, grad_heads, weight, sem = refs
    length, width = tokens.shape
    head_size = width // HEADS
    load_weight(pos, sides, weight, sem, n_planes, False)
    inputs = tokens[...].astype(F32)
    norm, inverse = normed(inputs)
    causal = causal_mask(length)
    lane = lax.broadcasted_iota(jnp.int32, (1, 2 * head_size), 1)
    wait_half(weight, 1, sem)
    grad_heads[...] = dot_nt(grad_low[...], weight[:, 3 * width : 4 * width]).astype(BF16)
    factor = head_size**-0.5

    def pair(i, _):
        at = pl.multiple_of(i * 2 * head_size, 2 * head_size)
        query = qkv[:, pl.ds(at, 2 * head_size)]
        key_rows = qkv[:, pl.ds(width + at, 2 * head_size)]
        value_rows = qkv[:, pl.ds(2 * width + at, 2 * head_size)]
        grad_out = grad_heads[:, pl.ds(at, 2 * head_size)]
        sums = [0.0, 0.0, 0.0]
        for head in range(2):
            own = (lane // head_size) == head
            masked = lambda v: jnp.where(own, v, 0).astype(BF16)
            own_query, own_grad = masked(query), masked(grad_out)
            scores = dot_nt(own_query, key_rows) * factor
            scores = jnp.where(causal, scores, -1e30)
            shifted = jnp.exp(scores - jnp.max(scores, axis=-1, keepdims=True))
            probs = shifted / jnp.sum(shifted, axis=-1, keepdims=True)
            grad_probs = dot_nt(own_grad, value_rows)
            row_terms = jnp.sum(probs * grad_probs, axis=-1, keepdims=True)
            grad_scores = (probs * (grad_probs - row_terms)).astype(BF16)
            sums[0] = sums[0] + dot_nn(grad_scores, masked(key_rows)) * factor
            sums[1] = sums[1] + dot_tn(grad_scores, own_query) * factor
            sums[2] = sums[2] + dot_tn(probs.astype(BF16), own_grad)
        for part in range(3):
            grad_qkv[:, pl.ds(part * width + at, 2 * head_size)] = sums[part].astype(BF16)
        return 0

    lax.fori_loop(0, HEADS // 2, pair, 0, unroll=True)
    wait_half(weight, 0, sem)
    grad_in = dot_nt(grad_qkv[...], weight[:, : 3 * width])
    grad_gain[...] = jnp.zeros_like(grad_gain)
    grad_gain[0:1, :] = jnp.sum(grad_in * norm, axis=0, keepdims=True)
    grad_tokens[...] = grad_hidden[...] + norm_back(grad_in * gains[0:1, :], norm, inverse)


def wide_columns(half, ffn_in, heads, grad_pre, grad_low, target, received):
    width = ffn_in.shape[1]
    columns = target.shape[1]
    rest = grad_pre.shape[1] - columns
    tile = 512

    def fill(lanes, left, right):
        def step(i, _):
            rows = pl.ds(pl.multiple_of(i * tile, tile), tile)
            value = dot_tn(left[:, rows], right())
            if received is not None:
                value = value + received[rows, lanes].astype(F32)
            target[rows, lanes] = value.astype(BF16)
            return 0

        lax.fori_loop(0, width // tile, step, 0)

    @pl.when(half == 0)
    def _():
        fill(slice(0, columns), ffn_in, lambda: grad_pre[:, :columns])

    @pl.when(half == 1)
    def _():
        fill(slice(0, rest), ffn_in, lambda: grad_pre[:, columns:])
        fill(slice(rest, columns), heads, lambda: grad_low[...])


def wide_keep_kernel(
    n_planes,
    pos,
    ffn_in,
    heads,
    grad_pre,
    grad_low,
    received,
    attn_in,
    grad_qkv,
    gain_one,
    gain_two,
    far,
    near,
    kept,
    send,
    total,
    sems,
):
    wide_columns(pos[3], ffn_in, heads, grad_pre, grad_low, total, received)
    lay_out(pos, total, far, near, kept, sems, n_planes)
    last_send_kernel(pos, attn_in, grad_qkv, gain_one, gain_two, send)


def last_send_kernel(pos, left, right, gain_one, gain_two, sent):
    put_vectors(sent, left.shape[1], gain_one[:1, :], gain_two[:1, :])
    sum_send_kernel(pos, left, right, sent)


def last_keep_kernel(
    n_planes,
    pos,
    left,
    right,
    gain_one,
    gain_two,
    received,
    far,
    near,
    kept,
    vector,
    total,
    vector_low,
    sems,
):
    at = received.shape[0] - VECTOR_ROWS
    width = gain_one.shape[1]
    vector[...] = jnp.zeros_like(vector)
    vector_low[...] = jnp.zeros_like(vector_low)
    for i, gain in enumerate((gain_one, gain_two)):
        row = slice(at, at + VECTOR_ROWS)
        summed = gain[:1, :] + received[row, :width].astype(F32)[i : i + 1]
        vector[i : i + 1, :width] = summed
    vector_low[:8, :] = vector[...].astype(BF16)
    sum_keep_kernel(
        n_planes, pos, left, right, received, far, near, kept, total, sems, vector_low
    )


def own_columns(values, core):
    half = values.shape[1] // 2
    mine = lax.dynamic_slice_in_dim(values, core * half, half, 1)
    other = lax.dynamic_slice_in_dim(values, (1 - core) * half, half, 1)
    got = swap_core(other)
    return jnp.where(
        core == 0, jnp.concatenate([mine, got], axis=0), jnp.concatenate([got, mine], axis=0)
    )


def exchange_rows(total, vector, swap):
    half = total.shape[0] // 2
    send = total[half:].astype(BF16)
    if vector is not None:
        send = jnp.concatenate(
            [send, jnp.pad(vector, ((0, VECTOR_ROWS - vector.shape[0]), (0, 0))).astype(BF16)], axis=0
        )
    got = swap(send).astype(F32)
    if vector is not None:
        vector = vector + got[half : half + vector.shape[0]]
    return total[:half] + got[:half], vector


def start_sum(got, kept):
    return kept.astype(F32) + got[: kept.shape[0]].astype(F32)


def plane_sum(total, vector, n_planes):
    block = total.shape[0] // n_planes
    result, sums = total[:block], vector
    for step in range(1, n_planes):
        send = total[step * block : (step + 1) * block].astype(BF16)
        if vector is not None:
            send = jnp.concatenate([send, vector.astype(BF16)], axis=0)
        got = swap_plane(send, step).astype(F32)
        result = result + got[:block]
        if vector is not None:
            sums = sums + got[block : block + vector.shape[0]]
    return result, sums


def second_sum(got_far, got_near, kept, vector=None, gate=()):
    half = kept.shape[0] // 2
    send = (kept[half:].astype(F32) + got_far[:half].astype(F32)).astype(BF16)
    if vector is not None:
        vector = vector[:2] + got_far[half : half + 2].astype(F32)
        send = jnp.concatenate([send, vector.astype(BF16)], axis=0)
    got = swap_first(after(send, *gate) if gate else send).astype(F32)
    if vector is not None:
        vector = vector + got[half : half + vector.shape[0]]
    return kept[:half].astype(F32) + got_near.astype(F32) + got[:half], vector, (send,)


def whole_rows(total, core):
    shard = total.shape[0] // 2
    mine = lax.dynamic_slice_in_dim(total, core * shard, shard, 0)
    other = lax.dynamic_slice_in_dim(total, (1 - core) * shard, shard, 0)
    got = swap_core(other.astype(BF16)).astype(F32)
    return jnp.where(
        core == 0, jnp.concatenate([mine, got], axis=1), jnp.concatenate([got, mine], axis=1)
    )


def on_device(
    tokens,
    route,
    w_qkv,
    w_attn_out,
    w_up,
    w_down,
    gain_attn,
    gain_ffn,
    expert_in,
    expert_out,
    centroids,
    expert_gain,
    cotangent,
):
    length, features = tokens.shape
    n_expert = lax.axis_size("expert")
    n_replica = lax.axis_size("replica")
    n_dev = n_expert * n_replica
    n_planes = n_dev // 8
    per_dest = length // n_expert
    hidden_size = w_up.shape[1]
    replica = lax.axis_index("replica")
    me = lax.axis_index("expert") * n_replica + replica
    core = me % 2
    pos = jnp.stack([me // 8, (me // 4) % 2, (me // 2) % 2, core]).astype(jnp.int32)
    route_pick = (route[0][:, None] == lax.iota(jnp.int32, length)[None]).astype(BF16)

    def to_expert(picked):
        return lax.all_to_all(
            picked.reshape(n_expert, per_dest, features),
            "expert",
            split_axis=0,
            concat_axis=0,
            tiled=True,
        ).reshape(length, features)

    padded_gains = jnp.pad(jnp.stack([gain_attn, gain_ffn], axis=1), ((0, 0), (0, 254)))
    first = jnp.concatenate([w_qkv, w_attn_out, padded_gains], axis=1)
    owned = [own_columns(v, core) for v in (first, w_up, w_down)]
    join = lambda *v: jnp.concatenate(v, axis=0)
    far_bit = n_planes // 2

    def near_planes(own, *earlier):
        stack = after(own, *earlier) if earlier else own
        bit = 1
        while bit < far_bit:
            stack = join(stack, swap_plane(stack, bit))
            bit *= 2
        return stack

    own_a, own_b, own_c = owned
    near_a = near_planes(own_a)
    gate = (near_a,)
    far_a = swap_plane(near_a, far_bit)
    near_one_a = swap_first(near_a)
    near_b, near_c = near_planes(own_b, *gate), near_planes(own_c, *gate)
    gate = (far_a, near_one_a, near_b, near_c)
    far_b = swap_plane(after(near_b, *gate), far_bit)
    near_two_a = swap_second(after(join(near_a, near_one_a), *gate))
    one_a = swap_first(after(far_a, *gate))
    near_one_b = swap_first(after(near_b, *gate))
    gate = (far_b, near_two_a, one_a, near_one_b)
    far_c = swap_plane(after(near_c, *gate), far_bit)
    two_a = swap_second(after(join(far_a, one_a), *gate))
    near_two_b = swap_second(after(join(near_b, near_one_b), *gate))
    one_b = swap_first(after(far_b, *gate))
    core_near_a = swap_core(after(join(near_a, near_one_a, near_two_a), *gate))
    gate = (far_c, two_a, near_two_b, one_b, core_near_a)
    two_b = swap_second(after(join(far_b, one_b), *gate))
    near_one_c = swap_first(after(near_c, *gate))
    one_c = swap_first(after(far_c, *gate))
    core_far_a = swap_core(after(join(far_a, one_a, two_a), *gate))
    core_near_b = swap_core(after(join(near_b, near_one_b, near_two_b), *gate))
    first_pieces = [near_a, near_one_a, near_two_a, far_a, one_a, two_a, core_near_a, core_far_a]
    gate = (two_b, near_one_c, one_c, core_far_a, core_near_b)
    near_two_c = swap_second(after(join(near_c, near_one_c), *gate))
    two_c = swap_second(after(join(far_c, one_c), *gate))
    core_far_b = swap_core(after(join(far_b, one_b, two_b), *gate))
    core_one_c = swap_core(after(join(far_c, one_c), *gate))
    up_pieces = [near_b, near_one_b, near_two_b, far_b, one_b, two_b, core_near_b, core_far_b]

    wide = first.shape[1]
    planes = functools.partial
    weight_first = pltpu.VMEM((features, wide), BF16)
    weight_up = pltpu.VMEM((features, hidden_size), BF16)
    weight_down = pltpu.VMEM((hidden_size, features), BF16)
    two_sems, three_sems, plane_sems = (pltpu.SemaphoreType.DMA((n,)) for n in (2, 3, n_planes))
    unit = 2 * length * features * features

    hidden, ffn_in, attn_in, qkv, heads, gains = run_kernel(
        planes(attend_kernel, n_planes, (6, 2)),
        [pos, tokens, *first_pieces],
        "sv" + "h" * 8,
        [
            shaped(length, features, dtype=F32),
            shaped(length, features),
            shaped(length, features),
            shaped(length, 3 * features),
            shaped(length, features),
            shaped(8, features, dtype=F32),
        ],
        [weight_first, two_sems],
        flops=5 * unit,
    )
    gate = (near_two_c, two_c, core_far_b, hidden)
    core_near_c = swap_core(after(join(near_c, near_one_c, near_two_c), *gate))
    core_two_c = swap_core(after(two_c, *gate))
    grad_delta = to_expert(
        after(
            jnp.dot(route_pick, cotangent, preferred_element_type=F32).astype(BF16), hidden
        )
    )
    act, slope = run_kernel(
        planes(up_kernel, n_planes, (6, 2)),
        [pos, ffn_in, *up_pieces],
        "sv" + "h" * 8,
        [shaped(length, hidden_size), shaped(length, hidden_size, dtype=F32)],
        [weight_up, two_sems],
        flops=4 * unit,
    )
    down_pieces = [near_c, near_one_c, near_two_c, far_c, one_c, two_c, core_near_c, core_one_c, core_two_c]
    dense_out, sent = run_kernel(
        planes(down_kernel, n_planes, (6, 3)),
        [pos, act, hidden, route_pick, *down_pieces],
        "svvv" + "h" * 9,
        [shaped(length, features, dtype=F32), shaped(length, features)],
        [weight_down, plane_sems],
        flops=4 * unit,
    )
    arrived = to_expert(after(sent, grad_delta))
    inner = expert_in.shape[2]
    (
        delta,
        grad_rows,
        expert_norm,
        pair,
        sent_low,
        sent_high,
        whole_low,
        expert_grad_pre,
        vectors,
    ) = run_kernel(
        expert_kernel,
        [pos, arrived, grad_delta, centroids, expert_gain, expert_in, expert_out],
        "svvvvhh",
        [
            shaped(length, features),
            shaped(length, features),
            shaped(length, features),
            shaped(length, inner // 2 + features),
            shaped(length, inner // 4),
            shaped(length, inner // 4),
            shaped(length, features),
            shaped(length, inner),
            shaped(8, features, dtype=F32),
        ],
        [
            pltpu.VMEM((features, inner), BF16),
            pltpu.VMEM((inner, features), BF16),
            pltpu.VMEM((length, inner), BF16),
            pltpu.VMEM((length, inner), F32),
            pltpu.SemaphoreType.DMA((2, inner // 512)),
        ],
        flops=16 * unit,
    )
    returned = to_expert(grad_rows)
    got_low = swap_y(sent_low)

    (send_in,) = run_kernel(
        copies_send_kernel,
        [pos, expert_norm, expert_grad_pre, vectors],
        "svvv",
        [shaped(features // 2 + VECTOR_ROWS, inner)],
        flops=2 * unit,
    )
    got_in = swap_core(send_in)

    grad_dense, grad_dense_low, send_down = run_kernel(
        dense_grad_kernel,
        [after(pos, send_in), returned, cotangent, route_pick, act],
        "svvvv",
        [
            shaped(length, features, dtype=F32),
            shaped(length, features),
            shaped(hidden_size, features // 2),
        ],
        flops=4 * unit,
    )
    got_down = swap_core(send_down)
    got_high = swap_y(after(sent_high, send_down))
    (grad_pre,) = run_kernel(
        planes(pre_back_kernel, n_planes, (6, 3)),
        [after(pos, send_down, got_in, got_low), grad_dense_low, slope, *down_pieces],
        "svv" + "h" * 9,
        [shaped(length, hidden_size)],
        [weight_down, plane_sems],
        flops=4 * unit,
    )
    core_kept = swap_core(pair)
    got_whole = swap_y(after(whole_low, grad_pre))
    far_down, near_down, kept_down = run_kernel(
        planes(sum_keep_kernel, n_planes),
        [after(pos, grad_pre, got_high, core_kept), act, grad_dense_low, got_down],
        "svvv",
        [shaped(hidden_size // 4, features // 2)] * 2 + [shaped(hidden_size // 2, features // 2)],
        [pltpu.VMEM((hidden_size, features // 2), BF16), three_sems],
        flops=4 * unit,
        out_spaces="hhh",
    )
    got_far_down = swap_second(far_down)
    got_near_down = swap_second(after(near_down, got_far_down))
    first_in, send_in, kept_in, vectors = run_kernel(
        copies_keep_kernel,
        [after(pos, kept_down), expert_norm, expert_grad_pre, vectors, got_in],
        "svvvv",
        [
            shaped(features // 16, inner),
            shaped(3 * features // 16 + VECTOR_ROWS, inner),
            shaped(features // 4, inner),
            shaped(8, features, dtype=F32),
        ],
        flops=2 * unit,
    )
    wide_half = (hidden_size + features) // 2
    grad_hidden, grad_hidden_low, grad_gain_two, send_up = run_kernel(
        planes(hidden_back_kernel, n_planes, (6, 2)),
        [
            after(pos, send_in, got_whole),
            grad_pre,
            hidden,
            grad_dense,
            gains,
            *up_pieces,
            ffn_in,
            heads,
        ],
        "svvvv" + "h" * 8 + "vv",
        [
            shaped(length, features, dtype=F32),
            shaped(length, features),
            shaped(8, features, dtype=F32),
            shaped(features, wide_half),
        ],
        [weight_up, two_sems],
        flops=7 * unit,
    )
    got_up = swap_core(send_up)
    core_rest = swap_core(join(*(after(v, send_up) for v in (got_low, got_high, got_whole))))
    grad_qkv, grad_tokens, grad_gain_one = run_kernel(
        planes(attend_back_kernel, n_planes, (6, 2)),
        [
            after(pos, got_far_down, send_up),
            grad_hidden_low,
            qkv,
            tokens,
            grad_hidden,
            gains,
            *first_pieces,
        ],
        "svvvvv" + "h" * 8,
        [
            shaped(length, 3 * features),
            shaped(length, features, dtype=F32),
            shaped(8, features, dtype=F32),
        ],
        [pltpu.VMEM((length, features), BF16), weight_first, two_sems],
        flops=8 * unit,
    )
    in_low = swap_y(after(first_in, grad_qkv))
    down_2 = second_sum(got_far_down, got_near_down, kept_down, gate=(send_up,))
    last_half = 3 * features // 2
    far_up, near_up, kept_up, send_last = run_kernel(
        planes(wide_keep_kernel, n_planes),
        [
            after(pos, grad_qkv, down_2[0], core_rest),
            ffn_in,
            heads,
            grad_pre,
            grad_hidden_low,
            got_up,
            attn_in,
            grad_qkv,
            grad_gain_one,
            grad_gain_two,
        ],
        "s" + "v" * 9,
        [shaped(features // 4, wide_half)] * 2
        + [shaped(features // 2, wide_half), shaped(features + VECTOR_ROWS, last_half)],
        [pltpu.VMEM((features, wide_half), BF16), three_sems],
        flops=5 * unit,
        out_spaces="hhhv",
    )
    swaps = [
        functools.partial(swap_plane, bit=bit)
        for bit in (1 << i for i in reversed(range(n_planes.bit_length() - 1)))
    ]
    got_far_up = swap_second(far_up)
    got_near_up = swap_second(after(near_up, got_far_up))
    got_last = swap_core(send_last)
    (sum_expert_out,) = run_kernel(
        copies_whole_kernel,
        [
            after(pos, send_last, in_low),
            pair,
            got_low,
            got_high,
            got_whole,
            core_kept,
            core_rest,
        ],
        "s" + "v" * 6,
        [shaped(inner // n_replica, features, dtype=F32)],
        flops=4 * unit,
    )
    far, near, kept, vector = run_kernel(
        planes(last_keep_kernel, n_planes),
        [
            after(pos, sum_expert_out, got_far_up),
            attn_in,
            grad_qkv,
            grad_gain_one,
            grad_gain_two,
            got_last,
        ],
        "s" + "v" * 5,
        [
            shaped(features // 4 + VECTOR_ROWS, last_half),
            shaped(features // 4, last_half),
            shaped(features // 2, last_half),
            shaped(8, last_half, dtype=F32),
        ],
        [
            pltpu.VMEM((features, last_half), BF16),
            pltpu.VMEM((VECTOR_ROWS, last_half), BF16),
            three_sems,
        ],
        flops=2 * unit,
        out_spaces="hhhv",
    )
    up_2 = second_sum(got_far_up, got_near_up, kept_up, gate=(kept,))
    last_2 = second_sum(swap_second(far), swap_second(after(near, up_2[0])), kept, vector)
    in_high = swap_y(after(send_in, up_2[0]))
    down_3, _ = exchange_rows(after(down_2[0], kept), None, swaps[0])
    delta_home = to_expert(after(delta, down_3))
    down_3 = after(down_3, last_2[0])
    for swap in swaps[1:]:
        down_3, _ = exchange_rows(down_3, None, swap)
    up_3, _ = plane_sum(after(up_2[0], *last_2[2]), None, n_planes)
    last_3, vector = plane_sum(*last_2[:2], n_planes)
    sum_down, sum_up, sum_last = (whole_rows(v, core) for v in (down_3, up_3, last_3))
    mixed = (
        dense_out
        + lax.dot_general(
            route_pick, delta_home, (((0,), (0,)), ((), ())), preferred_element_type=F32
        )
    ).astype(BF16)
    part = features // n_replica
    sum_expert_in = kept_in.astype(F32) + join(in_low, in_high[: 3 * features // 16]).astype(F32)
    vectors = vectors[:2] + in_high[3 * features // 16 : 3 * features // 16 + 2, :features].astype(F32)
    vectors = lax.dynamic_slice_in_dim(vectors, replica * part, part, 1)
    shard = features // n_dev
    gain_grads = lax.dynamic_slice_in_dim(vector[:2, :features], me * shard, shard, 1)
    return (
        mixed,
        grad_tokens,
        sum_last,
        sum_up[:, hidden_size:],
        sum_up[:, :hidden_size],
        sum_down,
        gain_grads[0],
        gain_grads[1],
        sum_expert_in[None],
        sum_expert_out[None],
        vectors[:1],
        vectors[1:],
    )


def solution(mesh):
    placed = (
        P(("expert", "replica"), None),
        P(("expert", "replica"), None),
        P(("expert", "replica"), None),
        P(("expert", "replica"), None),
        P(("expert", "replica"), None),
        P(("expert", "replica"), None),
        P(("expert", "replica")),
        P(("expert", "replica")),
        P("expert", None, None),
        P("expert", None, None),
        P("expert", None),
        P("expert", None),
        P(("expert", "replica"), None),
    )
    return jax.shard_map(
        on_device,
        mesh=mesh,
        in_specs=placed,
        out_specs=(
            P(("expert", "replica"), None),
            P(("expert", "replica"), None),
            P(("expert", "replica"), None),
            P(("expert", "replica"), None),
            P(("expert", "replica"), None),
            P(("expert", "replica"), None),
            P(("expert", "replica")),
            P(("expert", "replica")),
            P("expert", "replica", None),
            P("expert", "replica", None),
            P("expert", "replica"),
            P("expert", "replica"),
        ),
        check_vma=False,
    )
```
